256 devices in a mesh: seq: 32 (over x, z_hi, y), slide: 8 (over z_lo, core).
Axes of the slice: x: 4, y: 4, z: 8 (z_hi: 2, z_lo: 4; z = z_hi * 4 + z_lo), core: 2. Of those that a mesh axis runs over, the one named last changes fastest.
Arguments:
- tiles: bfloat16 [8, 16384, 1536], P('slide', 'seq'), may hold values from -6 to 6
- w_embed: bfloat16 [1536, 768], replicated, may hold values from -0.15625 to 0.15625
- attn_gain: float32 [768], replicated, may hold values from 0.5 to 1.5
- w_query: bfloat16 [768, 768], replicated, may hold values from -8 to 8, as said below
- w_key: bfloat16 [768, 768], replicated, may hold values from -8 to 8, as said below
- w_value: bfloat16 [768, 768], replicated, may hold values from -0.21875 to 0.21875
- w_out: bfloat16 [768, 768], replicated, may hold values from -0.21875 to 0.21875
- w_head: bfloat16 [768, 768], replicated, may hold values from -0.21875 to 0.21875
- head_offset: int32 [16], replicated, may hold values from 0 to 31
- slide_code: int32 [8], P('slide'), may hold values from 0 to 3, as said below
- report_emb: bfloat16 [8, 768], P('slide'), may hold values from -6 to 6
- report_code: int32 [8], P('slide'), may hold values from 0 to 3, as said below
Outputs:
- encoded: bfloat16 [8, 16384, 768], P('slide', 'seq')
- slide_unit_vectors: float32 [8, 768], P('slide')
- logits: float32 [8, 8], replicated
- loss: float32 [], replicated
The draws below stay inside these ranges and needn't reach their ends.
Inputs may be any that keep to these rules, and one draw needn't show every extreme that they name: `w_query`: entries of a projection of 768 features. `w_key`: entries of a projection of 768 features. `slide_code`: diagnosis code of a slide. `report_code`: diagnosis code of a report; the report of each index has a code different from the slide of the same index.
All inputs are finite; a program needn't handle non-finite values.
Results may differ from the reference program's by a relative error of at most 0.02.
Values may be sent and summed in bfloat16 or wider, within the bound.
No kernel may reach another device: no remote copies, remote signals or barrier semaphores. Data moves between devices by JAX's collectives and lax.ppermute only.
A program may use at most 128 MiB of HBM per device.

```python
import math
import jax
import jax.numpy as jnp
from jax import lax

IN_DIM = 1536
D = 768
HEADS = 16
E = 768
SEG = 1024
RATE = 32
CODES = 4
LEN = 16384
SLIDES = 8


def shared_basis(key):
    return jax.random.normal(key, (D, D), jnp.float32)


def draw_w_key(key, part):
    basis = shared_basis(key)
    key = jax.random.fold_in(key, 7)
    noise = jax.random.normal(key, (D, D), jnp.float32)
    return jnp.clip((0.6 * basis + 0.8 * noise) * D ** (-0.5), -8.0, 8.0).astype(jnp.bfloat16)


def draw_w_query(key, part):
    basis = shared_basis(key)
    key = jax.random.fold_in(key, 13)
    noise = jax.random.normal(key, (D, D), jnp.float32)
    share = 0.6
    return jnp.clip((share * basis + 0.8 * noise) * D ** (-0.5), -8.0, 8.0).astype(jnp.bfloat16)


def code_pair(key):
    key = jax.random.fold_in(key, 101)
    first_key, offset_key, place_key, other_key = jax.random.split(key, 4)
    slide_codes = jax.random.randint(first_key, (SLIDES,), 0, CODES, dtype=jnp.int32)
    offsets = jax.random.randint(offset_key, (SLIDES,), 1, CODES, dtype=jnp.int32)
    top_place = jax.random.randint(place_key, (), 0, SLIDES, dtype=jnp.int32)
    step_away = jax.random.randint(other_key, (), 1, SLIDES, dtype=jnp.int32)
    low_place = (top_place + step_away) % SLIDES
    positions = jnp.arange(SLIDES, dtype=jnp.int32)
    slide_codes = jnp.where(positions == top_place, CODES - 1, slide_codes)
    offsets = jnp.where(positions == top_place, 1, offsets)
    slide_codes = jnp.where(positions == low_place, 0, slide_codes)
    offsets = jnp.where(positions == low_place, CODES - 1, offsets)
    report_codes = (slide_codes + offsets) % CODES
    return (slide_codes.astype(jnp.int32), report_codes.astype(jnp.int32))


def draw_slide_code(key, part):
    return code_pair(key)[0]


def draw_report_code(key, part):
    return code_pair(key)[1]


def place_ends(drawn, stream_key, smallest, largest):
    extent = drawn.shape
    index_at = [jax.random.randint(jax.random.fold_in(stream_key, axis), (), 0, extent[axis]) for axis in range(len(extent))]
    drawn = drawn.at[tuple(index_at)].set(smallest)
    longest = extent.index(max(extent))
    index_at[longest] = (index_at[longest] + 1) % extent[longest]
    return drawn.at[tuple(index_at)].set(largest)


def level_of(key, extent, cuts, smallest, top_value):
    level = 1.0
    for axis_at, blocks in cuts:
        steps = jax.random.uniform(jax.random.fold_in(jax.random.fold_in(key, 6), axis_at), (blocks,), jnp.float32, smallest / len(cuts), top_value / len(cuts))
        level = level * jnp.repeat(jnp.exp(steps), extent[axis_at] // blocks).reshape((-1,) + (1,) * (len(extent) - 1 - axis_at))
    return level


def normal_values(key, extent, width, limit, cuts=(), held_as=jnp.bfloat16):
    entries = width * jax.random.normal(key, extent, jnp.float32)
    if cuts:
        entries = entries * level_of(key, extent, cuts, -0.22, 0.18)
    return jnp.clip(entries, -limit, limit).astype(held_as)


def setup_inputs(seed: int = 0) -> dict:
    seeds = jax.random.split(jax.random.key(seed), 13)
    tiles = normal_values(seeds[0], (SLIDES, LEN, IN_DIM), 1.0, 6.0, ((0, 8), (1, 32)))
    w_embed = normal_values(seeds[1], (IN_DIM, D), IN_DIM ** -0.5, 0.15625)
    attn_gain = jnp.clip(1.0 + 0.1 * jax.random.normal(seeds[2], (D,), jnp.float32), 0.5, 1.5)
    w_query = draw_w_query(jax.random.fold_in(seeds[12], 71), 0)
    w_key = draw_w_key(jax.random.fold_in(seeds[12], 71), 0)
    w_value = normal_values(seeds[5], (D, D), D ** -0.5, 0.21875)
    w_out = normal_values(seeds[6], (D, D), D ** -0.5, 0.21875)
    w_head = normal_values(seeds[7], (D, E), D ** -0.5, 0.21875)
    head_offset = place_ends(jax.random.randint(seeds[8], (HEADS,), 0, RATE), jax.random.fold_in(seeds[8], 1), 0, RATE - 1).astype(jnp.int32)
    slide_code = draw_slide_code(jax.random.fold_in(seeds[12], 71), 0)
    report_emb = normal_values(seeds[10], (SLIDES, E), 1.0, 6.0, ((0, 8),))
    report_code = draw_report_code(jax.random.fold_in(seeds[12], 71), 0)
    return dict(tiles=tiles, w_embed=w_embed, attn_gain=attn_gain, w_query=w_query, w_key=w_key, w_value=w_value, w_out=w_out, w_head=w_head, head_offset=head_offset, slide_code=slide_code, report_emb=report_emb, report_code=report_code)


SOFTMAX_TEMPER = 1.0 / 0.07
NORM_EPS = 1e-05

def layer_norm(inputs, gain):
    floats = inputs.astype(jnp.float32)
    centre = lax.optimization_barrier(jnp.mean(floats, axis=-1, keepdims=True))
    spread = lax.optimization_barrier(jnp.mean(jnp.square(floats - centre), axis=-1, keepdims=True))
    return (floats - centre) * lax.rsqrt(spread + NORM_EPS) * gain.astype(jnp.float32)

def unit_rows(matrix):
    return matrix * lax.rsqrt(lax.optimization_barrier(jnp.sum(matrix * matrix, axis=-1, keepdims=True)) + 1e-06)

def dilated_rows(tensor, head_offset):
    grouped = tensor.reshape(tensor.shape[0] // RATE, RATE, tensor.shape[1], tensor.shape[2])
    chosen = jnp.arange(RATE, dtype=jnp.int32)[:, None] == head_offset.astype(jnp.int32)[None, :]
    picked = jnp.where(chosen[None, :, :, None], grouped, jnp.zeros((), tensor.dtype))
    return lax.optimization_barrier(jnp.sum(picked, axis=1)).astype(tensor.dtype)

def contrastive(slide_unit_vectors, report_vectors, slide_codes, report_codes):
    logits = SOFTMAX_TEMPER * jnp.dot(slide_unit_vectors, report_vectors.T, precision=lax.Precision.HIGHEST)
    count = logits.shape[0]
    same = (slide_codes[:, None] == report_codes[None, :]) | jnp.eye(count, dtype=bool)
    positive = jnp.where(same, 1.0, 0.0).astype(logits.dtype)
    row_peak = lax.optimization_barrier(jnp.max(logits, axis=1, keepdims=True))
    row_lse = row_peak + jnp.log(lax.optimization_barrier(jnp.sum(jnp.exp(logits - row_peak), axis=1, keepdims=True)))
    col_peak = lax.optimization_barrier(jnp.max(logits, axis=0, keepdims=True))
    col_lse = col_peak + jnp.log(lax.optimization_barrier(jnp.sum(jnp.exp(logits - col_peak), axis=0, keepdims=True)))
    slide_terms = -lax.optimization_barrier(jnp.sum(positive * (logits - row_lse), axis=1)) / lax.optimization_barrier(jnp.sum(positive, axis=1))
    report_terms = -lax.optimization_barrier(jnp.sum(positive * (logits - col_lse), axis=0)) / lax.optimization_barrier(jnp.sum(positive, axis=0))
    loss = 0.5 * (jnp.mean(slide_terms) + jnp.mean(report_terms))
    return (logits, loss)

def reference(tiles, w_embed, attn_gain, w_query, w_key, w_value, w_out, w_head, head_offset, slide_code, report_emb, report_code):
    head_width = D // HEADS
    score_scale = 1.0 / math.sqrt(head_width)

    def one_slide(tile_rows):
        embedded = jnp.dot(tile_rows, w_embed, preferred_element_type=jnp.float32).astype(jnp.bfloat16)
        normed = layer_norm(embedded, attn_gain).astype(jnp.bfloat16)
        queries = jnp.dot(normed, w_query, preferred_element_type=jnp.float32).astype(jnp.bfloat16).reshape(LEN, HEADS, head_width)
        keys_all = jnp.dot(normed, w_key, preferred_element_type=jnp.float32).astype(jnp.bfloat16).reshape(LEN, HEADS, head_width)
        values_all = jnp.dot(normed, w_value, preferred_element_type=jnp.float32).astype(jnp.bfloat16).reshape(LEN, HEADS, head_width)
        far_keys = dilated_rows(keys_all, head_offset)
        far_values = dilated_rows(values_all, head_offset)

        def segment(block_items):
            seg_queries, seg_keys, seg_values = block_items
            joined_keys = jnp.concatenate([seg_keys, far_keys], axis=0).astype(jnp.float32)
            joined_values = jnp.concatenate([seg_values, far_values], axis=0).astype(jnp.float32)
            scores = jnp.einsum('qhd,khd->qhk', seg_queries.astype(jnp.float32), joined_keys) * score_scale
            peak = lax.optimization_barrier(jnp.max(scores, axis=-1, keepdims=True))
            weights = jnp.exp(scores - peak)
            total_weight = lax.optimization_barrier(jnp.sum(weights, axis=-1))
            rounded = lax.optimization_barrier(weights.astype(jnp.bfloat16)).astype(jnp.float32)
            mixed = jnp.einsum('qhk,khd->qhd', rounded, joined_values) / total_weight[..., None]
            return mixed.astype(jnp.bfloat16).reshape(SEG, D)
        blocks = LEN // SEG
        attended = lax.map(segment, (queries.reshape(blocks, SEG, HEADS, head_width), keys_all.reshape(blocks, SEG, HEADS, head_width), values_all.reshape(blocks, SEG, HEADS, head_width))).reshape(LEN, D)
        encoded = (embedded.astype(jnp.float32) + jnp.dot(attended, w_out, preferred_element_type=jnp.float32)).astype(jnp.bfloat16)
        pooled = lax.optimization_barrier(jnp.sum(encoded.astype(jnp.float32), axis=0)) / LEN
        return (encoded, pooled)
    encoded, pooled = lax.map(one_slide, tiles)
    projected_rows = jnp.dot(pooled, w_head.astype(jnp.float32), precision=lax.Precision.HIGHEST)
    slide_unit_vectors = unit_rows(projected_rows)
    report_vectors = unit_rows(report_emb.astype(jnp.float32))
    logits, loss = contrastive(slide_unit_vectors, report_vectors, slide_code, report_code)
    return (encoded, slide_unit_vectors, logits, loss)
```

```python
import functools
import math

import jax
import jax.numpy as jnp
from jax import lax
from jax.experimental import pallas as pl
from jax.experimental.pallas import tpu as pltpu
from jax.sharding import PartitionSpec as P

RATE = 32
LANES = 128
SOFTMAX_TEMPER = 1.0 / 0.07
NORM_EPS = 1e-05
NT = (((1,), (1,)), ((), ()))
NN = (((1,), (0,)), ((), ()))
VMEM_LIMIT = 48 << 20


def layer_norm(inputs, gain):
    floats = inputs.astype(jnp.float32)
    centre = jnp.mean(floats, axis=-1, keepdims=True)
    spread = jnp.mean(jnp.square(floats - centre), axis=-1, keepdims=True)
    return (floats - centre) * lax.rsqrt(spread + NORM_EPS) * gain


def unit_rows(matrix):
    return matrix * lax.rsqrt(jnp.sum(matrix * matrix, axis=-1, keepdims=True) + 1e-06)


def contrastive(slide_unit_vectors, report_vectors, slide_codes, report_codes):
    logits = SOFTMAX_TEMPER * jnp.dot(
        slide_unit_vectors, report_vectors.T, precision=lax.Precision.HIGHEST
    )
    count = logits.shape[0]
    same = (slide_codes[:, None] == report_codes[None, :]) | jnp.eye(count, dtype=bool)
    positive = jnp.where(same, 1.0, 0.0).astype(logits.dtype)
    row_peak = jnp.max(logits, axis=1, keepdims=True)
    row_lse = row_peak + jnp.log(jnp.sum(jnp.exp(logits - row_peak), axis=1, keepdims=True))
    col_peak = jnp.max(logits, axis=0, keepdims=True)
    col_lse = col_peak + jnp.log(jnp.sum(jnp.exp(logits - col_peak), axis=0, keepdims=True))
    slide_terms = -jnp.sum(positive * (logits - row_lse), axis=1) / jnp.sum(positive, axis=1)
    report_terms = -jnp.sum(positive * (logits - col_lse), axis=0) / jnp.sum(positive, axis=0)
    loss = 0.5 * (jnp.mean(slide_terms) + jnp.mean(report_terms))
    return (logits, loss)


def share_with_group(row, axis):
    size = lax.axis_size(axis)
    copies = jnp.broadcast_to(row[None], (size,) + row.shape)
    return lax.all_to_all(copies, axis, 0, 0, tiled=True)


def swap_halves(x, axis):
    return lax.ppermute(x, axis, [(i, i ^ 1) for i in range(lax.axis_size(axis))])


def head_window(head, width):
    first = head * width // LANES * LANES
    last = -(-(head * width + width) // LANES) * LANES
    return first, last, head * width - first


def in_head_lanes(head, width):
    first, last, offset = head_window(head, width)
    lane = lax.broadcasted_iota(jnp.int32, (1, last - first), 1)
    return (lane >= offset) & (lane < offset + width)


def head_softmax(queries, keys, values, head, width):
    first, last, offset = head_window(head, width)
    mine = in_head_lanes(head, width)
    masked = jnp.where(mine, queries[:, first:last], jnp.zeros((), queries.dtype))
    scores = lax.dot_general(masked, keys[:, first:last], NT, preferred_element_type=jnp.float32)
    peak = jnp.max(scores, axis=1, keepdims=True)
    weights = jnp.exp(scores - peak).astype(jnp.bfloat16)
    padded = jnp.where(mine, values[:, first:last], jnp.ones((), values.dtype))
    mixed = lax.dot_general(weights, padded, NN, preferred_element_type=jnp.float32)
    spare = offset + width if offset + width < last - first else 0
    return peak, mixed[:, spare : spare + 1], mixed


def far_rows_kernel(x_ref, wk_ref, wv_ref, chosen_ref, out_ref):
    rows, width = x_ref.shape
    half = width // 2
    chosen = chosen_ref[...]
    for place, w_ref in enumerate((wk_ref, wv_ref)):
        full = jnp.dot(x_ref[...], w_ref[...], preferred_element_type=jnp.float32)
        grouped = full.reshape(rows // RATE, RATE, width) * chosen[None]
        picked = jnp.sum(grouped, axis=1).astype(out_ref.dtype)
        for part in range(2):
            out_ref[part, :, place * half : (place + 1) * half] = picked[
                :, part * half : (part + 1) * half
            ]


def near_kernel(part_ref, own_ref, other_ref, wq_ref, wk_ref, wv_ref, q_ref, mixed_ref, stats_ref,
                k_scr, v_scr, *, head_width, score_scale):
    step = pl.program_id(0)
    rows = own_ref.shape[0]
    half = wq_ref.shape[1]
    heads = half // head_width

    @pl.when(step == 0)
    def _():
        for place, x_ref in enumerate((own_ref, other_ref)):
            span = slice(place * rows, (place + 1) * rows)
            x = x_ref[...]
            q = jnp.dot(x, wq_ref[...], preferred_element_type=jnp.float32) * score_scale
            q_ref[span, :] = q.astype(q_ref.dtype)
            k = jnp.dot(x, wk_ref[...], preferred_element_type=jnp.float32)
            k_scr[span, :] = k.astype(k_scr.dtype)
            v = jnp.dot(x, wv_ref[...], preferred_element_type=jnp.float32)
            v_scr[span, :] = v.astype(v_scr.dtype)

    queries = q_ref[pl.ds(pl.multiple_of(step * rows, rows), rows), :]
    lane = lax.broadcasted_iota(jnp.int32, (1, LANES), 1)
    stats = jnp.zeros((rows, LANES), jnp.float32)
    for head in range(heads):
        first, last, _ = head_window(head, head_width)
        peak, total, mixed = head_softmax(queries, k_scr[...], v_scr[...], head, head_width)
        mine = in_head_lanes(head, head_width)
        if head == 0:
            mixed_ref[:, first:last] = mixed
        else:
            mixed_ref[:, first:last] = jnp.where(mine, mixed, mixed_ref[:, first:last])
        stats = jnp.where(lane == head, peak, stats)
        stats = jnp.where(lane == heads + head, total, stats)
    stats_ref[...] = stats


def far_kernel(q_ref, far_ref, near_ref, stats_ref, out_ref, sum_ref, acc_scr, *, head_width):
    half = q_ref.shape[1]
    heads = half // head_width
    keys, values = far_ref[:, :half], far_ref[:, half:]
    queries = q_ref[...]
    for head in range(heads):
        first, last, _ = head_window(head, head_width)
        peak, total, mixed = head_softmax(queries, keys, values, head, head_width)
        near_peak = stats_ref[:, head : head + 1]
        near_total = stats_ref[:, heads + head : heads + head + 1]
        highest = jnp.maximum(peak, near_peak)
        far_factor = jnp.exp(peak - highest)
        near_factor = jnp.exp(near_peak - highest)
        share = 1.0 / (total * far_factor + near_total * near_factor)
        mine = in_head_lanes(head, head_width)
        joined = mixed * (far_factor * share) + near_ref[:, first:last] * (near_factor * share)
        if head == 0:
            acc_scr[:, first:last] = joined
        else:
            acc_scr[:, first:last] = jnp.where(mine, joined, acc_scr[:, first:last])
    out_ref[...] = acc_scr[...].astype(out_ref.dtype)

    @pl.when(pl.program_id(0) == 0)
    def _():
        sum_ref[...] = jnp.zeros_like(sum_ref)

    sum_ref[...] += jnp.sum(acc_scr[...], axis=0, keepdims=True)


def on_device(
    tiles,
    w_embed,
    attn_gain,
    w_query,
    w_key,
    w_value,
    w_out,
    w_head,
    head_offset,
    slide_code,
    report_emb,
    report_code,
):
    _, rows, in_width = tiles.shape
    width = w_embed.shape[1]
    half = width // 2
    heads_count = head_offset.shape[0]
    head_width = width // heads_count
    ranks = lax.axis_size("seq")
    score_scale = 1.0 / math.sqrt(head_width)
    part = lax.axis_index("seq") % 2
    params = pltpu.CompilerParams(vmem_limit_bytes=VMEM_LIMIT)

    embedded = jnp.dot(
        tiles.reshape(rows, in_width), w_embed, preferred_element_type=jnp.float32
    ).astype(jnp.bfloat16)
    normed = layer_norm(embedded, attn_gain).astype(jnp.bfloat16)
    other_normed = swap_halves(normed, "seq")

    lane_offset = jnp.broadcast_to(head_offset[:, None], (heads_count, head_width)).reshape(1, width)
    chosen = (jnp.arange(RATE, dtype=jnp.int32)[:, None] == lane_offset).astype(jnp.float32)
    far_rows = rows // RATE
    payload = pl.pallas_call(
        far_rows_kernel,
        out_shape=jax.ShapeDtypeStruct((2, far_rows, width), jnp.bfloat16),
        compiler_params=params,
        name="far_rows",
    )(normed, w_key, w_value, chosen)
    payload = jnp.broadcast_to(payload[None], (ranks // 2, 2, far_rows, width))
    payload = payload.reshape(ranks, far_rows, width)
    far = lax.all_to_all(payload, "seq", 0, 0, tiled=True).reshape(ranks * far_rows, width)

    weight_spec = pl.BlockSpec((width, half), lambda i, p: (0, p[0]))
    whole = pl.BlockSpec((rows, width), lambda i, p: (0, 0))
    queries, near_mixed, stats = pl.pallas_call(
        functools.partial(near_kernel, head_width=head_width, score_scale=score_scale),
        grid_spec=pltpu.PrefetchScalarGridSpec(
            num_scalar_prefetch=1,
            grid=(2,),
            in_specs=[whole, whole, weight_spec, weight_spec, weight_spec],
            out_specs=[
                pl.BlockSpec((2 * rows, half), lambda i, p: (0, 0)),
                pl.BlockSpec((rows, half), lambda i, p: (i, 0)),
                pl.BlockSpec((rows, LANES), lambda i, p: (i, 0)),
            ],
            scratch_shapes=[
                pltpu.VMEM((2 * rows, half), jnp.bfloat16),
                pltpu.VMEM((2 * rows, half), jnp.bfloat16),
            ],
        ),
        out_shape=[
            jax.ShapeDtypeStruct((2 * rows, half), jnp.bfloat16),
            jax.ShapeDtypeStruct((2 * rows, half), jnp.float32),
            jax.ShapeDtypeStruct((2 * rows, LANES), jnp.float32),
        ],
        compiler_params=params,
        cost_estimate=pl.CostEstimate(
            flops=12_000_000_000, bytes_accessed=8_000_000, transcendentals=8_000_000
        ),
        name="near_attention",
    )(part.reshape(1), normed, other_normed, w_query, w_key, w_value)

    attended, attended_sum = pl.pallas_call(
        functools.partial(far_kernel, head_width=head_width),
        grid=(2,),
        in_specs=[
            pl.BlockSpec((rows, half), lambda i: (i, 0)),
            pl.BlockSpec((ranks * far_rows, width), lambda i: (0, 0)),
            pl.BlockSpec((rows, half), lambda i: (i, 0)),
            pl.BlockSpec((rows, LANES), lambda i: (i, 0)),
        ],
        out_specs=[
            pl.BlockSpec((rows, half), lambda i: (i, 0)),
            pl.BlockSpec((1, half), lambda i: (0, 0)),
        ],
        out_shape=[
            jax.ShapeDtypeStruct((2 * rows, half), jnp.bfloat16),
            jax.ShapeDtypeStruct((1, half), jnp.float32),
        ],
        scratch_shapes=[pltpu.VMEM((rows, half), jnp.float32)],
        compiler_params=params,
        cost_estimate=pl.CostEstimate(
            flops=6_000_000_000, bytes_accessed=6_000_000, transcendentals=4_000_000
        ),
        name="far_attention",
    )(queries, far, near_mixed, stats)

    local_sum = jnp.sum(embedded, axis=0, dtype=jnp.float32, keepdims=True)
    sums = share_with_group(jnp.concatenate((local_sum, attended_sum), axis=1), "seq")
    sums = jnp.sum(sums.reshape(ranks // 2, 2, width + half), axis=0)
    embedded_sum = jnp.sum(sums[:, :width], axis=0, keepdims=True)
    attended_total = sums[:, width:].reshape(1, width)
    mixed_total = jnp.dot(
        attended_total, w_out.astype(jnp.float32), precision=lax.Precision.HIGHEST
    )
    pooled = (embedded_sum + mixed_total) / (rows * ranks)
    slide_unit_vectors = unit_rows(
        jnp.dot(pooled, w_head.astype(jnp.float32), precision=lax.Precision.HIGHEST)
    )

    own_half, lent_half = attended[:rows], attended[rows:]
    other_half = swap_halves(lent_half, "seq")
    joined = jnp.where(
        part == 1,
        jnp.concatenate((other_half, own_half), axis=1),
        jnp.concatenate((own_half, other_half), axis=1),
    )
    encoded = embedded.astype(jnp.float32) + jnp.dot(
        joined, w_out, preferred_element_type=jnp.float32
    )
    encoded = encoded.astype(jnp.bfloat16).reshape(1, rows, width)

    report_local = unit_rows(report_emb.astype(jnp.float32))
    codes = jnp.stack((slide_code, report_code), axis=1).astype(jnp.float32)
    early = share_with_group(
        jnp.concatenate((report_local, jnp.pad(codes, ((0, 0), (0, LANES - 2)))), axis=1), "slide"
    )[:, 0]
    all_vecs = share_with_group(slide_unit_vectors, "slide")[:, 0]
    logits, loss = contrastive(all_vecs, early[:, :width], early[:, width], early[:, width + 1])
    return (encoded, slide_unit_vectors, logits, loss)


def solution(mesh):
    return jax.shard_map(
        on_device,
        mesh=mesh,
        in_specs=(
            P("slide", "seq", None),
            P(),
            P(),
            P(),
            P(),
            P(),
            P(),
            P(),
            P(),
            P("slide"),
            P("slide", None),
            P("slide"),
        ),
        out_specs=(P("slide", "seq", None), P("slide", None), P(), P()),
        check_vma=False,
    )
```

```python
import functools
import math

import jax
import jax.numpy as jnp
from jax import lax
from jax.experimental import pallas as pl
from jax.experimental.pallas import tpu as pltpu
from jax.sharding import Mesh, PartitionSpec as P

RATE = 32
LANES = 128
PACK = (8, 256)
SOFTMAX_TEMPER = 1.0 / 0.07
NORM_EPS = 1e-05
NT = (((1,), (1,)), ((), ()))
NN = (((1,), (0,)), ((), ()))
VMEM_LIMIT = 56 << 20
SEQ_AXES = ("x", "z_hi", "y")
F32 = jnp.float32
BF16 = jnp.bfloat16


def swap_with(x, axis):
    return lax.ppermute(x, axis, [(i, i ^ 1) for i in range(lax.axis_size(axis))])


def head_window(head, width):
    first = head * width // LANES * LANES
    last = -(-(head * width + width) // LANES) * LANES
    return first, last, head * width - first


def in_head_lanes(head, width):
    first, last, offset = head_window(head, width)
    lane = lax.broadcasted_iota(jnp.int32, (1, last - first), 1)
    return (lane >= offset) & (lane < offset + width)


def attend(queries, keys, values, head_width, mixed_ref, lse_ref, rows):
    for head in range(queries.shape[1] // head_width):
        first, last, _ = head_window(head, head_width)
        mine = in_head_lanes(head, head_width)
        masked = jnp.where(mine, queries[:, first:last], jnp.zeros((), queries.dtype))
        scores = lax.dot_general(masked, keys[:, first:last], NT, preferred_element_type=F32)
        peak = jnp.max(scores, axis=1, keepdims=True)
        weights = jnp.exp(scores - peak)
        total = jnp.sum(weights, axis=1, keepdims=True)
        mixed = lax.dot_general(
            weights.astype(BF16), values[:, first:last], NN, preferred_element_type=F32
        )
        mixed = mixed * (1.0 / total)
        lse = jnp.broadcast_to(peak + jnp.log(total), mixed.shape)
        if head > 0:
            mixed = jnp.where(mine, mixed, mixed_ref[rows, first:last])
            lse = jnp.where(mine, lse, lse_ref[rows, first:last])
        mixed_ref[rows, first:last] = mixed
        lse_ref[rows, first:last] = lse


def embed_kernel(x_ref, w_ref, gain_ref, embedded_ref, normed_ref, sum_ref, acc_scr):
    step = pl.program_id(0)

    @pl.when(step == 0)
    def _():
        acc_scr[...] = jnp.dot(x_ref[...], w_ref[...], preferred_element_type=F32)

    @pl.when(step > 0)
    def _():
        acc_scr[...] += jnp.dot(x_ref[...], w_ref[...], preferred_element_type=F32)

    @pl.when(step == pl.num_programs(0) - 1)
    def _():
        embedded = acc_scr[...].astype(BF16)
        embedded_ref[...] = embedded
        floats = embedded.astype(F32)
        centred = floats - jnp.mean(floats, axis=1, keepdims=True)
        spread = jnp.mean(centred * centred, axis=1, keepdims=True)
        normed = centred * lax.rsqrt(spread + NORM_EPS) * gain_ref[...]
        normed_ref[...] = normed.astype(BF16)
        sum_ref[...] = jnp.sum(floats, axis=0, keepdims=True)


def own_rows_kernel(part_ref, x_ref, wk_ref, wv_ref, offset_ref, far_ref, k_ref, v_ref):
    rows, width = x_ref.shape
    half = width // 2
    phase = lax.broadcasted_iota(jnp.int32, (RATE, width), 0)
    chosen = jnp.where(phase == offset_ref[...], 1.0, 0.0)
    upper = part_ref[0] == 1
    for place, (w_ref, half_ref) in enumerate(((wk_ref, k_ref), (wv_ref, v_ref))):
        full = jnp.dot(x_ref[...], w_ref[...], preferred_element_type=F32)
        half_ref[...] = jnp.where(upper, full[:, half:], full[:, :half]).astype(BF16)
        grouped = full.reshape(rows // RATE, RATE, width) * chosen[None]
        picked = jnp.sum(grouped, axis=1).astype(BF16)
        for part in range(2):
            far_ref[part, :, place * half : (place + 1) * half] = picked[
                :, part * half : (part + 1) * half
            ]


def near_kernel(part_ref, own_ref, other_ref, k_ref, v_ref, wq_ref, wk_ref, wv_ref,
                q_ref, mixed_ref, lse_ref, k_scr, v_scr, *, head_width, score_scale):
    step = pl.program_id(0)
    rows = own_ref.shape[0]

    @pl.when(step == 0)
    def _():
        for place, x_ref in enumerate((own_ref, other_ref)):
            q = jnp.dot(x_ref[...], wq_ref[...], preferred_element_type=F32) * score_scale
            q_ref[place * rows : (place + 1) * rows, :] = q.astype(BF16)
        for scr, own_half_ref, w_ref in ((k_scr, k_ref, wk_ref), (v_scr, v_ref, wv_ref)):
            scr[:rows, :] = own_half_ref[...]
            other = jnp.dot(other_ref[...], w_ref[...], preferred_element_type=F32)
            scr[rows:, :] = other.astype(BF16)

    queries = q_ref[pl.ds(pl.multiple_of(step * rows, rows), rows), :]
    attend(queries, k_scr[...], v_scr[...], head_width, mixed_ref, lse_ref, slice(None))


def far_kernel(q_ref, far_ref, near_ref, near_lse_ref, embedded_sum_ref, out_ref, pack_ref,
               mixed_scr, lse_scr, sum_scr, *, head_width):
    step = pl.program_id(0)
    half = q_ref.shape[1]
    attend(
        q_ref[...], far_ref[:, :half], far_ref[:, half:], head_width, mixed_scr, lse_scr, slice(None)
    )
    near_share = 1.0 / (1.0 + jnp.exp(lse_scr[...] - near_lse_ref[...]))
    far_mixed = mixed_scr[...]
    attended = far_mixed + (near_ref[...] - far_mixed) * near_share
    out_ref[...] = attended.astype(BF16)

    @pl.when(step == 0)
    def _():
        sum_scr[...] = jnp.zeros_like(sum_scr)

    sum_scr[...] += jnp.sum(attended, axis=0, keepdims=True)

    @pl.when(step == pl.num_programs(0) - 1)
    def _():
        pad = jnp.zeros((1, pack_ref.shape[1] * pack_ref.shape[2] - 3 * half), F32)
        packed = pack_row((embedded_sum_ref[...], sum_scr[...], pad))
        pack_ref[...] = jnp.broadcast_to(packed[None], pack_ref.shape)


def pack_row(pieces):
    flat = jnp.concatenate(pieces, axis=1)
    rows, lanes = PACK
    return jnp.concatenate([flat[:, r * lanes : (r + 1) * lanes] for r in range(rows)], axis=0)


def exact_row_times(row, matrix):
    top = row.astype(BF16).astype(F32)
    middle = (row - top).astype(BF16).astype(F32)
    low = row - top - middle
    parts = jnp.concatenate((top, middle, low, jnp.zeros((13, row.shape[1]), F32)), axis=0)
    product = jnp.dot(parts.astype(BF16), matrix, preferred_element_type=F32)
    return jnp.sum(product, axis=0, keepdims=True)


def unit_row(row):
    return row * lax.rsqrt(jnp.sum(row * row, axis=1, keepdims=True) + 1e-06)


def pooled_kernel(slide_code_ref, report_code_ref, sums_ref, w_out_ref, w_head_ref, report_ref,
                  unit_ref, pack_ref, *, length):
    peers = sums_ref.shape[0]
    width = w_out_ref.shape[0]
    half = width // 2
    lanes = PACK[1]
    even = sums_ref[0]
    odd = sums_ref[1]
    for peer in range(2, peers, 2):
        even = even + sums_ref[peer]
        odd = odd + sums_ref[peer + 1]

    def flat(packed):
        return jnp.concatenate([packed[r : r + 1, :] for r in range(PACK[0])], axis=1)

    even, odd = flat(even), flat(odd)
    embedded_sum = even[:, :width] + odd[:, :width]
    attended_sum = jnp.concatenate(
        (even[:, width : width + half], odd[:, width : width + half]), axis=1
    )
    pooled = (embedded_sum + exact_row_times(attended_sum, w_out_ref[...])) * (1.0 / length)
    unit = unit_row(exact_row_times(pooled, w_head_ref[...]))
    unit_ref[...] = unit
    lane = lax.broadcasted_iota(jnp.int32, (1, 2 * lanes), 1)
    codes = jnp.where(
        lane == 0,
        slide_code_ref[0].astype(F32),
        jnp.where(lane == 1, report_code_ref[0].astype(F32), 0.0),
    )
    packed = pack_row((unit, unit_row(report_ref[...].astype(F32)), codes))
    pack_ref[...] = jnp.broadcast_to(packed[None], pack_ref.shape)


def contrast_kernel(all_ref, logits_ref, loss_ref):
    count = all_ref.shape[0]
    lanes = PACK[1]
    logits = jnp.zeros((count, count), F32)
    parts = 768 // lanes
    for r in range(parts):
        logits += lax.dot_general(
            all_ref[:, r, :], all_ref[:, parts + r, :], NT,
            precision=lax.Precision.HIGHEST, preferred_element_type=F32,
        )
    logits = logits * SOFTMAX_TEMPER
    logits_ref[...] = logits
    codes = all_ref[:, 2 * parts, :]
    down = lax.broadcasted_iota(jnp.int32, (count, count), 0)
    across = lax.broadcasted_iota(jnp.int32, (count, count), 1)
    diagonal = down == across
    slide_codes = codes[:, 0:1]
    report_codes = jnp.sum(jnp.where(diagonal, codes[:, 1:2], 0.0), axis=0, keepdims=True)
    positive = jnp.where((slide_codes == report_codes) | diagonal, 1.0, 0.0)

    def terms(axis):
        peak = jnp.max(logits, axis=axis, keepdims=True)
        lse = peak + jnp.log(jnp.sum(jnp.exp(logits - peak), axis=axis, keepdims=True))
        picked = jnp.sum(positive * (logits - lse), axis=axis, keepdims=True)
        return -picked / jnp.sum(positive, axis=axis, keepdims=True)

    both = jnp.sum(terms(1), axis=0, keepdims=True) + jnp.sum(terms(0), axis=1, keepdims=True)
    loss_ref[...] = both * (0.5 / count)


def on_device(
    tiles,
    w_embed,
    attn_gain,
    w_query,
    w_key,
    w_value,
    w_out,
    w_head,
    head_offset,
    slide_code,
    report_emb,
    report_code,
):
    _, rows, in_width = tiles.shape
    width = w_embed.shape[1]
    half = width // 2
    heads_count = head_offset.shape[0]
    head_width = width // heads_count
    ranks = lax.axis_size(SEQ_AXES)
    plane = lax.axis_size(("x", "y"))
    score_scale = 1.0 / math.sqrt(head_width)
    part = lax.axis_index("y") % 2
    parts = part.reshape(1)
    params = pltpu.CompilerParams(vmem_limit_bytes=VMEM_LIMIT)

    steps = 3
    depth = in_width // steps
    embedded, normed, embedded_sum = pl.pallas_call(
        embed_kernel,
        grid=(steps,),
        in_specs=[
            pl.BlockSpec((rows, depth), lambda i: (0, i)),
            pl.BlockSpec((depth, width), lambda i: (i, 0)),
            pl.BlockSpec((1, width), lambda i: (0, 0)),
        ],
        out_specs=[
            pl.BlockSpec((rows, width), lambda i: (0, 0)),
            pl.BlockSpec((rows, width), lambda i: (0, 0)),
            pl.BlockSpec((1, width), lambda i: (0, 0)),
        ],
        out_shape=[
            jax.ShapeDtypeStruct((rows, width), BF16),
            jax.ShapeDtypeStruct((rows, width), BF16),
            jax.ShapeDtypeStruct((1, width), F32),
        ],
        scratch_shapes=[pltpu.VMEM((rows, width), F32)],
        compiler_params=params,
        name="embed",
    )(tiles.reshape(rows, in_width), w_embed, attn_gain.reshape(1, width))
    other_normed = swap_with(normed, "y")

    lane_offset = jnp.broadcast_to(head_offset[:, None], (heads_count, head_width)).reshape(1, width)
    far_rows = rows // RATE
    smem = pl.BlockSpec(memory_space=pltpu.SMEM)
    vmem = pl.BlockSpec(memory_space=pltpu.VMEM)
    far_own, keys_own, values_own = pl.pallas_call(
        own_rows_kernel,
        in_specs=[smem, vmem, vmem, vmem, vmem],
        out_shape=[
            jax.ShapeDtypeStruct((2, far_rows, width), BF16),
            jax.ShapeDtypeStruct((rows, half), BF16),
            jax.ShapeDtypeStruct((rows, half), BF16),
        ],
        compiler_params=params,
        name="own_rows",
    )(parts, normed, w_key, w_value, lane_offset)
    far_pair = jnp.stack((far_own, swap_with(far_own, "z_hi")), axis=1)
    far_pair = far_pair.reshape(2, 2 * far_rows, width)
    payload = jnp.broadcast_to(far_pair[None], (plane // 2, 2, 2 * far_rows, width))
    payload = payload.reshape(plane, 2 * far_rows, width)
    far = lax.all_to_all(payload, ("x", "y"), 0, 0, tiled=True).reshape(ranks * far_rows, width)

    weight_spec = pl.BlockSpec((width, half), lambda i, p: (0, p[0]))
    whole = pl.BlockSpec((rows, width), lambda i, p: (0, 0))
    whole_half = pl.BlockSpec((rows, half), lambda i, p: (0, 0))
    row_block = pl.BlockSpec((rows, half), lambda i, p: (i, 0))
    queries, near_mixed, near_lse = pl.pallas_call(
        functools.partial(near_kernel, head_width=head_width, score_scale=score_scale),
        grid_spec=pltpu.PrefetchScalarGridSpec(
            num_scalar_prefetch=1,
            grid=(2,),
            in_specs=[whole, whole, whole_half, whole_half, weight_spec, weight_spec, weight_spec],
            out_specs=[pl.BlockSpec((2 * rows, half), lambda i, p: (0, 0)), row_block, row_block],
            scratch_shapes=[
                pltpu.VMEM((2 * rows, half), BF16),
                pltpu.VMEM((2 * rows, half), BF16),
            ],
        ),
        out_shape=[
            jax.ShapeDtypeStruct((2 * rows, half), BF16),
            jax.ShapeDtypeStruct((2 * rows, half), F32),
            jax.ShapeDtypeStruct((2 * rows, half), F32),
        ],
        compiler_params=params,
        cost_estimate=pl.CostEstimate(
            flops=12_000_000_000, bytes_accessed=8_000_000, transcendentals=8_000_000
        ),
        name="near_attention",
    )(parts, normed, other_normed, keys_own, values_own, w_query, w_key, w_value)

    row_block = pl.BlockSpec((rows, half), lambda i: (i, 0))
    attended, sums = pl.pallas_call(
        functools.partial(far_kernel, head_width=head_width),
        grid=(2,),
        in_specs=[
            row_block,
            pl.BlockSpec((ranks * far_rows, width), lambda i: (0, 0)),
            row_block,
            row_block,
            pl.BlockSpec((1, width), lambda i: (0, 0)),
        ],
        out_specs=[row_block, pl.BlockSpec((ranks,) + PACK, lambda i: (0, 0, 0))],
        out_shape=[
            jax.ShapeDtypeStruct((2 * rows, half), BF16),
            jax.ShapeDtypeStruct((ranks,) + PACK, F32),
        ],
        scratch_shapes=[
            pltpu.VMEM((rows, half), F32),
            pltpu.VMEM((rows, half), F32),
            pltpu.VMEM((1, half), F32),
        ],
        compiler_params=params,
        cost_estimate=pl.CostEstimate(
            flops=6_000_000_000, bytes_accessed=6_000_000, transcendentals=4_000_000
        ),
        name="far_attention",
    )(queries, far, near_mixed, near_lse, embedded_sum)

    own_half, lent_half = attended[:rows], attended[rows:]
    other_half = swap_with(lent_half, "y")
    joined = jnp.where(
        part == 1,
        jnp.concatenate((other_half, own_half), axis=1),
        jnp.concatenate((own_half, other_half), axis=1),
    )
    encoded = embedded.astype(F32) + jnp.dot(joined, w_out, preferred_element_type=F32)
    encoded = encoded.astype(BF16).reshape(1, rows, width)

    sums = lax.all_to_all(sums, SEQ_AXES, 0, 0, tiled=True)
    sums, encoded = lax.optimization_barrier((sums, encoded))
    slides = lax.axis_size("slide")
    slide_unit_vectors, packed = pl.pallas_call(
        functools.partial(pooled_kernel, length=rows * ranks),
        in_specs=[smem, smem, vmem, vmem, vmem, vmem],
        out_shape=[
            jax.ShapeDtypeStruct((1, width), F32),
            jax.ShapeDtypeStruct((slides,) + PACK, F32),
        ],
        compiler_params=params,
        name="pooled",
    )(slide_code, report_code, sums, w_out, w_head, report_emb)
    everyone = lax.all_to_all(packed, "slide", 0, 0, tiled=True)
    logits, loss = pl.pallas_call(
        contrast_kernel,
        in_specs=[vmem],
        out_shape=[
            jax.ShapeDtypeStruct((slides, slides), F32),
            jax.ShapeDtypeStruct((1, 1), F32),
        ],
        compiler_params=params,
        name="contrast",
    )(everyone)
    return (encoded, slide_unit_vectors, logits, loss.reshape(()))


def solution(mesh):
    split = Mesh(mesh.devices.reshape(4, 2, 4, 8), SEQ_AXES + ("slide",))
    rows = P("slide", SEQ_AXES, None)
    return jax.shard_map(
        on_device,
        mesh=split,
        in_specs=(
            rows,
            P(),
            P(),
            P(),
            P(),
            P(),
            P(),
            P(),
            P(),
            P("slide"),
            P("slide", None),
            P("slide"),
        ),
        out_specs=(rows, P("slide", None), P(), P()),
        check_vma=False,
    )
```

```python
import functools
import math

import jax
import jax.numpy as jnp
from jax import lax
from jax.experimental import pallas as pl
from jax.experimental.pallas import tpu as pltpu
from jax.sharding import Mesh, PartitionSpec as P

RATE = 32
LANES = 128
PACK = (8, 256)
SOFTMAX_TEMPER = 1.0 / 0.07
NORM_EPS = 1e-05
NT = (((1,), (1,)), ((), ()))
NN = (((1,), (0,)), ((), ()))
ATTEND_VMEM = 32 << 20
SMALL_VMEM = 16 << 20
EMBED_VMEM = 58 << 20
EMBED_STEPS = 3
SEQ_AXES = ("x", "z_hi", "y")
F32 = jnp.float32
BF16 = jnp.bfloat16


def swap_with(x, axis):
    return lax.ppermute(x, axis, [(i, i ^ 1) for i in range(lax.axis_size(axis))])


def head_window(head, width):
    first = head * width // LANES * LANES
    last = -(-(head * width + width) // LANES) * LANES
    return first, last, head * width - first


def in_head_lanes(head, width):
    first, last, offset = head_window(head, width)
    lane = lax.broadcasted_iota(jnp.int32, (1, last - first), 1)
    return (lane >= offset) & (lane < offset + width)


def attend(queries, keys, values, head_width, mixed_ref, lse_ref, rows):
    for head in range(queries.shape[1] // head_width):
        first, last, _ = head_window(head, head_width)
        mine = in_head_lanes(head, head_width)
        masked = jnp.where(mine, queries[:, first:last], jnp.zeros((), queries.dtype))
        scores = lax.dot_general(masked, keys[:, first:last], NT, preferred_element_type=F32)
        peak = jnp.max(scores, axis=1, keepdims=True)
        weights = jnp.exp(scores - peak)
        total = jnp.sum(weights, axis=1, keepdims=True)
        mixed = lax.dot_general(
            weights.astype(BF16), values[:, first:last], NN, preferred_element_type=F32
        )
        mixed = mixed * (1.0 / total)
        lse = jnp.broadcast_to(peak + jnp.log(total), mixed.shape)
        if head > 0:
            mixed = jnp.where(mine, mixed, mixed_ref[rows, first:last])
            lse = jnp.where(mine, lse, lse_ref[rows, first:last])
        mixed_ref[rows, first:last] = mixed
        lse_ref[rows, first:last] = lse


def merge_states(one, one_lse, two, two_lse):
    share = 1.0 / (1.0 + jnp.exp(two_lse - one_lse))
    return two + (one - two) * share


def embed_kernel(x_hbm, w_hbm, gain_ref, embedded_ref, normed_ref, sum_ref, x_scr, w_scr, sems):
    depth = x_scr.shape[2]
    halves = 2
    part_rows, part_depth = x_scr.shape[1] // halves, depth // halves
    copies = []
    for step in range(EMBED_STEPS):
        group = []
        for i in range(halves):
            rows = slice(i * part_rows, (i + 1) * part_rows)
            group.append(
                pltpu.make_async_copy(
                    x_hbm.at[rows, step * depth : (step + 1) * depth],
                    x_scr.at[step, rows, :],
                    sems.at[step, i],
                )
            )
            first = step * depth + i * part_depth
            group.append(
                pltpu.make_async_copy(
                    w_hbm.at[first : first + part_depth, :],
                    w_scr.at[step, i * part_depth : (i + 1) * part_depth, :],
                    sems.at[step, halves + i],
                )
            )
        for copy in group:
            copy.start()
        copies.append(group)
    total = None
    for step, group in enumerate(copies):
        for copy in group:
            copy.wait()
        product = jnp.dot(x_scr[step], w_scr[step], preferred_element_type=F32)
        total = product if total is None else total + product
    embedded = total.astype(BF16)
    embedded_ref[...] = embedded
    floats = embedded.astype(F32)
    centred = floats - jnp.mean(floats, axis=1, keepdims=True)
    spread = jnp.mean(centred * centred, axis=1, keepdims=True)
    normed = centred * lax.rsqrt(spread + NORM_EPS) * gain_ref[...][None, :]
    normed_ref[...] = normed.astype(BF16)
    sum_ref[...] = jnp.sum(floats, axis=0, keepdims=True)


def own_rows_kernel(part_ref, offset_ref, x_ref, wk_hbm, wv_hbm, far_ref, k_ref, v_ref,
                    w_scr, sems):
    rows, width = x_ref.shape
    half = width // 2
    heads = offset_ref.shape[0]
    pieces = sems.shape[1]
    depth = width // pieces
    copies = []
    for place, w_hbm in enumerate((wk_hbm, wv_hbm)):
        for i in range(pieces):
            span = slice(i * depth, (i + 1) * depth)
            copy = pltpu.make_async_copy(
                w_hbm.at[span, :], w_scr.at[place, span, :], sems.at[place, i]
            )
            copy.start()
            copies.append(copy)
    lane = lax.broadcasted_iota(jnp.int32, (1, width), 1)
    lane_offset = jnp.zeros((1, width), jnp.int32)
    for head in range(heads):
        lane_offset = jnp.where(lane >= head * (width // heads), offset_ref[head], lane_offset)
    phase = lax.broadcasted_iota(jnp.int32, (RATE, width), 0)
    chosen = jnp.where(phase == lane_offset, 1.0, 0.0)
    upper = part_ref[0] == 1
    for place, half_ref in enumerate((k_ref, v_ref)):
        for copy in copies[place * pieces : (place + 1) * pieces]:
            copy.wait()
        full = jnp.dot(x_ref[...], w_scr[place], preferred_element_type=F32)
        half_ref[...] = jnp.where(upper, full[:, half:], full[:, :half]).astype(BF16)
        grouped = full.reshape(rows // RATE, RATE, width) * chosen[None]
        picked = jnp.sum(grouped, axis=1).astype(BF16)
        for part in range(2):
            far_ref[part, :, place * half : (place + 1) * half] = picked[
                :, part * half : (part + 1) * half
            ]


def payload_kernel(own_ref, other_ref, out_ref):
    for place, ref in enumerate((own_ref, other_ref)):
        out_ref[:, :, place, :, :] = jnp.broadcast_to(ref[...][None], out_ref.shape[:2] + ref.shape[1:])


def own_kernel(part_ref, x_ref, k_ref, v_ref, wq_ref, q_ref, mixed_ref, lse_ref, *, head_width,
               score_scale):
    q = jnp.dot(x_ref[...], wq_ref[...], preferred_element_type=F32) * score_scale
    q_ref[...] = q.astype(BF16)
    attend(q_ref[...], k_ref[...], v_ref[...], head_width, mixed_ref, lse_ref, slice(None))


def near_kernel(part_ref, other_ref, k_ref, v_ref, q_own_ref, own_mixed_ref, own_lse_ref,
                wq_ref, wk_ref, wv_ref, q_ref, mixed_ref, lse_ref, k_scr, v_scr,
                *, head_width, score_scale):
    step = pl.program_id(0)
    rows = other_ref.shape[0]

    @pl.when(step == 0)
    def _():
        other = other_ref[...]
        for scr, own_half_ref, w_ref in ((k_scr, k_ref, wk_ref), (v_scr, v_ref, wv_ref)):
            scr[:rows, :] = own_half_ref[...]
            scr[rows:, :] = jnp.dot(other, w_ref[...], preferred_element_type=F32).astype(BF16)
        q_ref[:rows, :] = q_own_ref[...]
        q = jnp.dot(other, wq_ref[...], preferred_element_type=F32) * score_scale
        q_ref[rows:, :] = q.astype(BF16)
        attend(q_own_ref[...], k_scr[rows:, :], v_scr[rows:, :], head_width, mixed_ref, lse_ref,
               slice(None))
        own_lse, new_lse = own_lse_ref[...], lse_ref[...]
        mixed_ref[...] = merge_states(own_mixed_ref[...], own_lse, mixed_ref[...], new_lse)
        gap = jnp.exp(-jnp.abs(own_lse - new_lse))
        lse_ref[...] = jnp.maximum(own_lse, new_lse) + jnp.log(1.0 + gap)

    @pl.when(step == 1)
    def _():
        attend(q_ref[rows:, :], k_scr[...], v_scr[...], head_width, mixed_ref, lse_ref, slice(None))


def far_kernel(q_ref, far_ref, near_ref, near_lse_ref, embedded_sum_ref, own_ref, lent_ref,
               pack_ref, mixed_scr, lse_scr, sum_scr, *, head_width):
    step = pl.program_id(0)
    half = q_ref.shape[1]
    attend(
        q_ref[...], far_ref[:, :half], far_ref[:, half:], head_width, mixed_scr, lse_scr, slice(None)
    )
    attended = merge_states(near_ref[...], near_lse_ref[...], mixed_scr[...], lse_scr[...])
    summed = jnp.sum(attended, axis=0, keepdims=True)

    @pl.when(step == 0)
    def _():
        own_ref[...] = attended.astype(BF16)
        sum_scr[...] = summed

    @pl.when(step == 1)
    def _():
        lent_ref[...] = attended.astype(BF16)
        pad = jnp.zeros((1, pack_ref.shape[1] * pack_ref.shape[2] - 3 * half), F32)
        packed = pack_row((embedded_sum_ref[...], sum_scr[...] + summed, pad))
        pack_ref[...] = jnp.broadcast_to(packed[None], pack_ref.shape)


def pack_row(pieces):
    flat = jnp.concatenate(pieces, axis=1)
    rows, lanes = PACK
    return jnp.concatenate([flat[:, r * lanes : (r + 1) * lanes] for r in range(rows)], axis=0)


def exact_row_times(row, matrix):
    top = row.astype(BF16).astype(F32)
    middle = (row - top).astype(BF16).astype(F32)
    low = row - top - middle
    parts = jnp.concatenate((top, middle, low, jnp.zeros((13, row.shape[1]), F32)), axis=0)
    product = jnp.dot(parts.astype(BF16), matrix, preferred_element_type=F32)
    return jnp.sum(product, axis=0, keepdims=True)


def unit_row(row):
    return row * lax.rsqrt(jnp.sum(row * row, axis=1, keepdims=True) + 1e-06)


def pooled_kernel(slide_code_ref, report_code_ref, sums_ref, w_out_ref, w_head_ref, report_ref,
                  unit_ref, pack_ref, *, length):
    peers = sums_ref.shape[0]
    width = w_out_ref.shape[0]
    half = width // 2
    lanes = PACK[1]
    even = sums_ref[0]
    odd = sums_ref[1]
    for peer in range(2, peers, 2):
        even = even + sums_ref[peer]
        odd = odd + sums_ref[peer + 1]

    def flat(packed):
        return jnp.concatenate([packed[r : r + 1, :] for r in range(PACK[0])], axis=1)

    even, odd = flat(even), flat(odd)
    embedded_sum = even[:, :width] + odd[:, :width]
    attended_sum = jnp.concatenate(
        (even[:, width : width + half], odd[:, width : width + half]), axis=1
    )
    pooled = (embedded_sum + exact_row_times(attended_sum, w_out_ref[...])) * (1.0 / length)
    unit = unit_row(exact_row_times(pooled, w_head_ref[...]))
    unit_ref[...] = unit
    lane = lax.broadcasted_iota(jnp.int32, (1, 2 * lanes), 1)
    codes = jnp.where(
        lane == 0,
        slide_code_ref[0].astype(F32),
        jnp.where(lane == 1, report_code_ref[0].astype(F32), 0.0),
    )
    packed = pack_row((unit, unit_row(report_ref[...].astype(F32)), codes))
    pack_ref[...] = jnp.broadcast_to(packed[None], pack_ref.shape)


def contrast_kernel(all_ref, logits_ref, loss_ref):
    count = all_ref.shape[0]
    lanes = PACK[1]
    logits = jnp.zeros((count, count), F32)
    parts = 768 // lanes
    for r in range(parts):
        logits += lax.dot_general(
            all_ref[:, r, :], all_ref[:, parts + r, :], NT,
            precision=lax.Precision.HIGHEST, preferred_element_type=F32,
        )
    logits = logits * SOFTMAX_TEMPER
    logits_ref[...] = logits
    codes = all_ref[:, 2 * parts, :]
    down = lax.broadcasted_iota(jnp.int32, (count, count), 0)
    across = lax.broadcasted_iota(jnp.int32, (count, count), 1)
    diagonal = down == across
    slide_codes = codes[:, 0:1]
    report_codes = jnp.sum(jnp.where(diagonal, codes[:, 1:2], 0.0), axis=0, keepdims=True)
    positive = jnp.where((slide_codes == report_codes) | diagonal, 1.0, 0.0)

    def terms(axis):
        peak = jnp.max(logits, axis=axis, keepdims=True)
        lse = peak + jnp.log(jnp.sum(jnp.exp(logits - peak), axis=axis, keepdims=True))
        picked = jnp.sum(positive * (logits - lse), axis=axis, keepdims=True)
        return -picked / jnp.sum(positive, axis=axis, keepdims=True)

    both = jnp.sum(terms(1), axis=0, keepdims=True) + jnp.sum(terms(0), axis=1, keepdims=True)
    loss_ref[...] = both * (0.5 / count)


def on_device(
    tiles,
    w_embed,
    attn_gain,
    w_query,
    w_key,
    w_value,
    w_out,
    w_head,
    head_offset,
    slide_code,
    report_emb,
    report_code,
):
    _, rows, in_width = tiles.shape
    width = w_embed.shape[1]
    half = width // 2
    heads_count = head_offset.shape[0]
    head_width = width // heads_count
    ranks = lax.axis_size(SEQ_AXES)
    plane = lax.axis_size(("x", "y"))
    score_scale = 1.0 / math.sqrt(head_width)
    part = lax.axis_index("y") % 2
    parts = part.reshape(1)
    params = pltpu.CompilerParams(vmem_limit_bytes=ATTEND_VMEM)
    small = pltpu.CompilerParams(vmem_limit_bytes=SMALL_VMEM)
    smem = pl.BlockSpec(memory_space=pltpu.SMEM)
    vmem = pl.BlockSpec(memory_space=pltpu.VMEM)
    anywhere = pl.BlockSpec(memory_space=pl.ANY)

    depth = in_width // EMBED_STEPS
    embedded, normed, embedded_sum = pl.pallas_call(
        embed_kernel,
        in_specs=[anywhere, anywhere, vmem],
        out_shape=[
            jax.ShapeDtypeStruct((rows, width), BF16),
            jax.ShapeDtypeStruct((rows, width), BF16),
            jax.ShapeDtypeStruct((1, width), F32),
        ],
        scratch_shapes=[
            pltpu.VMEM((EMBED_STEPS, rows, depth), BF16),
            pltpu.VMEM((EMBED_STEPS, depth, width), BF16),
            pltpu.SemaphoreType.DMA((EMBED_STEPS, 4)),
        ],
        compiler_params=pltpu.CompilerParams(vmem_limit_bytes=EMBED_VMEM),
        name="embed",
    )(tiles.reshape(rows, in_width), w_embed, attn_gain)
    other_normed = swap_with(normed, "y")

    far_rows = rows // RATE
    far_own, keys_own, values_own = pl.pallas_call(
        own_rows_kernel,
        in_specs=[smem, smem, vmem, anywhere, anywhere],
        out_shape=[
            jax.ShapeDtypeStruct((2, far_rows, width), BF16),
            jax.ShapeDtypeStruct((rows, half), BF16),
            jax.ShapeDtypeStruct((rows, half), BF16),
        ],
        scratch_shapes=[
            pltpu.VMEM((2, width, width), BF16),
            pltpu.SemaphoreType.DMA((2, 2)),
        ],
        compiler_params=small,
        name="own_rows",
    )(parts, head_offset, normed, w_key, w_value)
    far_other = swap_with(far_own, "z_hi")
    payload = pl.pallas_call(
        payload_kernel,
        in_specs=[vmem, vmem],
        out_shape=jax.ShapeDtypeStruct((plane // 2, 2, 2, far_rows, width), BF16),
        compiler_params=small,
        name="payload",
    )(far_own, far_other).reshape(plane, 2 * far_rows, width)
    far = lax.all_to_all(payload, ("x", "y"), 0, 0, tiled=True).reshape(ranks * far_rows, width)

    weight_spec = pl.BlockSpec((width, half), lambda i, p: (0, p[0]))
    whole = pl.BlockSpec((rows, width), lambda i, p: (0, 0))
    whole_half = pl.BlockSpec((rows, half), lambda i, p: (0, 0))
    row_block = pl.BlockSpec((rows, half), lambda i, p: (i, 0))
    queries_own, own_mixed, own_lse = pl.pallas_call(
        functools.partial(own_kernel, head_width=head_width, score_scale=score_scale),
        grid_spec=pltpu.PrefetchScalarGridSpec(
            num_scalar_prefetch=1,
            grid=(1,),
            in_specs=[whole, whole_half, whole_half, weight_spec],
            out_specs=[whole_half, whole_half, whole_half],
        ),
        out_shape=[
            jax.ShapeDtypeStruct((rows, half), BF16),
            jax.ShapeDtypeStruct((rows, half), F32),
            jax.ShapeDtypeStruct((rows, half), F32),
        ],
        compiler_params=params,
        cost_estimate=pl.CostEstimate(
            flops=3_000_000_000, bytes_accessed=4_000_000, transcendentals=2_000_000
        ),
        name="own_attention",
    )(parts, normed, keys_own, values_own, w_query)

    queries, near_mixed, near_lse = pl.pallas_call(
        functools.partial(near_kernel, head_width=head_width, score_scale=score_scale),
        grid_spec=pltpu.PrefetchScalarGridSpec(
            num_scalar_prefetch=1,
            grid=(2,),
            in_specs=[whole] + [whole_half] * 5 + [weight_spec] * 3,
            out_specs=[pl.BlockSpec((2 * rows, half), lambda i, p: (0, 0)), row_block, row_block],
            scratch_shapes=[
                pltpu.VMEM((2 * rows, half), BF16),
                pltpu.VMEM((2 * rows, half), BF16),
            ],
        ),
        out_shape=[
            jax.ShapeDtypeStruct((2 * rows, half), BF16),
            jax.ShapeDtypeStruct((2 * rows, half), F32),
            jax.ShapeDtypeStruct((2 * rows, half), F32),
        ],
        compiler_params=params,
        cost_estimate=pl.CostEstimate(
            flops=9_000_000_000, bytes_accessed=8_000_000, transcendentals=6_000_000
        ),
        name="near_attention",
    )(parts, other_normed, keys_own, values_own, queries_own, own_mixed, own_lse,
      w_query, w_key, w_value)

    row_block = pl.BlockSpec((rows, half), lambda i: (i, 0))
    own_half, lent_half, sums = pl.pallas_call(
        functools.partial(far_kernel, head_width=head_width),
        grid=(2,),
        in_specs=[
            row_block,
            pl.BlockSpec((ranks * far_rows, width), lambda i: (0, 0)),
            row_block,
            row_block,
            pl.BlockSpec((1, width), lambda i: (0, 0)),
        ],
        out_specs=[
            pl.BlockSpec((rows, half), lambda i: (0, 0)),
            pl.BlockSpec((rows, half), lambda i: (0, 0)),
            pl.BlockSpec((ranks,) + PACK, lambda i: (0, 0, 0)),
        ],
        out_shape=[
            jax.ShapeDtypeStruct((rows, half), BF16),
            jax.ShapeDtypeStruct((rows, half), BF16),
            jax.ShapeDtypeStruct((ranks,) + PACK, F32),
        ],
        scratch_shapes=[
            pltpu.VMEM((rows, half), F32),
            pltpu.VMEM((rows, half), F32),
            pltpu.VMEM((1, half), F32),
        ],
        compiler_params=params,
        cost_estimate=pl.CostEstimate(
            flops=6_000_000_000, bytes_accessed=6_000_000, transcendentals=4_000_000
        ),
        name="far_attention",
    )(queries, far, near_mixed, near_lse, embedded_sum)

    sums = lax.all_to_all(sums, SEQ_AXES, 0, 0, tiled=True)
    sums, lent_half = lax.optimization_barrier((sums, lent_half))
    other_half = swap_with(lent_half, "y")
    joined = jnp.where(
        part == 1,
        jnp.concatenate((other_half, own_half), axis=1),
        jnp.concatenate((own_half, other_half), axis=1),
    )
    encoded = embedded.astype(F32) + jnp.dot(joined, w_out, preferred_element_type=F32)
    encoded = encoded.astype(BF16).reshape(1, rows, width)

    slides = lax.axis_size("slide")
    slide_unit_vectors, packed = pl.pallas_call(
        functools.partial(pooled_kernel, length=rows * ranks),
        in_specs=[smem, smem, vmem, vmem, vmem, vmem],
        out_shape=[
            jax.ShapeDtypeStruct((1, width), F32),
            jax.ShapeDtypeStruct((slides,) + PACK, F32),
        ],
        compiler_params=small,
        name="pooled",
    )(slide_code, report_code, sums, w_out, w_head, report_emb)
    everyone = lax.all_to_all(packed, "slide", 0, 0, tiled=True)
    everyone, encoded = lax.optimization_barrier((everyone, encoded))
    logits, loss = pl.pallas_call(
        contrast_kernel,
        in_specs=[vmem],
        out_shape=[
            jax.ShapeDtypeStruct((slides, slides), F32),
            jax.ShapeDtypeStruct((1, 1), F32),
        ],
        compiler_params=small,
        name="contrast",
    )(everyone)
    return (encoded, slide_unit_vectors, logits, loss.reshape(()))


def solution(mesh):
    split = Mesh(mesh.devices.reshape(4, 2, 4, 8), SEQ_AXES + ("slide",))
    rows = P("slide", SEQ_AXES, None)
    return jax.shard_map(
        on_device,
        mesh=split,
        in_specs=(
            rows,
            P(),
            P(),
            P(),
            P(),
            P(),
            P(),
            P(),
            P(),
            P("slide"),
            P("slide", None),
            P("slide"),
        ),
        out_specs=(rows, P("slide", None), P(), P()),
        check_vma=False,
    )
```

```python
import functools
import math

import jax
import jax.numpy as jnp
from jax import lax
from jax.experimental import pallas as pl
from jax.experimental.pallas import tpu as pltpu
from jax.sharding import Mesh, PartitionSpec as P

RATE = 32
LANES = 128
PACK = (8, 256)
SOFTMAX_TEMPER = 1.0 / 0.07
NORM_EPS = 1e-05
NT = (((1,), (1,)), ((), ()))
NN = (((1,), (0,)), ((), ()))
SMALL_VMEM = 16 << 20
LARGE_VMEM = 58 << 20
EMBED_STEPS = 6
SEQ_AXES = ("x", "z_hi", "y")
F32 = jnp.float32
BF16 = jnp.bfloat16


def swap_with(x, axis):
    return lax.ppermute(x, axis, [(i, i ^ 1) for i in range(lax.axis_size(axis))])


def head_window(head, width):
    first = head * width // LANES * LANES
    last = -(-(head * width + width) // LANES) * LANES
    return first, last, head * width - first


def in_head_lanes(head, width):
    first, last, offset = head_window(head, width)
    lane = lax.broadcasted_iota(jnp.int32, (1, last - first), 1)
    return (lane >= offset) & (lane < offset + width)


def attend(queries, keys, values, head_width, mixed_ref, lse_ref, rows):
    for head in range(queries.shape[1] // head_width):
        first, last, _ = head_window(head, head_width)
        mine = in_head_lanes(head, head_width)
        masked = jnp.where(mine, queries[:, first:last], jnp.zeros((), queries.dtype))
        scores = lax.dot_general(masked, keys[:, first:last], NT, preferred_element_type=F32)
        peak = jnp.max(scores, axis=1, keepdims=True)
        weights = jnp.exp(scores - peak)
        total = jnp.sum(weights, axis=1, keepdims=True)
        mixed = lax.dot_general(
            weights.astype(BF16), values[:, first:last], NN, preferred_element_type=F32
        )
        mixed = mixed * (1.0 / total)
        lse = jnp.broadcast_to(peak + jnp.log(total), mixed.shape)
        if head > 0:
            mixed = jnp.where(mine, mixed, mixed_ref[rows, first:last])
            lse = jnp.where(mine, lse, lse_ref[rows, first:last])
        mixed_ref[rows, first:last] = mixed
        lse_ref[rows, first:last] = lse


def merge_states(one, one_lse, two, two_lse):
    share = 1.0 / (1.0 + jnp.exp(two_lse - one_lse))
    return two + (one - two) * share


def started(sources, targets, sems, first=0):
    copies = []
    for place, (source, target) in enumerate(zip(sources, targets)):
        copies.append(pltpu.make_async_copy(source, target, sems.at[first + place]))
        copies[-1].start()
    return copies


def embed_kernel(x_hbm, w_hbm, gain_ref, embedded_hbm, normed_hbm, sum_ref, x_scr, w_scr,
                 embedded_scr, normed_scr, sems, out_sems):
    depth = x_scr.shape[2]
    halves = 2
    part_rows, part_depth = x_scr.shape[1] // halves, depth // halves
    copies = []
    for step in range(EMBED_STEPS):
        group = []
        for i in range(halves):
            rows = slice(i * part_rows, (i + 1) * part_rows)
            group.append(
                pltpu.make_async_copy(
                    x_hbm.at[rows, step * depth : (step + 1) * depth],
                    x_scr.at[step, rows, :],
                    sems.at[step, i],
                )
            )
            first = step * depth + i * part_depth
            group.append(
                pltpu.make_async_copy(
                    w_hbm.at[first : first + part_depth, :],
                    w_scr.at[step, i * part_depth : (i + 1) * part_depth, :],
                    sems.at[step, halves + i],
                )
            )
        for copy in group:
            copy.start()
        copies.append(group)
    total = None
    for step, group in enumerate(copies):
        for copy in group:
            copy.wait()
        product = jnp.dot(x_scr[step], w_scr[step], preferred_element_type=F32)
        total = product if total is None else total + product
    embedded = total.astype(BF16)
    embedded_scr[...] = embedded
    stores = started((embedded_scr,), (embedded_hbm,), out_sems)
    floats = embedded.astype(F32)
    centred = floats - jnp.mean(floats, axis=1, keepdims=True)
    spread = jnp.mean(centred * centred, axis=1, keepdims=True)
    normed = centred * lax.rsqrt(spread + NORM_EPS) * gain_ref[...][None, :]
    normed_scr[...] = normed.astype(BF16)
    stores += started((normed_scr,), (normed_hbm,), out_sems, 1)
    sum_ref[...] = jnp.sum(floats, axis=0, keepdims=True)
    for store in stores:
        store.wait()


def own_rows_kernel(part_ref, offset_ref, x_hbm, wk_hbm, wv_hbm, far_ref, k_out, v_out,
                    x_scr, w_scr, half_scr, sems, out_sems):
    rows, width = x_scr.shape
    half = width // 2
    heads = offset_ref.shape[0]
    spans = (pl.ds(0, half), pl.ds(half, half))
    loads = started(
        [x_hbm] + [wk_hbm.at[span] for span in spans] + [wv_hbm.at[span] for span in spans],
        [x_scr] + [w_scr.at[0, span] for span in spans] + [w_scr.at[1, span] for span in spans],
        sems,
    )
    lane = lax.broadcasted_iota(jnp.int32, (1, width), 1)
    lane_offset = jnp.zeros((1, width), jnp.int32)
    for head in range(heads):
        lane_offset = jnp.where(lane >= head * (width // heads), offset_ref[head], lane_offset)
    phase = lax.broadcasted_iota(jnp.int32, (RATE, width), 0)
    chosen = jnp.where(phase == lane_offset, 1.0, 0.0)
    upper = part_ref[0] == 1
    loads[0].wait()
    stores = []
    for place, half_out in enumerate((k_out, v_out)):
        loads[1 + 2 * place].wait()
        loads[2 + 2 * place].wait()
        full = jnp.dot(x_scr[...], w_scr[place], preferred_element_type=F32)
        half_scr[place] = jnp.where(upper, full[:, half:], full[:, :half]).astype(BF16)
        stores += started((half_scr.at[place],), (half_out,), out_sems, place)
        grouped = full.reshape(rows // RATE, RATE, width) * chosen[None]
        picked = jnp.sum(grouped, axis=1).astype(BF16)
        for part in range(2):
            far_ref[part, :, place * half : (place + 1) * half] = picked[
                :, part * half : (part + 1) * half
            ]
    for store in stores:
        store.wait()


def payload_kernel(own_ref, other_ref, out_ref):
    for place, ref in enumerate((own_ref, other_ref)):
        out_ref[:, :, place, :, :] = jnp.broadcast_to(ref[...][None], out_ref.shape[:2] + ref.shape[1:])


def half_columns(w_hbm, part_ref):
    half = w_hbm.shape[1] // 2
    return w_hbm.at[:, pl.ds(pl.multiple_of(part_ref[0] * half, half), half)]


def own_kernel(part_ref, x_hbm, wq_hbm, k_hbm, v_hbm, q_out, mixed_out, lse_out,
               x_scr, wq_scr, k_scr, v_scr, q_scr, mixed_scr, lse_scr, in_sems, out_sems,
               *, head_width, score_scale):
    loads = started(
        (x_hbm, half_columns(wq_hbm, part_ref), k_hbm, v_hbm), (x_scr, wq_scr, k_scr, v_scr), in_sems
    )
    loads[0].wait()
    loads[1].wait()
    q = jnp.dot(x_scr[...], wq_scr[...], preferred_element_type=F32) * score_scale
    q_scr[...] = q.astype(BF16)
    stores = started((q_scr,), (q_out,), out_sems)
    loads[2].wait()
    loads[3].wait()
    attend(q_scr[...], k_scr[...], v_scr[...], head_width, mixed_scr, lse_scr, slice(None))
    stores += started((mixed_scr, lse_scr), (mixed_out, lse_out), out_sems, 1)
    for store in stores:
        store.wait()


def near_kernel(part_ref, other_hbm, k_hbm, v_hbm, q_hbm, own_mixed_hbm, own_lse_hbm,
                wq_hbm, wk_hbm, wv_hbm, q_out, mixed_out, lse_out,
                x_scr, w_scr, k_scr, v_scr, q_scr, own_mixed_scr, own_lse_scr, mixed_scr, lse_scr,
                in_sems, out_sems, *, head_width, score_scale):
    rows = x_scr.shape[0]
    own, other = pl.ds(0, rows), pl.ds(rows, rows)
    loads = started(
        (
            half_columns(wk_hbm, part_ref), other_hbm, half_columns(wv_hbm, part_ref),
            half_columns(wq_hbm, part_ref), k_hbm, v_hbm, q_hbm, own_mixed_hbm, own_lse_hbm,
        ),
        (
            w_scr.at[0], x_scr, w_scr.at[1],
            w_scr.at[2], k_scr.at[own], v_scr.at[own], q_scr.at[own], own_mixed_scr, own_lse_scr,
        ),
        in_sems,
    )
    loads[0].wait()
    loads[1].wait()
    k_scr[rows:, :] = jnp.dot(x_scr[...], w_scr[0], preferred_element_type=F32).astype(BF16)
    loads[2].wait()
    v_scr[rows:, :] = jnp.dot(x_scr[...], w_scr[1], preferred_element_type=F32).astype(BF16)
    loads[3].wait()
    q = jnp.dot(x_scr[...], w_scr[2], preferred_element_type=F32) * score_scale
    q_scr[rows:, :] = q.astype(BF16)
    stores = started((q_scr.at[other],), (q_out.at[other],), out_sems)
    loads[4].wait()
    loads[5].wait()
    attend(q_scr[rows:, :], k_scr[...], v_scr[...], head_width, mixed_scr.at[1], lse_scr.at[1],
           slice(None))
    stores += started(
        (mixed_scr.at[1], lse_scr.at[1]), (mixed_out.at[other], lse_out.at[other]), out_sems, 1
    )
    loads[6].wait()
    stores += started((q_scr.at[own],), (q_out.at[own],), out_sems, 3)
    attend(q_scr[:rows, :], k_scr[rows:, :], v_scr[rows:, :], head_width, mixed_scr.at[0],
           lse_scr.at[0], slice(None))
    loads[7].wait()
    loads[8].wait()
    own_lse, new_lse = own_lse_scr[...], lse_scr[0]
    mixed_scr[0] = merge_states(own_mixed_scr[...], own_lse, mixed_scr[0], new_lse)
    gap = jnp.exp(-jnp.abs(own_lse - new_lse))
    lse_scr[0] = jnp.maximum(own_lse, new_lse) + jnp.log(1.0 + gap)
    stores += started(
        (mixed_scr.at[0], lse_scr.at[0]), (mixed_out.at[own], lse_out.at[own]), out_sems, 4
    )
    for store in stores:
        store.wait()


def far_kernel(q_hbm, far_hbm, near_hbm, near_lse_hbm, embedded_sum_ref, own_ref, lent_ref,
               pack_ref, q_scr, far_scr, near_scr, near_lse_scr, mixed_scr, lse_scr, sems,
               *, head_width):
    half = q_scr.shape[1]
    rows = own_ref.shape[0]
    loads = started(
        (far_hbm, q_hbm, near_hbm, near_lse_hbm), (far_scr, q_scr, near_scr, near_lse_scr), sems
    )
    loads[0].wait()
    loads[1].wait()
    total = jnp.zeros((1, half), F32)
    for place, out_ref in enumerate((own_ref, lent_ref)):
        span = slice(place * rows, (place + 1) * rows)
        attend(q_scr[span, :], far_scr[:, :half], far_scr[:, half:], head_width,
               mixed_scr.at[place], lse_scr.at[place], slice(None))
        if place == 0:
            loads[2].wait()
            loads[3].wait()
        attended = merge_states(
            near_scr[span, :], near_lse_scr[span, :], mixed_scr[place], lse_scr[place]
        )
        out_ref[...] = attended.astype(BF16)
        total += jnp.sum(attended, axis=0, keepdims=True)
    pad = jnp.zeros((1, pack_ref.shape[1] * pack_ref.shape[2] - 3 * half), F32)
    packed = pack_row((embedded_sum_ref[...], total, pad))
    pack_ref[...] = jnp.broadcast_to(packed[None], pack_ref.shape)


def pack_row(pieces):
    flat = jnp.concatenate(pieces, axis=1)
    rows, lanes = PACK
    return jnp.concatenate([flat[:, r * lanes : (r + 1) * lanes] for r in range(rows)], axis=0)


def exact_row_times(row, matrix):
    top = row.astype(BF16).astype(F32)
    middle = (row - top).astype(BF16).astype(F32)
    low = row - top - middle
    parts = jnp.concatenate((top, middle, low, jnp.zeros((13, row.shape[1]), F32)), axis=0)
    product = jnp.dot(parts.astype(BF16), matrix, preferred_element_type=F32)
    return jnp.sum(product, axis=0, keepdims=True)


def unit_row(row):
    return row * lax.rsqrt(jnp.sum(row * row, axis=1, keepdims=True) + 1e-06)


def pooled_kernel(slide_code_ref, report_code_ref, sums_ref, w_out_ref, w_head_ref, report_ref,
                  unit_ref, pack_ref, *, length):
    peers = sums_ref.shape[0]
    width = w_out_ref.shape[0]
    half = width // 2
    lanes = PACK[1]
    even = sums_ref[0]
    odd = sums_ref[1]
    for peer in range(2, peers, 2):
        even = even + sums_ref[peer]
        odd = odd + sums_ref[peer + 1]

    def flat(packed):
        return jnp.concatenate([packed[r : r + 1, :] for r in range(PACK[0])], axis=1)

    even, odd = flat(even), flat(odd)
    embedded_sum = even[:, :width] + odd[:, :width]
    attended_sum = jnp.concatenate(
        (even[:, width : width + half], odd[:, width : width + half]), axis=1
    )
    pooled = (embedded_sum + exact_row_times(attended_sum, w_out_ref[...])) * (1.0 / length)
    unit = unit_row(exact_row_times(pooled, w_head_ref[...]))
    unit_ref[...] = unit
    lane = lax.broadcasted_iota(jnp.int32, (1, 2 * lanes), 1)
    codes = jnp.where(
        lane == 0,
        slide_code_ref[0].astype(F32),
        jnp.where(lane == 1, report_code_ref[0].astype(F32), 0.0),
    )
    packed = pack_row((unit, unit_row(report_ref[...].astype(F32)), codes))
    pack_ref[...] = jnp.broadcast_to(packed[None], pack_ref.shape)


def contrast_kernel(all_ref, logits_ref, loss_ref):
    count = all_ref.shape[0]
    lanes = PACK[1]
    logits = jnp.zeros((count, count), F32)
    parts = 768 // lanes
    for r in range(parts):
        logits += lax.dot_general(
            all_ref[:, r, :], all_ref[:, parts + r, :], NT,
            precision=lax.Precision.HIGHEST, preferred_element_type=F32,
        )
    logits = logits * SOFTMAX_TEMPER
    logits_ref[...] = logits
    codes = all_ref[:, 2 * parts, :]
    down = lax.broadcasted_iota(jnp.int32, (count, count), 0)
    across = lax.broadcasted_iota(jnp.int32, (count, count), 1)
    diagonal = down == across
    slide_codes = codes[:, 0:1]
    report_codes = jnp.sum(jnp.where(diagonal, codes[:, 1:2], 0.0), axis=0, keepdims=True)
    positive = jnp.where((slide_codes == report_codes) | diagonal, 1.0, 0.0)

    def terms(axis):
        peak = jnp.max(logits, axis=axis, keepdims=True)
        lse = peak + jnp.log(jnp.sum(jnp.exp(logits - peak), axis=axis, keepdims=True))
        picked = jnp.sum(positive * (logits - lse), axis=axis, keepdims=True)
        return -picked / jnp.sum(positive, axis=axis, keepdims=True)

    both = jnp.sum(terms(1), axis=0, keepdims=True) + jnp.sum(terms(0), axis=1, keepdims=True)
    loss_ref[...] = both * (0.5 / count)


def on_device(
    tiles,
    w_embed,
    attn_gain,
    w_query,
    w_key,
    w_value,
    w_out,
    w_head,
    head_offset,
    slide_code,
    report_emb,
    report_code,
):
    _, rows, in_width = tiles.shape
    width = w_embed.shape[1]
    half = width // 2
    heads_count = head_offset.shape[0]
    head_width = width // heads_count
    ranks = lax.axis_size(SEQ_AXES)
    plane = lax.axis_size(("x", "y"))
    score_scale = 1.0 / math.sqrt(head_width)
    part = lax.axis_index("y") % 2
    parts = part.reshape(1)
    params = pltpu.CompilerParams(vmem_limit_bytes=LARGE_VMEM)
    small = pltpu.CompilerParams(vmem_limit_bytes=SMALL_VMEM)
    smem = pl.BlockSpec(memory_space=pltpu.SMEM)
    vmem = pl.BlockSpec(memory_space=pltpu.VMEM)
    anywhere = pl.BlockSpec(memory_space=pl.ANY)

    depth = in_width // EMBED_STEPS
    embedded, normed, embedded_sum = pl.pallas_call(
        embed_kernel,
        in_specs=[anywhere, anywhere, vmem],
        out_specs=[anywhere, anywhere, vmem],
        out_shape=[
            jax.ShapeDtypeStruct((rows, width), BF16),
            jax.ShapeDtypeStruct((rows, width), BF16),
            jax.ShapeDtypeStruct((1, width), F32),
        ],
        scratch_shapes=[
            pltpu.VMEM((EMBED_STEPS, rows, depth), BF16),
            pltpu.VMEM((EMBED_STEPS, depth, width), BF16),
            pltpu.VMEM((rows, width), BF16),
            pltpu.VMEM((rows, width), BF16),
            pltpu.SemaphoreType.DMA((EMBED_STEPS, 4)),
            pltpu.SemaphoreType.DMA((2,)),
        ],
        compiler_params=pltpu.CompilerParams(vmem_limit_bytes=LARGE_VMEM),
        name="embed",
    )(tiles.reshape(rows, in_width), w_embed, attn_gain)
    other_normed = swap_with(normed, "y")

    far_rows = rows // RATE
    far_own, keys_own, values_own = pl.pallas_call(
        own_rows_kernel,
        in_specs=[smem, smem, anywhere, anywhere, anywhere],
        out_specs=[vmem, anywhere, anywhere],
        out_shape=[
            jax.ShapeDtypeStruct((2, far_rows, width), BF16),
            jax.ShapeDtypeStruct((rows, half), BF16),
            jax.ShapeDtypeStruct((rows, half), BF16),
        ],
        scratch_shapes=[
            pltpu.VMEM((rows, width), BF16),
            pltpu.VMEM((2, width, width), BF16),
            pltpu.VMEM((2, rows, half), BF16),
            pltpu.SemaphoreType.DMA((5,)),
            pltpu.SemaphoreType.DMA((2,)),
        ],
        compiler_params=params,
        name="own_rows",
    )(parts, head_offset, normed, w_key, w_value)
    far_other = swap_with(far_own, "z_hi")
    payload = pl.pallas_call(
        payload_kernel,
        in_specs=[vmem, vmem],
        out_shape=jax.ShapeDtypeStruct((plane // 2, 2, 2, far_rows, width), BF16),
        compiler_params=small,
        name="payload",
    )(far_own, far_other).reshape(plane, 2 * far_rows, width)
    far = lax.all_to_all(payload, ("x", "y"), 0, 0, tiled=True).reshape(ranks * far_rows, width)

    half_rows = jax.ShapeDtypeStruct((rows, half), BF16)
    half_state = jax.ShapeDtypeStruct((rows, half), F32)
    queries_own, own_mixed, own_lse = pl.pallas_call(
        functools.partial(own_kernel, head_width=head_width, score_scale=score_scale),
        in_specs=[smem] + [anywhere] * 4,
        out_specs=[anywhere] * 3,
        out_shape=[half_rows, half_state, half_state],
        scratch_shapes=[
            pltpu.VMEM((rows, width), BF16),
            pltpu.VMEM((width, half), BF16),
            pltpu.VMEM((rows, half), BF16),
            pltpu.VMEM((rows, half), BF16),
            pltpu.VMEM((rows, half), BF16),
            pltpu.VMEM((rows, half), F32),
            pltpu.VMEM((rows, half), F32),
            pltpu.SemaphoreType.DMA((4,)),
            pltpu.SemaphoreType.DMA((3,)),
        ],
        compiler_params=params,
        cost_estimate=pl.CostEstimate(
            flops=3_000_000_000, bytes_accessed=4_000_000, transcendentals=2_000_000
        ),
        name="own_attention",
    )(parts, normed, w_query, keys_own, values_own)

    both_rows = jax.ShapeDtypeStruct((2 * rows, half), BF16)
    both_state = jax.ShapeDtypeStruct((2 * rows, half), F32)
    queries, near_mixed, near_lse = pl.pallas_call(
        functools.partial(near_kernel, head_width=head_width, score_scale=score_scale),
        in_specs=[smem] + [anywhere] * 9,
        out_specs=[anywhere] * 3,
        out_shape=[both_rows, both_state, both_state],
        scratch_shapes=[
            pltpu.VMEM((rows, width), BF16),
            pltpu.VMEM((3, width, half), BF16),
            pltpu.VMEM((2 * rows, half), BF16),
            pltpu.VMEM((2 * rows, half), BF16),
            pltpu.VMEM((2 * rows, half), BF16),
            pltpu.VMEM((rows, half), F32),
            pltpu.VMEM((rows, half), F32),
            pltpu.VMEM((2, rows, half), F32),
            pltpu.VMEM((2, rows, half), F32),
            pltpu.SemaphoreType.DMA((9,)),
            pltpu.SemaphoreType.DMA((6,)),
        ],
        compiler_params=params,
        cost_estimate=pl.CostEstimate(
            flops=9_000_000_000, bytes_accessed=8_000_000, transcendentals=6_000_000
        ),
        name="near_attention",
    )(parts, other_normed, keys_own, values_own, queries_own, own_mixed, own_lse,
      w_query, w_key, w_value)

    own_half, lent_half, sums = pl.pallas_call(
        functools.partial(far_kernel, head_width=head_width),
        in_specs=[anywhere] * 4 + [vmem],
        out_specs=[vmem] * 3,
        out_shape=[half_rows, half_rows, jax.ShapeDtypeStruct((ranks,) + PACK, F32)],
        scratch_shapes=[
            pltpu.VMEM((2 * rows, half), BF16),
            pltpu.VMEM((ranks * far_rows, width), BF16),
            pltpu.VMEM((2 * rows, half), F32),
            pltpu.VMEM((2 * rows, half), F32),
            pltpu.VMEM((2, rows, half), F32),
            pltpu.VMEM((2, rows, half), F32),
            pltpu.SemaphoreType.DMA((4,)),
        ],
        compiler_params=params,
        cost_estimate=pl.CostEstimate(
            flops=6_000_000_000, bytes_accessed=6_000_000, transcendentals=4_000_000
        ),
        name="far_attention",
    )(queries, far, near_mixed, near_lse, embedded_sum)

    sums = lax.all_to_all(sums, SEQ_AXES, 0, 0, tiled=True)
    sums, lent_half = lax.optimization_barrier((sums, lent_half))
    other_half = swap_with(lent_half, "y")
    joined = jnp.where(
        part == 1,
        jnp.concatenate((other_half, own_half), axis=1),
        jnp.concatenate((own_half, other_half), axis=1),
    )
    encoded = embedded.astype(F32) + jnp.dot(joined, w_out, preferred_element_type=F32)
    encoded = encoded.astype(BF16).reshape(1, rows, width)

    slides = lax.axis_size("slide")
    slide_unit_vectors, packed = pl.pallas_call(
        functools.partial(pooled_kernel, length=rows * ranks),
        in_specs=[smem, smem, vmem, vmem, vmem, vmem],
        out_shape=[
            jax.ShapeDtypeStruct((1, width), F32),
            jax.ShapeDtypeStruct((slides,) + PACK, F32),
        ],
        compiler_params=small,
        name="pooled",
    )(slide_code, report_code, sums, w_out, w_head, report_emb)
    everyone = lax.all_to_all(packed, "slide", 0, 0, tiled=True)
    everyone, encoded = lax.optimization_barrier((everyone, encoded))
    logits, loss = pl.pallas_call(
        contrast_kernel,
        in_specs=[vmem],
        out_shape=[
            jax.ShapeDtypeStruct((slides, slides), F32),
            jax.ShapeDtypeStruct((1, 1), F32),
        ],
        compiler_params=small,
        name="contrast",
    )(everyone)
    return (encoded, slide_unit_vectors, logits, loss.reshape(()))


def solution(mesh):
    split = Mesh(mesh.devices.reshape(4, 2, 4, 8), SEQ_AXES + ("slide",))
    rows = P("slide", SEQ_AXES, None)
    return jax.shard_map(
        on_device,
        mesh=split,
        in_specs=(
            rows,
            P(),
            P(),
            P(),
            P(),
            P(),
            P(),
            P(),
            P(),
            P("slide"),
            P("slide", None),
            P("slide"),
        ),
        out_specs=(rows, P("slide", None), P(), P()),
        check_vma=False,
    )
```

```python
import functools
import math

import jax
import jax.numpy as jnp
from jax import lax
from jax.experimental import pallas as pl
from jax.experimental.pallas import tpu as pltpu
from jax.sharding import Mesh, PartitionSpec as P

RATE = 32
LANES = 128
PACK = (8, 256)
SOFTMAX_TEMPER = 1.0 / 0.07
NORM_EPS = 1e-05
NT = (((1,), (1,)), ((), ()))
NN = (((1,), (0,)), ((), ()))
SMALL_VMEM = 16 << 20
LARGE_VMEM = 58 << 20
EMBED_STEPS = 2
EMBED_VMEM = 59 << 20
SEQ_AXES = ("x", "z_hi", "y")
F32 = jnp.float32
BF16 = jnp.bfloat16


def swap_with(x, axis):
    return lax.ppermute(x, axis, [(i, i ^ 1) for i in range(lax.axis_size(axis))])


def head_window(head, width):
    first = head * width // LANES * LANES
    last = -(-(head * width + width) // LANES) * LANES
    return first, last, head * width - first


def in_head_lanes(head, width):
    first, last, offset = head_window(head, width)
    lane = lax.broadcasted_iota(jnp.int32, (1, last - first), 1)
    return (lane >= offset) & (lane < offset + width)


def attend(queries, keys, values, head_width, mixed_ref, lse_ref, rows):
    for head in range(queries.shape[1] // head_width):
        first, last, _ = head_window(head, head_width)
        mine = in_head_lanes(head, head_width)
        masked = jnp.where(mine, queries[:, first:last], jnp.zeros((), queries.dtype))
        scores = lax.dot_general(masked, keys[:, first:last], NT, preferred_element_type=F32)
        peak = jnp.max(scores, axis=1, keepdims=True)
        weights = jnp.exp(scores - peak)
        total = jnp.sum(weights, axis=1, keepdims=True)
        mixed = lax.dot_general(
            weights.astype(BF16), values[:, first:last], NN, preferred_element_type=F32
        )
        mixed = mixed * (1.0 / total)
        lse = jnp.broadcast_to(peak + jnp.log(total), mixed.shape)
        if head > 0:
            mixed = jnp.where(mine, mixed, mixed_ref[rows, first:last])
            lse = jnp.where(mine, lse, lse_ref[rows, first:last])
        mixed_ref[rows, first:last] = mixed
        lse_ref[rows, first:last] = lse


def merge_states(one, one_lse, two, two_lse):
    share = 1.0 / (1.0 + jnp.exp(two_lse - one_lse))
    return two + (one - two) * share


def started(sources, targets, sems, first=0):
    copies = []
    for place, (source, target) in enumerate(zip(sources, targets)):
        copies.append(pltpu.make_async_copy(source, target, sems.at[first + place]))
        copies[-1].start()
    return copies


def embed_kernel(x_hbm, w_hbm, gain_ref, embedded_hbm, normed_ref, sum_ref, x_scr, w_scr,
                 embedded_scr, x_sems, w_sems, out_sems):
    rows = x_scr.shape[0] // EMBED_STEPS
    spans = [pl.ds(step * rows, rows) for step in range(EMBED_STEPS)]
    pieces = w_sems.shape[0]
    depth = w_scr.shape[0] // pieces
    parts = [pl.ds(i * depth, depth) for i in range(pieces)]
    x_loads = started([x_hbm.at[spans[0]]], [x_scr.at[spans[0]]], x_sems)
    w_loads = started([w_hbm.at[p] for p in parts], [w_scr.at[p] for p in parts], w_sems)
    x_loads += started(
        [x_hbm.at[span] for span in spans[1:]], [x_scr.at[span] for span in spans[1:]], x_sems, 1
    )
    stores = []
    summed = jnp.zeros(sum_ref.shape, F32)
    for step, span in enumerate(spans):
        x_loads[step].wait()
        if step == 0:
            total = None
            for piece, load in enumerate(w_loads):
                load.wait()
                columns = slice(piece * depth, (piece + 1) * depth)
                product = jnp.dot(
                    x_scr[span, columns], w_scr[parts[piece], :], preferred_element_type=F32
                )
                total = product if total is None else total + product
        else:
            total = jnp.dot(x_scr[span, :], w_scr[...], preferred_element_type=F32)
        embedded = total.astype(BF16)
        embedded_scr[span, :] = embedded
        stores += started([embedded_scr.at[span]], [embedded_hbm.at[span]], out_sems, step)
        floats = embedded.astype(F32)
        centred = floats - jnp.mean(floats, axis=1, keepdims=True)
        spread = jnp.mean(centred * centred, axis=1, keepdims=True)
        normed = centred * lax.rsqrt(spread + NORM_EPS) * gain_ref[...][None, :]
        normed_ref[span, :] = normed.astype(BF16)
        summed += jnp.sum(floats, axis=0, keepdims=True)
    sum_ref[...] = summed
    for store in stores:
        store.wait()


def own_rows_kernel(part_ref, offset_ref, x_ref, wk_ref, wv_ref, far_ref, k_ref, v_ref):
    rows, width = x_ref.shape
    half = width // 2
    heads = offset_ref.shape[0]
    lane = lax.broadcasted_iota(jnp.int32, (1, width), 1)
    lane_offset = jnp.zeros((1, width), jnp.int32)
    for head in range(heads):
        lane_offset = jnp.where(lane >= head * (width // heads), offset_ref[head], lane_offset)
    phase = lax.broadcasted_iota(jnp.int32, (RATE, width), 0)
    chosen = jnp.where(phase == lane_offset, 1.0, 0.0)
    upper = part_ref[0] == 1
    for place, (w_ref, half_ref) in enumerate(((wk_ref, k_ref), (wv_ref, v_ref))):
        full = jnp.dot(x_ref[...], w_ref[...], preferred_element_type=F32)
        half_ref[...] = jnp.where(upper, full[:, half:], full[:, :half]).astype(BF16)
        grouped = full.reshape(rows // RATE, RATE, width) * chosen[None]
        picked = jnp.sum(grouped, axis=1).astype(BF16)
        for part in range(2):
            far_ref[part, :, place * half : (place + 1) * half] = picked[
                :, part * half : (part + 1) * half
            ]


def payload_kernel(own_ref, other_ref, out_ref):
    for place, ref in enumerate((own_ref, other_ref)):
        out_ref[:, :, place, :, :] = jnp.broadcast_to(ref[...][None], out_ref.shape[:2] + ref.shape[1:])


def half_columns(w_hbm, part_ref):
    half = w_hbm.shape[1] // 2
    return w_hbm.at[:, pl.ds(pl.multiple_of(part_ref[0] * half, half), half)]


def own_kernel(part_ref, x_ref, wq_ref, k_ref, v_ref, q_out, mixed_out, lse_out,
               q_scr, mixed_scr, lse_scr, out_sems, *, head_width, score_scale):
    half = wq_ref.shape[1] // 2
    upper = part_ref[0] == 1
    wq = jnp.where(upper, wq_ref[:, half:], wq_ref[:, :half])
    q = jnp.dot(x_ref[...], wq, preferred_element_type=F32) * score_scale
    q_scr[...] = q.astype(BF16)
    stores = started((q_scr,), (q_out,), out_sems)
    attend(q_scr[...], k_ref[...], v_ref[...], head_width, mixed_scr, lse_scr, slice(None))
    stores += started((mixed_scr, lse_scr), (mixed_out, lse_out), out_sems, 1)
    for store in stores:
        store.wait()


def near_kernel(part_ref, other_hbm, k_hbm, v_hbm, q_hbm, own_mixed_hbm, own_lse_hbm,
                wq_hbm, wk_hbm, wv_hbm, q_out, mixed_out, lse_out,
                x_scr, w_scr, k_scr, v_scr, q_scr, own_mixed_scr, own_lse_scr, mixed_scr, lse_scr,
                in_sems, out_sems, *, head_width, score_scale):
    rows = x_scr.shape[0]
    own, other = pl.ds(0, rows), pl.ds(rows, rows)
    loads = started(
        (
            half_columns(wk_hbm, part_ref), other_hbm, half_columns(wv_hbm, part_ref),
            half_columns(wq_hbm, part_ref), k_hbm, v_hbm, q_hbm, own_mixed_hbm, own_lse_hbm,
        ),
        (
            w_scr.at[0], x_scr, w_scr.at[1],
            w_scr.at[2], k_scr.at[own], v_scr.at[own], q_scr.at[own], own_mixed_scr, own_lse_scr,
        ),
        in_sems,
    )
    loads[0].wait()
    loads[1].wait()
    k_scr[rows:, :] = jnp.dot(x_scr[...], w_scr[0], preferred_element_type=F32).astype(BF16)
    loads[2].wait()
    v_scr[rows:, :] = jnp.dot(x_scr[...], w_scr[1], preferred_element_type=F32).astype(BF16)
    loads[3].wait()
    q = jnp.dot(x_scr[...], w_scr[2], preferred_element_type=F32) * score_scale
    q_scr[rows:, :] = q.astype(BF16)
    stores = started((q_scr.at[other],), (q_out.at[other],), out_sems)
    loads[4].wait()
    loads[5].wait()
    attend(q_scr[rows:, :], k_scr[...], v_scr[...], head_width, mixed_scr.at[1], lse_scr.at[1],
           slice(None))
    stores += started(
        (mixed_scr.at[1], lse_scr.at[1]), (mixed_out.at[other], lse_out.at[other]), out_sems, 1
    )
    loads[6].wait()
    stores += started((q_scr.at[own],), (q_out.at[own],), out_sems, 3)
    attend(q_scr[:rows, :], k_scr[rows:, :], v_scr[rows:, :], head_width, mixed_scr.at[0],
           lse_scr.at[0], slice(None))
    loads[7].wait()
    loads[8].wait()
    own_lse, new_lse = own_lse_scr[...], lse_scr[0]
    mixed_scr[0] = merge_states(own_mixed_scr[...], own_lse, mixed_scr[0], new_lse)
    gap = jnp.exp(-jnp.abs(own_lse - new_lse))
    lse_scr[0] = jnp.maximum(own_lse, new_lse) + jnp.log(1.0 + gap)
    stores += started(
        (mixed_scr.at[0], lse_scr.at[0]), (mixed_out.at[own], lse_out.at[own]), out_sems, 4
    )
    for store in stores:
        store.wait()


def far_kernel(q_hbm, far_hbm, near_hbm, near_lse_hbm, embedded_sum_ref, own_ref, lent_ref,
               pack_ref, q_scr, far_scr, near_scr, near_lse_scr, mixed_scr, lse_scr, sems,
               *, head_width):
    half = q_scr.shape[1]
    rows = own_ref.shape[0]
    loads = started(
        (far_hbm, q_hbm, near_hbm, near_lse_hbm), (far_scr, q_scr, near_scr, near_lse_scr), sems
    )
    loads[0].wait()
    loads[1].wait()
    total = jnp.zeros((1, half), F32)
    for place, out_ref in enumerate((own_ref, lent_ref)):
        span = slice(place * rows, (place + 1) * rows)
        attend(q_scr[span, :], far_scr[:, :half], far_scr[:, half:], head_width,
               mixed_scr.at[place], lse_scr.at[place], slice(None))
        if place == 0:
            loads[2].wait()
            loads[3].wait()
        attended = merge_states(
            near_scr[span, :], near_lse_scr[span, :], mixed_scr[place], lse_scr[place]
        )
        out_ref[...] = attended.astype(BF16)
        total += jnp.sum(attended, axis=0, keepdims=True)
    pad = jnp.zeros((1, pack_ref.shape[1] * pack_ref.shape[2] - 3 * half), F32)
    packed = pack_row((embedded_sum_ref[...], total, pad))
    pack_ref[...] = jnp.broadcast_to(packed[None], pack_ref.shape)


def pack_row(pieces):
    flat = jnp.concatenate(pieces, axis=1)
    rows, lanes = PACK
    return jnp.concatenate([flat[:, r * lanes : (r + 1) * lanes] for r in range(rows)], axis=0)


def exact_row_times(row, matrix):
    top = row.astype(BF16).astype(F32)
    middle = (row - top).astype(BF16).astype(F32)
    low = row - top - middle
    parts = jnp.concatenate((top, middle, low, jnp.zeros((13, row.shape[1]), F32)), axis=0)
    product = jnp.dot(parts.astype(BF16), matrix, preferred_element_type=F32)
    return jnp.sum(product, axis=0, keepdims=True)


def unit_row(row):
    return row * lax.rsqrt(jnp.sum(row * row, axis=1, keepdims=True) + 1e-06)


def pooled_kernel(codes_ref, sums_ref, w_out_ref, w_head_ref, report_ref,
                  unit_ref, pack_ref, *, length):
    peers = sums_ref.shape[0]
    width = w_out_ref.shape[0]
    half = width // 2
    even = sums_ref[0]
    odd = sums_ref[1]
    for peer in range(2, peers, 2):
        even = even + sums_ref[peer]
        odd = odd + sums_ref[peer + 1]

    def flat(packed):
        return jnp.concatenate([packed[r : r + 1, :] for r in range(PACK[0])], axis=1)

    even, odd = flat(even), flat(odd)
    embedded_sum = even[:, :width] + odd[:, :width]
    attended_sum = jnp.concatenate(
        (even[:, width : width + half], odd[:, width : width + half]), axis=1
    )
    pooled = (embedded_sum + exact_row_times(attended_sum, w_out_ref[...])) * (1.0 / length)
    unit = unit_row(exact_row_times(pooled, w_head_ref[...]))
    unit_ref[...] = unit
    packed = pack_row((unit, unit_row(report_ref[...].astype(F32)), codes_ref[...]))
    pack_ref[...] = jnp.broadcast_to(packed[None], pack_ref.shape)


def contrast_kernel(all_ref, logits_ref, loss_ref):
    count = all_ref.shape[0]
    lanes = PACK[1]
    logits = jnp.zeros((count, count), F32)
    parts = 768 // lanes
    for r in range(parts):
        logits += lax.dot_general(
            all_ref[:, r, :], all_ref[:, parts + r, :], NT,
            precision=lax.Precision.HIGHEST, preferred_element_type=F32,
        )
    logits = logits * SOFTMAX_TEMPER
    logits_ref[...] = logits
    codes = all_ref[:, 2 * parts, :]
    down = lax.broadcasted_iota(jnp.int32, (count, count), 0)
    across = lax.broadcasted_iota(jnp.int32, (count, count), 1)
    diagonal = down == across
    slide_codes = codes[:, 0:1]
    report_codes = jnp.sum(jnp.where(diagonal, codes[:, 1:2], 0.0), axis=0, keepdims=True)
    positive = jnp.where((slide_codes == report_codes) | diagonal, 1.0, 0.0)

    def terms(axis):
        peak = jnp.max(logits, axis=axis, keepdims=True)
        lse = peak + jnp.log(jnp.sum(jnp.exp(logits - peak), axis=axis, keepdims=True))
        picked = jnp.sum(positive * (logits - lse), axis=axis, keepdims=True)
        return -picked / jnp.sum(positive, axis=axis, keepdims=True)

    both = jnp.sum(terms(1), axis=0, keepdims=True) + jnp.sum(terms(0), axis=1, keepdims=True)
    loss_ref[...] = both * (0.5 / count)


def on_device(
    tiles,
    w_embed,
    attn_gain,
    w_query,
    w_key,
    w_value,
    w_out,
    w_head,
    head_offset,
    slide_code,
    report_emb,
    report_code,
):
    _, rows, in_width = tiles.shape
    width = w_embed.shape[1]
    half = width // 2
    heads_count = head_offset.shape[0]
    head_width = width // heads_count
    ranks = lax.axis_size(SEQ_AXES)
    plane = lax.axis_size(("x", "y"))
    score_scale = 1.0 / math.sqrt(head_width)
    part = lax.axis_index("y") % 2
    parts = part.reshape(1)
    params = pltpu.CompilerParams(vmem_limit_bytes=LARGE_VMEM)
    small = pltpu.CompilerParams(vmem_limit_bytes=SMALL_VMEM)
    smem = pl.BlockSpec(memory_space=pltpu.SMEM)
    vmem = pl.BlockSpec(memory_space=pltpu.VMEM)
    anywhere = pl.BlockSpec(memory_space=pl.ANY)

    pieces = 3
    embedded, normed, embedded_sum = pl.pallas_call(
        embed_kernel,
        in_specs=[anywhere, anywhere, vmem],
        out_specs=[anywhere, vmem, vmem],
        out_shape=[
            jax.ShapeDtypeStruct((rows, width), BF16),
            pltpu.VMEM((rows, width), BF16),
            jax.ShapeDtypeStruct((1, width), F32),
        ],
        scratch_shapes=[
            pltpu.VMEM((rows, in_width), BF16),
            pltpu.VMEM((in_width, width), BF16),
            pltpu.VMEM((rows, width), BF16),
            pltpu.SemaphoreType.DMA((EMBED_STEPS,)),
            pltpu.SemaphoreType.DMA((pieces,)),
            pltpu.SemaphoreType.DMA((EMBED_STEPS,)),
        ],
        compiler_params=pltpu.CompilerParams(vmem_limit_bytes=EMBED_VMEM),
        name="embed",
    )(tiles.reshape(rows, in_width), w_embed, attn_gain)
    other_normed = swap_with(normed, "y")

    far_rows = rows // RATE
    far_own, keys_own, values_own = pl.pallas_call(
        own_rows_kernel,
        in_specs=[smem, smem, vmem, vmem, vmem],
        out_specs=[vmem, vmem, vmem],
        out_shape=[
            jax.ShapeDtypeStruct((2, far_rows, width), BF16),
            jax.ShapeDtypeStruct((rows, half), BF16),
            jax.ShapeDtypeStruct((rows, half), BF16),
        ],
        compiler_params=small,
        name="own_rows",
    )(parts, head_offset, normed, w_key, w_value)
    far_other = swap_with(far_own, "z_hi")
    payload = pl.pallas_call(
        payload_kernel,
        in_specs=[vmem, vmem],
        out_shape=jax.ShapeDtypeStruct((plane // 2, 2, 2, far_rows, width), BF16),
        compiler_params=small,
        name="payload",
    )(far_own, far_other).reshape(plane, 2 * far_rows, width)
    far = lax.all_to_all(payload, ("x", "y"), 0, 0, tiled=True).reshape(ranks * far_rows, width)

    half_rows = jax.ShapeDtypeStruct((rows, half), BF16)
    queries_own, own_mixed, own_lse = pl.pallas_call(
        functools.partial(own_kernel, head_width=head_width, score_scale=score_scale),
        in_specs=[smem] + [vmem] * 4,
        out_specs=[anywhere] * 3,
        out_shape=[
            pltpu.HBM((rows, half), BF16),
            pltpu.HBM((rows, half), F32),
            pltpu.HBM((rows, half), F32),
        ],
        scratch_shapes=[
            pltpu.VMEM((rows, half), BF16),
            pltpu.VMEM((rows, half), F32),
            pltpu.VMEM((rows, half), F32),
            pltpu.SemaphoreType.DMA((3,)),
        ],
        compiler_params=pltpu.CompilerParams(vmem_limit_bytes=32 << 20),
        cost_estimate=pl.CostEstimate(
            flops=3_000_000_000, bytes_accessed=4_000_000, transcendentals=2_000_000
        ),
        name="own_attention",
    )(parts, normed, w_query, keys_own, values_own)

    both_rows = jax.ShapeDtypeStruct((2 * rows, half), BF16)
    both_state = jax.ShapeDtypeStruct((2 * rows, half), F32)
    queries, near_mixed, near_lse = pl.pallas_call(
        functools.partial(near_kernel, head_width=head_width, score_scale=score_scale),
        in_specs=[smem] + [anywhere] * 9,
        out_specs=[anywhere] * 3,
        out_shape=[both_rows, both_state, both_state],
        scratch_shapes=[
            pltpu.VMEM((rows, width), BF16),
            pltpu.VMEM((3, width, half), BF16),
            pltpu.VMEM((2 * rows, half), BF16),
            pltpu.VMEM((2 * rows, half), BF16),
            pltpu.VMEM((2 * rows, half), BF16),
            pltpu.VMEM((rows, half), F32),
            pltpu.VMEM((rows, half), F32),
            pltpu.VMEM((2, rows, half), F32),
            pltpu.VMEM((2, rows, half), F32),
            pltpu.SemaphoreType.DMA((9,)),
            pltpu.SemaphoreType.DMA((6,)),
        ],
        compiler_params=params,
        cost_estimate=pl.CostEstimate(
            flops=9_000_000_000, bytes_accessed=8_000_000, transcendentals=6_000_000
        ),
        name="near_attention",
    )(parts, other_normed, keys_own, values_own, queries_own, own_mixed, own_lse,
      w_query, w_key, w_value)

    own_half, lent_half, sums = pl.pallas_call(
        functools.partial(far_kernel, head_width=head_width),
        in_specs=[anywhere] * 4 + [vmem],
        out_specs=[vmem] * 3,
        out_shape=[half_rows, half_rows, jax.ShapeDtypeStruct((ranks,) + PACK, F32)],
        scratch_shapes=[
            pltpu.VMEM((2 * rows, half), BF16),
            pltpu.VMEM((ranks * far_rows, width), BF16),
            pltpu.VMEM((2 * rows, half), F32),
            pltpu.VMEM((2 * rows, half), F32),
            pltpu.VMEM((2, rows, half), F32),
            pltpu.VMEM((2, rows, half), F32),
            pltpu.SemaphoreType.DMA((4,)),
        ],
        compiler_params=params,
        cost_estimate=pl.CostEstimate(
            flops=6_000_000_000, bytes_accessed=6_000_000, transcendentals=4_000_000
        ),
        name="far_attention",
    )(queries, far, near_mixed, near_lse, embedded_sum)

    sums = lax.all_to_all(sums, SEQ_AXES, 0, 0, tiled=True)
    sums, lent_half = lax.optimization_barrier((sums, lent_half))
    other_half = swap_with(lent_half, "y")
    joined = jnp.where(
        part == 1,
        jnp.concatenate((other_half, own_half), axis=1),
        jnp.concatenate((own_half, other_half), axis=1),
    )
    encoded = embedded.astype(F32) + jnp.dot(joined, w_out, preferred_element_type=F32)
    encoded = encoded.astype(BF16).reshape(1, rows, width)

    lane = jnp.arange(2 * PACK[1], dtype=jnp.int32)[None, :]
    codes = jnp.where(lane == 0, slide_code[:, None], jnp.where(lane == 1, report_code[:, None], 0))
    codes = codes.astype(F32)
    slides = lax.axis_size("slide")
    slide_unit_vectors, packed = pl.pallas_call(
        functools.partial(pooled_kernel, length=rows * ranks),
        in_specs=[vmem] * 5,
        out_shape=[
            jax.ShapeDtypeStruct((1, width), F32),
            jax.ShapeDtypeStruct((slides,) + PACK, F32),
        ],
        compiler_params=small,
        name="pooled",
    )(codes, sums, w_out, w_head, report_emb)
    everyone = lax.all_to_all(packed, "slide", 0, 0, tiled=True)
    everyone, encoded = lax.optimization_barrier((everyone, encoded))
    logits, loss = pl.pallas_call(
        contrast_kernel,
        in_specs=[vmem],
        out_shape=[
            jax.ShapeDtypeStruct((slides, slides), F32),
            jax.ShapeDtypeStruct((1, 1), F32),
        ],
        compiler_params=small,
        name="contrast",
    )(everyone)
    return (encoded, slide_unit_vectors, logits, loss.reshape(()))


def solution(mesh):
    split = Mesh(mesh.devices.reshape(4, 2, 4, 8), SEQ_AXES + ("slide",))
    rows = P("slide", SEQ_AXES, None)
    return jax.shard_map(
        on_device,
        mesh=split,
        in_specs=(
            rows,
            P(),
            P(),
            P(),
            P(),
            P(),
            P(),
            P(),
            P(),
            P("slide"),
            P("slide", None),
            P("slide"),
        ),
        out_specs=(rows, P("slide", None), P(), P()),
        check_vma=False,
    )
```

```python
import functools
import math

import jax
import jax.numpy as jnp
from jax import lax
from jax.experimental import pallas as pl
from jax.experimental.pallas import tpu as pltpu
from jax.sharding import Mesh, PartitionSpec as P

RATE = 32
LANES = 128
PACK = (8, 256)
SOFTMAX_TEMPER = 1.0 / 0.07
NORM_EPS = 1e-05
NT = (((1,), (1,)), ((), ()))
NN = (((1,), (0,)), ((), ()))
SMALL_VMEM = 16 << 20
LARGE_VMEM = 58 << 20
EMBED_STEPS = 2
EMBED_VMEM = 59 << 20
SEQ_AXES = ("x", "z_hi", "y")
F32 = jnp.float32
BF16 = jnp.bfloat16


def swap_with(x, axis):
    return lax.ppermute(x, axis, [(i, i ^ 1) for i in range(lax.axis_size(axis))])


def head_window(head, width):
    first = head * width // LANES * LANES
    last = -(-(head * width + width) // LANES) * LANES
    return first, last, head * width - first


def in_head_lanes(head, width):
    first, last, offset = head_window(head, width)
    lane = lax.broadcasted_iota(jnp.int32, (1, last - first), 1)
    return (lane >= offset) & (lane < offset + width)


def attend(queries, keys, values, head_width, mixed_ref, lse_ref, finish):
    width = queries.shape[1]
    finished = 0
    for head in range(width // head_width):
        first, last, _ = head_window(head, head_width)
        mine = in_head_lanes(head, head_width)
        masked = jnp.where(mine, queries[:, first:last], jnp.zeros((), queries.dtype))
        scores = lax.dot_general(masked, keys[:, first:last], NT, preferred_element_type=F32)
        peak = jnp.max(scores, axis=1, keepdims=True)
        weights = jnp.exp(scores - peak)
        total = jnp.sum(weights, axis=1, keepdims=True)
        mixed = lax.dot_general(
            weights.astype(BF16), values[:, first:last], NN, preferred_element_type=F32
        )
        mixed = mixed * (1.0 / total)
        lse = jnp.broadcast_to(peak + jnp.log(total), mixed.shape)
        if head > 0:
            mixed = jnp.where(mine, mixed, mixed_ref[:, first:last])
            lse = jnp.where(mine, lse, lse_ref[:, first:last])
        mixed_ref[:, first:last] = mixed
        lse_ref[:, first:last] = lse
        while (finished + 1) * LANES <= (head + 1) * head_width:
            finish(finished, slice(finished * LANES, (finished + 1) * LANES))
            finished += 1


def merge_states(one, one_lse, two, two_lse):
    share = 1.0 / (1.0 + jnp.exp(two_lse - one_lse))
    return two + (one - two) * share


def started(sources, targets, sems, first=0):
    copies = []
    for place, (source, target) in enumerate(zip(sources, targets)):
        copies.append(pltpu.make_async_copy(source, target, sems.at[first + place]))
        copies[-1].start()
    return copies


def embed_kernel(x_hbm, w_hbm, gain_ref, embedded_hbm, normed_ref, sum_ref, x_scr, w_scr,
                 embedded_scr, x_sems, w_sems, out_sems):
    rows = x_scr.shape[0] // EMBED_STEPS
    spans = [pl.ds(step * rows, rows) for step in range(EMBED_STEPS)]
    pieces = w_sems.shape[0]
    depth = w_scr.shape[0] // pieces
    parts = [pl.ds(i * depth, depth) for i in range(pieces)]
    x_loads = started([x_hbm.at[spans[0]]], [x_scr.at[spans[0]]], x_sems)
    w_loads = started([w_hbm.at[p] for p in parts], [w_scr.at[p] for p in parts], w_sems)
    x_loads += started(
        [x_hbm.at[span] for span in spans[1:]], [x_scr.at[span] for span in spans[1:]], x_sems, 1
    )
    stores = []
    summed = jnp.zeros(sum_ref.shape, F32)
    for step, span in enumerate(spans):
        x_loads[step].wait()
        if step == 0:
            total = None
            for piece, load in enumerate(w_loads):
                load.wait()
                columns = slice(piece * depth, (piece + 1) * depth)
                product = jnp.dot(
                    x_scr[span, columns], w_scr[parts[piece], :], preferred_element_type=F32
                )
                total = product if total is None else total + product
        else:
            total = jnp.dot(x_scr[span, :], w_scr[...], preferred_element_type=F32)
        embedded = total.astype(BF16)
        embedded_scr[span, :] = embedded
        stores += started([embedded_scr.at[span]], [embedded_hbm.at[span]], out_sems, step)
        floats = embedded.astype(F32)
        centred = floats - jnp.mean(floats, axis=1, keepdims=True)
        spread = jnp.mean(centred * centred, axis=1, keepdims=True)
        normed = centred * lax.rsqrt(spread + NORM_EPS) * gain_ref[...][None, :]
        normed_ref[span, :] = normed.astype(BF16)
        summed += jnp.sum(floats, axis=0, keepdims=True)
    sum_ref[...] = summed
    for store in stores:
        store.wait()


def own_rows_kernel(part_ref, offset_ref, x_ref, wk_ref, wv_ref, far_ref, k_ref, v_ref):
    rows, width = x_ref.shape
    half = width // 2
    heads = offset_ref.shape[0]
    lane = lax.broadcasted_iota(jnp.int32, (1, width), 1)
    lane_offset = jnp.zeros((1, width), jnp.int32)
    for head in range(heads):
        lane_offset = jnp.where(lane >= head * (width // heads), offset_ref[head], lane_offset)
    phase = lax.broadcasted_iota(jnp.int32, (RATE, width), 0)
    chosen = jnp.where(phase == lane_offset, 1.0, 0.0)
    upper = part_ref[0] == 1
    for place, (w_ref, half_ref) in enumerate(((wk_ref, k_ref), (wv_ref, v_ref))):
        full = jnp.dot(x_ref[...], w_ref[...], preferred_element_type=F32)
        half_ref[...] = jnp.where(upper, full[:, half:], full[:, :half]).astype(BF16)
        grouped = full.reshape(rows // RATE, RATE, width) * chosen[None]
        picked = jnp.sum(grouped, axis=1).astype(BF16)
        for part in range(2):
            far_ref[part, :, place * half : (place + 1) * half] = picked[
                :, part * half : (part + 1) * half
            ]


def payload_kernel(own_ref, other_ref, out_ref):
    for place, ref in enumerate((own_ref, other_ref)):
        out_ref[:, :, place, :, :] = jnp.broadcast_to(ref[...][None], out_ref.shape[:2] + ref.shape[1:])


def half_columns(w_hbm, part_ref):
    half = w_hbm.shape[1] // 2
    return w_hbm.at[:, pl.ds(pl.multiple_of(part_ref[0] * half, half), half)]


def own_kernel(part_ref, x_ref, wq_ref, k_ref, v_ref, q_out, mixed_out, lse_out,
               q_scr, mixed_scr, lse_scr, out_sems, *, head_width, score_scale):
    half = wq_ref.shape[1] // 2
    upper = part_ref[0] == 1
    wq = jnp.where(upper, wq_ref[:, half:], wq_ref[:, :half])
    q = jnp.dot(x_ref[...], wq, preferred_element_type=F32) * score_scale
    q_scr[...] = q.astype(BF16)
    stores = started((q_scr,), (q_out,), out_sems)

    def finish(tile, lanes):
        stores.extend(
            started(
                (mixed_scr.at[:, lanes], lse_scr.at[:, lanes]),
                (mixed_out.at[:, lanes], lse_out.at[:, lanes]),
                out_sems,
                1 + 2 * tile,
            )
        )

    attend(q_scr[...], k_ref[...], v_ref[...], head_width, mixed_scr, lse_scr, finish)
    for store in stores:
        store.wait()


def near_kernel(part_ref, other_hbm, k_hbm, v_hbm, q_hbm, own_mixed_hbm, own_lse_hbm,
                wq_hbm, wk_hbm, wv_hbm, q_out, mixed_out, lse_out,
                x_scr, w_scr, k_scr, v_scr, q_scr, own_mixed_scr, own_lse_scr, mixed_scr, lse_scr,
                in_sems, out_sems, *, head_width, score_scale):
    rows = x_scr.shape[0]
    own, other = pl.ds(0, rows), pl.ds(rows, rows)
    loads = started(
        (
            half_columns(wk_hbm, part_ref), other_hbm, half_columns(wv_hbm, part_ref),
            half_columns(wq_hbm, part_ref), k_hbm, v_hbm, q_hbm, own_mixed_hbm, own_lse_hbm,
        ),
        (
            w_scr.at[0], x_scr, w_scr.at[1],
            w_scr.at[2], k_scr.at[own], v_scr.at[own], q_scr.at[own], own_mixed_scr, own_lse_scr,
        ),
        in_sems,
    )
    loads[0].wait()
    loads[1].wait()
    k_scr[rows:, :] = jnp.dot(x_scr[...], w_scr[0], preferred_element_type=F32).astype(BF16)
    loads[2].wait()
    v_scr[rows:, :] = jnp.dot(x_scr[...], w_scr[1], preferred_element_type=F32).astype(BF16)
    loads[3].wait()
    q = jnp.dot(x_scr[...], w_scr[2], preferred_element_type=F32) * score_scale
    q_scr[rows:, :] = q.astype(BF16)
    stores = started((q_scr.at[other],), (q_out.at[other],), out_sems)
    loads[4].wait()
    loads[5].wait()

    def store_tile(place, span, first, lanes):
        stores.extend(
            started(
                (mixed_scr.at[place, :, lanes], lse_scr.at[place, :, lanes]),
                (mixed_out.at[span, lanes], lse_out.at[span, lanes]),
                out_sems,
                first,
            )
        )

    tiles = mixed_scr.shape[2] // LANES
    attend(q_scr[rows:, :], k_scr[...], v_scr[...], head_width, mixed_scr.at[1], lse_scr.at[1],
           lambda tile, lanes: store_tile(1, other, 2 + 2 * tile, lanes))
    loads[6].wait()
    stores += started((q_scr.at[own],), (q_out.at[own],), out_sems, 1)

    def finish_own(tile, lanes):
        if tile == 0:
            loads[7].wait()
            loads[8].wait()
        own_lse, new_lse = own_lse_scr[:, lanes], lse_scr[0, :, lanes]
        mixed_scr[0, :, lanes] = merge_states(
            own_mixed_scr[:, lanes], own_lse, mixed_scr[0, :, lanes], new_lse
        )
        gap = jnp.exp(-jnp.abs(own_lse - new_lse))
        lse_scr[0, :, lanes] = jnp.maximum(own_lse, new_lse) + jnp.log(1.0 + gap)
        store_tile(0, own, 2 + 2 * tiles + 2 * tile, lanes)

    attend(q_scr[:rows, :], k_scr[rows:, :], v_scr[rows:, :], head_width, mixed_scr.at[0],
           lse_scr.at[0], finish_own)
    for store in stores:
        store.wait()


def far_kernel(q_hbm, far_hbm, near_hbm, near_lse_hbm, embedded_sum_ref, own_out, lent_out,
               pack_ref, q_scr, far_scr, near_scr, near_lse_scr, mixed_scr, lse_scr, out_scr,
               in_sems, out_sems, *, head_width):
    half = q_scr.shape[1]
    rows = out_scr.shape[1]
    spans = (pl.ds(0, rows), pl.ds(rows, rows))
    sources, targets = [far_hbm], [far_scr]
    for refs in ((q_hbm, q_scr), (near_hbm, near_scr), (near_lse_hbm, near_lse_scr)):
        for span in spans:
            sources.append(refs[0].at[span])
            targets.append(refs[1].at[span])
    loads = started(sources, targets, in_sems)
    loads[0].wait()
    stores = []
    sums = []
    for place, out in enumerate((own_out, lent_out)):
        loads[1 + place].wait()
        span = slice(place * rows, (place + 1) * rows)

        def finish(tile, lanes):
            if tile == 0:
                loads[3 + place].wait()
                loads[5 + place].wait()
            attended = merge_states(
                near_scr[span, lanes], near_lse_scr[span, lanes],
                mixed_scr[place, :, lanes], lse_scr[place, :, lanes],
            )
            out_scr[place, :, lanes] = attended.astype(BF16)
            sums.append(jnp.sum(attended, axis=0, keepdims=True))
            stores.extend(
                started(
                    (out_scr.at[place, :, lanes],), (out.at[:, lanes],), out_sems,
                    place * (half // LANES) + tile,
                )
            )

        attend(q_scr[span, :], far_scr[:, :half], far_scr[:, half:], head_width,
               mixed_scr.at[place], lse_scr.at[place], finish)
    tiles = half // LANES
    total = jnp.concatenate([sums[t] + sums[tiles + t] for t in range(tiles)], axis=1)
    pad = jnp.zeros((1, pack_ref.shape[1] * pack_ref.shape[2] - 3 * half), F32)
    packed = pack_row((embedded_sum_ref[...], total, pad))
    pack_ref[...] = jnp.broadcast_to(packed[None], pack_ref.shape)
    for store in stores:
        store.wait()


def pack_row(pieces):
    flat = jnp.concatenate(pieces, axis=1)
    rows, lanes = PACK
    return jnp.concatenate([flat[:, r * lanes : (r + 1) * lanes] for r in range(rows)], axis=0)


def exact_row_times(row, matrix):
    top = row.astype(BF16).astype(F32)
    middle = (row - top).astype(BF16).astype(F32)
    low = row - top - middle
    parts = jnp.concatenate((top, middle, low, jnp.zeros((13, row.shape[1]), F32)), axis=0)
    product = jnp.dot(parts.astype(BF16), matrix, preferred_element_type=F32)
    return jnp.sum(product, axis=0, keepdims=True)


def unit_row(row):
    return row * lax.rsqrt(jnp.sum(row * row, axis=1, keepdims=True) + 1e-06)


def pooled_kernel(codes_ref, sums_ref, w_out_ref, w_head_ref, report_ref,
                  unit_ref, pack_ref, *, length):
    peers = sums_ref.shape[0]
    width = w_out_ref.shape[0]
    half = width // 2
    even = sums_ref[0]
    odd = sums_ref[1]
    for peer in range(2, peers, 2):
        even = even + sums_ref[peer]
        odd = odd + sums_ref[peer + 1]

    def flat(packed):
        return jnp.concatenate([packed[r : r + 1, :] for r in range(PACK[0])], axis=1)

    even, odd = flat(even), flat(odd)
    embedded_sum = even[:, :width] + odd[:, :width]
    attended_sum = jnp.concatenate(
        (even[:, width : width + half], odd[:, width : width + half]), axis=1
    )
    pooled = (embedded_sum + exact_row_times(attended_sum, w_out_ref[...])) * (1.0 / length)
    unit = unit_row(exact_row_times(pooled, w_head_ref[...]))
    unit_ref[...] = unit
    packed = pack_row((unit, unit_row(report_ref[...].astype(F32)), codes_ref[...][None, :]))
    pack_ref[...] = jnp.broadcast_to(packed[None], pack_ref.shape)


def contrast_kernel(all_ref, logits_ref, loss_ref):
    count = all_ref.shape[0]
    lanes = PACK[1]
    logits = jnp.zeros((count, count), F32)
    parts = 768 // lanes
    for r in range(parts):
        logits += lax.dot_general(
            all_ref[:, r, :], all_ref[:, parts + r, :], NT,
            precision=lax.Precision.HIGHEST, preferred_element_type=F32,
        )
    logits = logits * SOFTMAX_TEMPER
    logits_ref[...] = logits
    codes = all_ref[:, 2 * parts, :]
    down = lax.broadcasted_iota(jnp.int32, (count, count), 0)
    across = lax.broadcasted_iota(jnp.int32, (count, count), 1)
    diagonal = down == across
    slide_codes = codes[:, 0:1]
    report_codes = jnp.sum(jnp.where(diagonal, codes[:, 1:2], 0.0), axis=0, keepdims=True)
    positive = jnp.where((slide_codes == report_codes) | diagonal, 1.0, 0.0)

    def terms(axis):
        peak = jnp.max(logits, axis=axis, keepdims=True)
        lse = peak + jnp.log(jnp.sum(jnp.exp(logits - peak), axis=axis, keepdims=True))
        picked = jnp.sum(positive * (logits - lse), axis=axis, keepdims=True)
        return -picked / jnp.sum(positive, axis=axis, keepdims=True)

    both = jnp.sum(terms(1), axis=0, keepdims=True) + jnp.sum(terms(0), axis=1, keepdims=True)
    loss_ref[...] = both * (0.5 / count)


def on_device(
    tiles,
    w_embed,
    attn_gain,
    w_query,
    w_key,
    w_value,
    w_out,
    w_head,
    head_offset,
    slide_code,
    report_emb,
    report_code,
):
    _, rows, in_width = tiles.shape
    width = w_embed.shape[1]
    half = width // 2
    heads_count = head_offset.shape[0]
    head_width = width // heads_count
    ranks = lax.axis_size(SEQ_AXES)
    plane = lax.axis_size(("x", "y"))
    score_scale = 1.0 / math.sqrt(head_width)
    part = lax.axis_index("y") % 2
    parts = part.reshape(1)
    params = pltpu.CompilerParams(vmem_limit_bytes=LARGE_VMEM)
    small = pltpu.CompilerParams(vmem_limit_bytes=SMALL_VMEM)
    smem = pl.BlockSpec(memory_space=pltpu.SMEM)
    vmem = pl.BlockSpec(memory_space=pltpu.VMEM)
    anywhere = pl.BlockSpec(memory_space=pl.ANY)

    pieces = 3
    embedded, normed, embedded_sum = pl.pallas_call(
        embed_kernel,
        in_specs=[anywhere, anywhere, vmem],
        out_specs=[anywhere, vmem, vmem],
        out_shape=[
            jax.ShapeDtypeStruct((rows, width), BF16),
            pltpu.VMEM((rows, width), BF16),
            jax.ShapeDtypeStruct((1, width), F32),
        ],
        scratch_shapes=[
            pltpu.VMEM((rows, in_width), BF16),
            pltpu.VMEM((in_width, width), BF16),
            pltpu.VMEM((rows, width), BF16),
            pltpu.SemaphoreType.DMA((EMBED_STEPS,)),
            pltpu.SemaphoreType.DMA((pieces,)),
            pltpu.SemaphoreType.DMA((EMBED_STEPS,)),
        ],
        compiler_params=pltpu.CompilerParams(vmem_limit_bytes=EMBED_VMEM),
        name="embed",
    )(tiles.reshape(rows, in_width), w_embed, attn_gain)
    other_normed = swap_with(normed, "y")

    far_rows = rows // RATE
    far_own, keys_own, values_own = pl.pallas_call(
        own_rows_kernel,
        in_specs=[smem, smem, vmem, vmem, vmem],
        out_specs=[vmem, vmem, vmem],
        out_shape=[
            jax.ShapeDtypeStruct((2, far_rows, width), BF16),
            jax.ShapeDtypeStruct((rows, half), BF16),
            jax.ShapeDtypeStruct((rows, half), BF16),
        ],
        compiler_params=small,
        name="own_rows",
    )(parts, head_offset, normed, w_key, w_value)
    far_other = swap_with(far_own, "z_hi")
    payload = pl.pallas_call(
        payload_kernel,
        in_specs=[vmem, vmem],
        out_shape=jax.ShapeDtypeStruct((plane // 2, 2, 2, far_rows, width), BF16),
        compiler_params=small,
        name="payload",
    )(far_own, far_other).reshape(plane, 2 * far_rows, width)
    far = lax.all_to_all(payload, ("x", "y"), 0, 0, tiled=True).reshape(ranks * far_rows, width)

    lane_tiles = half // LANES
    half_rows = jax.ShapeDtypeStruct((rows, half), BF16)
    queries_own, own_mixed, own_lse = pl.pallas_call(
        functools.partial(own_kernel, head_width=head_width, score_scale=score_scale),
        in_specs=[smem] + [vmem] * 4,
        out_specs=[anywhere] * 3,
        out_shape=[
            pltpu.HBM((rows, half), BF16),
            pltpu.HBM((rows, half), F32),
            pltpu.HBM((rows, half), F32),
        ],
        scratch_shapes=[
            pltpu.VMEM((rows, half), BF16),
            pltpu.VMEM((rows, half), F32),
            pltpu.VMEM((rows, half), F32),
            pltpu.SemaphoreType.DMA((1 + 2 * lane_tiles,)),
        ],
        compiler_params=pltpu.CompilerParams(vmem_limit_bytes=32 << 20),
        cost_estimate=pl.CostEstimate(
            flops=3_000_000_000, bytes_accessed=4_000_000, transcendentals=2_000_000
        ),
        name="own_attention",
    )(parts, normed, w_query, keys_own, values_own)

    both_rows = jax.ShapeDtypeStruct((2 * rows, half), BF16)
    both_state = jax.ShapeDtypeStruct((2 * rows, half), F32)
    queries, near_mixed, near_lse = pl.pallas_call(
        functools.partial(near_kernel, head_width=head_width, score_scale=score_scale),
        in_specs=[smem] + [anywhere] * 9,
        out_specs=[anywhere] * 3,
        out_shape=[both_rows, both_state, both_state],
        scratch_shapes=[
            pltpu.VMEM((rows, width), BF16),
            pltpu.VMEM((3, width, half), BF16),
            pltpu.VMEM((2 * rows, half), BF16),
            pltpu.VMEM((2 * rows, half), BF16),
            pltpu.VMEM((2 * rows, half), BF16),
            pltpu.VMEM((rows, half), F32),
            pltpu.VMEM((rows, half), F32),
            pltpu.VMEM((2, rows, half), F32),
            pltpu.VMEM((2, rows, half), F32),
            pltpu.SemaphoreType.DMA((9,)),
            pltpu.SemaphoreType.DMA((2 + 4 * lane_tiles,)),
        ],
        compiler_params=params,
        cost_estimate=pl.CostEstimate(
            flops=9_000_000_000, bytes_accessed=8_000_000, transcendentals=6_000_000
        ),
        name="near_attention",
    )(parts, other_normed, keys_own, values_own, queries_own, own_mixed, own_lse,
      w_query, w_key, w_value)

    own_half, lent_half, sums = pl.pallas_call(
        functools.partial(far_kernel, head_width=head_width),
        in_specs=[anywhere] * 4 + [vmem],
        out_specs=[anywhere, anywhere, vmem],
        out_shape=[half_rows, half_rows, jax.ShapeDtypeStruct((ranks,) + PACK, F32)],
        scratch_shapes=[
            pltpu.VMEM((2 * rows, half), BF16),
            pltpu.VMEM((ranks * far_rows, width), BF16),
            pltpu.VMEM((2 * rows, half), F32),
            pltpu.VMEM((2 * rows, half), F32),
            pltpu.VMEM((2, rows, half), F32),
            pltpu.VMEM((2, rows, half), F32),
            pltpu.VMEM((2, rows, half), BF16),
            pltpu.SemaphoreType.DMA((7,)),
            pltpu.SemaphoreType.DMA((2 * lane_tiles,)),
        ],
        compiler_params=params,
        cost_estimate=pl.CostEstimate(
            flops=6_000_000_000, bytes_accessed=6_000_000, transcendentals=4_000_000
        ),
        name="far_attention",
    )(queries, far, near_mixed, near_lse, embedded_sum)

    sums = lax.all_to_all(sums, SEQ_AXES, 0, 0, tiled=True)
    lane = jnp.arange(2 * PACK[1], dtype=jnp.int32)
    codes = jnp.where(lane == 0, slide_code, jnp.where(lane == 1, report_code, 0)).astype(F32)
    w_mine = lax.dynamic_slice_in_dim(w_out, part * half, half, axis=0)
    w_theirs = lax.dynamic_slice_in_dim(w_out, (1 - part) * half, half, axis=0)
    encoded = embedded.astype(F32) + jnp.dot(own_half, w_mine, preferred_element_type=F32)
    sums, lent_half, encoded, codes = lax.optimization_barrier((sums, lent_half, encoded, codes))
    other_half = swap_with(lent_half, "y")
    encoded = encoded + jnp.dot(other_half, w_theirs, preferred_element_type=F32)
    encoded = encoded.astype(BF16).reshape(1, rows, width)

    slides = lax.axis_size("slide")
    slide_unit_vectors, packed = pl.pallas_call(
        functools.partial(pooled_kernel, length=rows * ranks),
        in_specs=[vmem] * 5,
        out_shape=[
            jax.ShapeDtypeStruct((1, width), F32),
            jax.ShapeDtypeStruct((slides,) + PACK, F32),
        ],
        compiler_params=small,
        name="pooled",
    )(codes, sums, w_out, w_head, report_emb)
    everyone = lax.all_to_all(packed, "slide", 0, 0, tiled=True)
    everyone, encoded = lax.optimization_barrier((everyone, encoded))
    logits, loss = pl.pallas_call(
        contrast_kernel,
        in_specs=[vmem],
        out_shape=[
            jax.ShapeDtypeStruct((slides, slides), F32),
            jax.ShapeDtypeStruct((1, 1), F32),
        ],
        compiler_params=small,
        name="contrast",
    )(everyone)
    return (encoded, slide_unit_vectors, logits, loss.reshape(()))


def solution(mesh):
    split = Mesh(mesh.devices.reshape(4, 2, 4, 8), SEQ_AXES + ("slide",))
    rows = P("slide", SEQ_AXES, None)
    return jax.shard_map(
        on_device,
        mesh=split,
        in_specs=(
            rows,
            P(),
            P(),
            P(),
            P(),
            P(),
            P(),
            P(),
            P(),
            P("slide"),
            P("slide", None),
            P("slide"),
        ),
        out_specs=(rows, P("slide", None), P(), P()),
        check_vma=False,
    )
```

```python
import functools
import math

import jax
import jax.numpy as jnp
from jax import lax
from jax.experimental import pallas as pl
from jax.experimental.pallas import tpu as pltpu
from jax.sharding import Mesh, PartitionSpec as P

RATE = 32
LANES = 128
PACK = (8, 256)
SOFTMAX_TEMPER = 1.0 / 0.07
NORM_EPS = 1e-05
NT = (((1,), (1,)), ((), ()))
NN = (((1,), (0,)), ((), ()))
SMALL_VMEM = 16 << 20
LARGE_VMEM = 58 << 20
EMBED_PIECES = 3
EMBED_VMEM = 59 << 20
SEQ_AXES = ("x", "z_hi", "y")
F32 = jnp.float32
BF16 = jnp.bfloat16


def swap_with(x, axis):
    return lax.ppermute(x, axis, [(i, i ^ 1) for i in range(lax.axis_size(axis))])


def head_window(head, width):
    first = head * width // LANES * LANES
    last = -(-(head * width + width) // LANES) * LANES
    return first, last, head * width - first


def in_head_lanes(head, width):
    first, last, offset = head_window(head, width)
    lane = lax.broadcasted_iota(jnp.int32, (1, last - first), 1)
    return (lane >= offset) & (lane < offset + width)


def attend(queries, keys, values, head_width, mixed_ref, lse_ref, finish=None):
    width = queries.shape[1]
    finished = 0
    for head in range(width // head_width):
        first, last, _ = head_window(head, head_width)
        mine = in_head_lanes(head, head_width)
        masked = jnp.where(mine, queries[:, first:last], jnp.zeros((), queries.dtype))
        scores = lax.dot_general(masked, keys[:, first:last], NT, preferred_element_type=F32)
        peak = jnp.max(scores, axis=1, keepdims=True)
        weights = jnp.exp(scores - peak)
        total = jnp.sum(weights, axis=1, keepdims=True)
        mixed = lax.dot_general(
            weights.astype(BF16), values[:, first:last], NN, preferred_element_type=F32
        )
        mixed = mixed * (1.0 / total)
        lse = jnp.broadcast_to(peak + jnp.log(total), mixed.shape)
        if head > 0:
            mixed = jnp.where(mine, mixed, mixed_ref[:, first:last])
            lse = jnp.where(mine, lse, lse_ref[:, first:last])
        mixed_ref[:, first:last] = mixed
        lse_ref[:, first:last] = lse
        while finish is not None and (finished + 1) * LANES <= (head + 1) * head_width:
            finish(finished, slice(finished * LANES, (finished + 1) * LANES))
            finished += 1


def merge_states(one, one_lse, two, two_lse):
    share = 1.0 / (1.0 + jnp.exp(two_lse - one_lse))
    return two + (one - two) * share


def started(sources, targets, sems, first=0):
    copies = []
    for place, (source, target) in enumerate(zip(sources, targets)):
        copies.append(pltpu.make_async_copy(source, target, sems.at[first + place]))
        copies[-1].start()
    return copies


def embed_kernel(x_hbm, w_hbm, gain_ref, embedded_hbm, normed_ref, sum_ref, x_scr, w_scr,
                 embedded_scr, x_sems, w_sems, out_sems):
    rows = x_scr.shape[0] // x_sems.shape[0]
    spans = [pl.ds(i * rows, rows) for i in range(x_sems.shape[0])]
    pieces = w_sems.shape[0]
    depth = w_scr.shape[0] // pieces
    parts = [pl.ds(i * depth, depth) for i in range(pieces)]
    x_loads = started([x_hbm.at[span] for span in spans], [x_scr.at[span] for span in spans], x_sems)
    w_loads = started([w_hbm.at[p] for p in parts], [w_scr.at[p] for p in parts], w_sems)
    for load in x_loads:
        load.wait()
    total = None
    for piece, load in enumerate(w_loads):
        load.wait()
        columns = slice(piece * depth, (piece + 1) * depth)
        product = jnp.dot(x_scr[:, columns], w_scr[columns, :], preferred_element_type=F32)
        total = product if total is None else total + product
    embedded = total.astype(BF16)
    embedded_scr[...] = embedded
    stores = started([embedded_scr], [embedded_hbm], out_sems)
    floats = embedded.astype(F32)
    centred = floats - jnp.mean(floats, axis=1, keepdims=True)
    spread = jnp.mean(centred * centred, axis=1, keepdims=True)
    normed = centred * lax.rsqrt(spread + NORM_EPS) * gain_ref[...][None, :]
    normed_ref[...] = normed.astype(BF16)
    sum_ref[...] = jnp.sum(floats, axis=0, keepdims=True)
    for store in stores:
        store.wait()


def own_rows_kernel(part_ref, offset_ref, x_ref, wk_ref, wv_ref, far_ref, k_ref, v_ref):
    rows, width = x_ref.shape
    half = width // 2
    heads = offset_ref.shape[0]
    lane = lax.broadcasted_iota(jnp.int32, (1, width), 1)
    lane_offset = jnp.zeros((1, width), jnp.int32)
    for head in range(heads):
        lane_offset = jnp.where(lane >= head * (width // heads), offset_ref[head], lane_offset)
    phase = lax.broadcasted_iota(jnp.int32, (RATE, width), 0)
    chosen = jnp.where(phase == lane_offset, 1.0, 0.0)
    upper = part_ref[0] == 1
    for place, (w_ref, half_ref) in enumerate(((wk_ref, k_ref), (wv_ref, v_ref))):
        full = jnp.dot(x_ref[...], w_ref[...], preferred_element_type=F32)
        half_ref[...] = jnp.where(upper, full[:, half:], full[:, :half]).astype(BF16)
        grouped = full.reshape(rows // RATE, RATE, width) * chosen[None]
        picked = jnp.sum(grouped, axis=1).astype(BF16)
        for part in range(2):
            far_ref[part, :, place * half : (place + 1) * half] = picked[
                :, part * half : (part + 1) * half
            ]


def payload_kernel(own_ref, other_ref, out_ref):
    for place, ref in enumerate((own_ref, other_ref)):
        out_ref[:, :, place, :, :] = jnp.broadcast_to(ref[...][None], out_ref.shape[:2] + ref.shape[1:])


def half_columns(w_hbm, part_ref):
    half = w_hbm.shape[1] // 2
    return w_hbm.at[:, pl.ds(pl.multiple_of(part_ref[0] * half, half), half)]


def own_kernel(part_ref, x_ref, wq_ref, k_ref, v_ref, q_out, mixed_out, lse_out,
               q_scr, mixed_scr, lse_scr, out_sems, *, head_width, score_scale):
    half = wq_ref.shape[1] // 2
    upper = part_ref[0] == 1
    wq = jnp.where(upper, wq_ref[:, half:], wq_ref[:, :half])
    q = jnp.dot(x_ref[...], wq, preferred_element_type=F32) * score_scale
    q_scr[...] = q.astype(BF16)
    stores = started((q_scr,), (q_out,), out_sems)

    def finish(tile, lanes):
        stores.extend(
            started(
                (mixed_scr.at[:, lanes], lse_scr.at[:, lanes]),
                (mixed_out.at[:, lanes], lse_out.at[:, lanes]),
                out_sems,
                1 + 2 * tile,
            )
        )

    attend(q_scr[...], k_ref[...], v_ref[...], head_width, mixed_scr, lse_scr, finish)
    for store in stores:
        store.wait()


def near_kernel(part_ref, other_hbm, k_hbm, v_hbm, q_hbm, own_mixed_hbm, own_lse_hbm,
                wq_hbm, wk_hbm, wv_hbm, q_out, mixed_out, lse_out,
                x_scr, w_scr, k_scr, v_scr, q_scr, own_mixed_scr, own_lse_scr, mixed_scr, lse_scr,
                in_sems, out_sems, *, head_width, score_scale):
    rows = x_scr.shape[0]
    own, other = pl.ds(0, rows), pl.ds(rows, rows)
    loads = started(
        (
            half_columns(wk_hbm, part_ref), other_hbm, half_columns(wv_hbm, part_ref),
            half_columns(wq_hbm, part_ref), k_hbm, v_hbm, q_hbm, own_mixed_hbm, own_lse_hbm,
        ),
        (
            w_scr.at[0], x_scr, w_scr.at[1],
            w_scr.at[2], k_scr.at[own], v_scr.at[own], q_scr.at[own], own_mixed_scr, own_lse_scr,
        ),
        in_sems,
    )
    loads[0].wait()
    loads[1].wait()
    k_scr[rows:, :] = jnp.dot(x_scr[...], w_scr[0], preferred_element_type=F32).astype(BF16)
    loads[2].wait()
    v_scr[rows:, :] = jnp.dot(x_scr[...], w_scr[1], preferred_element_type=F32).astype(BF16)
    loads[3].wait()
    q = jnp.dot(x_scr[...], w_scr[2], preferred_element_type=F32) * score_scale
    q_scr[rows:, :] = q.astype(BF16)
    stores = started((q_scr.at[other],), (q_out.at[other],), out_sems)
    loads[4].wait()
    loads[5].wait()

    def store_block(place, span, first):
        stores.extend(
            started(
                (mixed_scr.at[place], lse_scr.at[place]),
                (mixed_out.at[span], lse_out.at[span]),
                out_sems,
                first,
            )
        )

    attend(q_scr[rows:, :], k_scr[...], v_scr[...], head_width, mixed_scr.at[1], lse_scr.at[1])
    store_block(1, other, 2)
    loads[6].wait()
    stores += started((q_scr.at[own],), (q_out.at[own],), out_sems, 1)
    attend(q_scr[:rows, :], k_scr[rows:, :], v_scr[rows:, :], head_width, mixed_scr.at[0],
           lse_scr.at[0])
    loads[7].wait()
    loads[8].wait()
    own_lse, new_lse = own_lse_scr[...], lse_scr[0]
    mixed_scr[0] = merge_states(own_mixed_scr[...], own_lse, mixed_scr[0], new_lse)
    gap = jnp.exp(-jnp.abs(own_lse - new_lse))
    lse_scr[0] = jnp.maximum(own_lse, new_lse) + jnp.log(1.0 + gap)
    store_block(0, own, 4)
    for store in stores:
        store.wait()


def far_kernel(q_hbm, far_hbm, near_hbm, near_lse_hbm, embedded_sum_ref, own_out, lent_out,
               pack_ref, q_scr, far_scr, near_scr, near_lse_scr, mixed_scr, lse_scr, out_scr,
               in_sems, out_sems, *, head_width):
    half = q_scr.shape[1]
    rows = out_scr.shape[1]
    spans = (pl.ds(0, rows), pl.ds(rows, rows))
    sources, targets = [far_hbm], [far_scr]
    for refs in ((q_hbm, q_scr), (near_hbm, near_scr), (near_lse_hbm, near_lse_scr)):
        for span in spans:
            sources.append(refs[0].at[span])
            targets.append(refs[1].at[span])
    loads = started(sources, targets, in_sems)
    loads[0].wait()
    stores = []
    sums = []
    for place, out in enumerate((own_out, lent_out)):
        loads[1 + place].wait()
        span = slice(place * rows, (place + 1) * rows)
        attend(q_scr[span, :], far_scr[:, :half], far_scr[:, half:], head_width,
               mixed_scr.at[place], lse_scr.at[place])
        loads[3 + place].wait()
        loads[5 + place].wait()
        attended = merge_states(
            near_scr[span, :], near_lse_scr[span, :], mixed_scr[place], lse_scr[place]
        )
        out_scr[place] = attended.astype(BF16)
        stores += started((out_scr.at[place],), (out,), out_sems, place)
        sums.append(jnp.sum(attended, axis=0, keepdims=True))
    total = sums[0] + sums[1]
    pad = jnp.zeros((1, pack_ref.shape[1] * pack_ref.shape[2] - 3 * half), F32)
    packed = pack_row((embedded_sum_ref[...], total, pad))
    pack_ref[...] = jnp.broadcast_to(packed[None], pack_ref.shape)
    for store in stores:
        store.wait()


def pack_row(pieces):
    flat = jnp.concatenate(pieces, axis=1)
    rows, lanes = PACK
    return jnp.concatenate([flat[:, r * lanes : (r + 1) * lanes] for r in range(rows)], axis=0)


def exact_row_times(row, matrix):
    top = row.astype(BF16).astype(F32)
    middle = (row - top).astype(BF16).astype(F32)
    low = row - top - middle
    parts = jnp.concatenate((top, middle, low, jnp.zeros((13, row.shape[1]), F32)), axis=0)
    product = jnp.dot(parts.astype(BF16), matrix, preferred_element_type=F32)
    return jnp.sum(product, axis=0, keepdims=True)


def unit_row(row):
    return row * lax.rsqrt(jnp.sum(row * row, axis=1, keepdims=True) + 1e-06)


def pooled_kernel(codes_ref, sums_ref, w_out_ref, w_head_ref, report_ref,
                  unit_ref, pack_ref, *, length):
    peers = sums_ref.shape[0]
    width = w_out_ref.shape[0]
    half = width // 2
    even = sums_ref[0]
    odd = sums_ref[1]
    for peer in range(2, peers, 2):
        even = even + sums_ref[peer]
        odd = odd + sums_ref[peer + 1]

    def flat(packed):
        return jnp.concatenate([packed[r : r + 1, :] for r in range(PACK[0])], axis=1)

    even, odd = flat(even), flat(odd)
    embedded_sum = even[:, :width] + odd[:, :width]
    attended_sum = jnp.concatenate(
        (even[:, width : width + half], odd[:, width : width + half]), axis=1
    )
    pooled = (embedded_sum + exact_row_times(attended_sum, w_out_ref[...])) * (1.0 / length)
    unit = unit_row(exact_row_times(pooled, w_head_ref[...]))
    unit_ref[...] = unit
    packed = pack_row((unit, unit_row(report_ref[...].astype(F32)), codes_ref[...][None, :]))
    pack_ref[...] = jnp.broadcast_to(packed[None], pack_ref.shape)


def contrast_kernel(all_ref, logits_ref, loss_ref):
    count = all_ref.shape[0]
    lanes = PACK[1]
    logits = jnp.zeros((count, count), F32)
    parts = 768 // lanes
    for r in range(parts):
        logits += lax.dot_general(
            all_ref[:, r, :], all_ref[:, parts + r, :], NT,
            precision=lax.Precision.HIGHEST, preferred_element_type=F32,
        )
    logits = logits * SOFTMAX_TEMPER
    logits_ref[...] = logits
    codes = all_ref[:, 2 * parts, :]
    down = lax.broadcasted_iota(jnp.int32, (count, count), 0)
    across = lax.broadcasted_iota(jnp.int32, (count, count), 1)
    diagonal = down == across
    slide_codes = codes[:, 0:1]
    report_codes = jnp.sum(jnp.where(diagonal, codes[:, 1:2], 0.0), axis=0, keepdims=True)
    positive = jnp.where((slide_codes == report_codes) | diagonal, 1.0, 0.0)

    def terms(axis):
        peak = jnp.max(logits, axis=axis, keepdims=True)
        lse = peak + jnp.log(jnp.sum(jnp.exp(logits - peak), axis=axis, keepdims=True))
        picked = jnp.sum(positive * (logits - lse), axis=axis, keepdims=True)
        return -picked / jnp.sum(positive, axis=axis, keepdims=True)

    both = jnp.sum(terms(1), axis=0, keepdims=True) + jnp.sum(terms(0), axis=1, keepdims=True)
    loss_ref[...] = both * (0.5 / count)


def on_device(
    tiles,
    w_embed,
    attn_gain,
    w_query,
    w_key,
    w_value,
    w_out,
    w_head,
    head_offset,
    slide_code,
    report_emb,
    report_code,
):
    _, rows, in_width = tiles.shape
    width = w_embed.shape[1]
    half = width // 2
    heads_count = head_offset.shape[0]
    head_width = width // heads_count
    ranks = lax.axis_size(SEQ_AXES)
    plane = lax.axis_size(("x", "y"))
    score_scale = 1.0 / math.sqrt(head_width)
    part = lax.axis_index("y") % 2
    parts = part.reshape(1)
    params = pltpu.CompilerParams(vmem_limit_bytes=LARGE_VMEM)
    small = pltpu.CompilerParams(vmem_limit_bytes=SMALL_VMEM)
    smem = pl.BlockSpec(memory_space=pltpu.SMEM)
    vmem = pl.BlockSpec(memory_space=pltpu.VMEM)
    anywhere = pl.BlockSpec(memory_space=pl.ANY)

    embedded, normed, embedded_sum = pl.pallas_call(
        embed_kernel,
        in_specs=[anywhere, anywhere, vmem],
        out_specs=[anywhere, vmem, vmem],
        out_shape=[
            jax.ShapeDtypeStruct((rows, width), BF16),
            pltpu.VMEM((rows, width), BF16),
            jax.ShapeDtypeStruct((1, width), F32),
        ],
        scratch_shapes=[
            pltpu.VMEM((rows, in_width), BF16),
            pltpu.VMEM((in_width, width), BF16),
            pltpu.VMEM((rows, width), BF16),
            pltpu.SemaphoreType.DMA((2,)),
            pltpu.SemaphoreType.DMA((EMBED_PIECES,)),
            pltpu.SemaphoreType.DMA((1,)),
        ],
        compiler_params=pltpu.CompilerParams(vmem_limit_bytes=EMBED_VMEM),
        name="embed",
    )(tiles.reshape(rows, in_width), w_embed, attn_gain)
    other_normed = swap_with(normed, "y")

    far_rows = rows // RATE
    far_own, keys_own, values_own = pl.pallas_call(
        own_rows_kernel,
        in_specs=[smem, smem, vmem, vmem, vmem],
        out_specs=[vmem, vmem, vmem],
        out_shape=[
            jax.ShapeDtypeStruct((2, far_rows, width), BF16),
            jax.ShapeDtypeStruct((rows, half), BF16),
            jax.ShapeDtypeStruct((rows, half), BF16),
        ],
        compiler_params=small,
        name="own_rows",
    )(parts, head_offset, normed, w_key, w_value)
    far_other = swap_with(far_own, "z_hi")
    payload = pl.pallas_call(
        payload_kernel,
        in_specs=[vmem, vmem],
        out_shape=jax.ShapeDtypeStruct((plane // 2, 2, 2, far_rows, width), BF16),
        compiler_params=small,
        name="payload",
    )(far_own, far_other).reshape(plane, 2 * far_rows, width)
    far = lax.all_to_all(payload, ("x", "y"), 0, 0, tiled=True).reshape(ranks * far_rows, width)

    lane_tiles = half // LANES
    half_rows = jax.ShapeDtypeStruct((rows, half), BF16)
    queries_own, own_mixed, own_lse = pl.pallas_call(
        functools.partial(own_kernel, head_width=head_width, score_scale=score_scale),
        in_specs=[smem] + [vmem] * 4,
        out_specs=[anywhere] * 3,
        out_shape=[
            pltpu.HBM((rows, half), BF16),
            pltpu.HBM((rows, half), F32),
            pltpu.HBM((rows, half), F32),
        ],
        scratch_shapes=[
            pltpu.VMEM((rows, half), BF16),
            pltpu.VMEM((rows, half), F32),
            pltpu.VMEM((rows, half), F32),
            pltpu.SemaphoreType.DMA((1 + 2 * lane_tiles,)),
        ],
        compiler_params=pltpu.CompilerParams(vmem_limit_bytes=32 << 20),
        cost_estimate=pl.CostEstimate(
            flops=3_000_000_000, bytes_accessed=4_000_000, transcendentals=2_000_000
        ),
        name="own_attention",
    )(parts, normed, w_query, keys_own, values_own)

    both_rows = jax.ShapeDtypeStruct((2 * rows, half), BF16)
    both_state = jax.ShapeDtypeStruct((2 * rows, half), F32)
    queries, near_mixed, near_lse = pl.pallas_call(
        functools.partial(near_kernel, head_width=head_width, score_scale=score_scale),
        in_specs=[smem] + [anywhere] * 9,
        out_specs=[anywhere] * 3,
        out_shape=[both_rows, both_state, both_state],
        scratch_shapes=[
            pltpu.VMEM((rows, width), BF16),
            pltpu.VMEM((3, width, half), BF16),
            pltpu.VMEM((2 * rows, half), BF16),
            pltpu.VMEM((2 * rows, half), BF16),
            pltpu.VMEM((2 * rows, half), BF16),
            pltpu.VMEM((rows, half), F32),
            pltpu.VMEM((rows, half), F32),
            pltpu.VMEM((2, rows, half), F32),
            pltpu.VMEM((2, rows, half), F32),
            pltpu.SemaphoreType.DMA((9,)),
            pltpu.SemaphoreType.DMA((6,)),
        ],
        compiler_params=params,
        cost_estimate=pl.CostEstimate(
            flops=9_000_000_000, bytes_accessed=8_000_000, transcendentals=6_000_000
        ),
        name="near_attention",
    )(parts, other_normed, keys_own, values_own, queries_own, own_mixed, own_lse,
      w_query, w_key, w_value)

    own_half, lent_half, sums = pl.pallas_call(
        functools.partial(far_kernel, head_width=head_width),
        in_specs=[anywhere] * 4 + [vmem],
        out_specs=[anywhere, anywhere, vmem],
        out_shape=[half_rows, half_rows, jax.ShapeDtypeStruct((ranks,) + PACK, F32)],
        scratch_shapes=[
            pltpu.VMEM((2 * rows, half), BF16),
            pltpu.VMEM((ranks * far_rows, width), BF16),
            pltpu.VMEM((2 * rows, half), F32),
            pltpu.VMEM((2 * rows, half), F32),
            pltpu.VMEM((2, rows, half), F32),
            pltpu.VMEM((2, rows, half), F32),
            pltpu.VMEM((2, rows, half), BF16),
            pltpu.SemaphoreType.DMA((7,)),
            pltpu.SemaphoreType.DMA((2,)),
        ],
        compiler_params=params,
        cost_estimate=pl.CostEstimate(
            flops=6_000_000_000, bytes_accessed=6_000_000, transcendentals=4_000_000
        ),
        name="far_attention",
    )(queries, far, near_mixed, near_lse, embedded_sum)

    sums = lax.all_to_all(sums, SEQ_AXES, 0, 0, tiled=True)
    lane = jnp.arange(2 * PACK[1], dtype=jnp.int32)
    codes = jnp.where(lane == 0, slide_code, jnp.where(lane == 1, report_code, 0)).astype(F32)
    w_mine = lax.dynamic_slice_in_dim(w_out, part * half, half, axis=0)
    w_theirs = lax.dynamic_slice_in_dim(w_out, (1 - part) * half, half, axis=0)
    encoded = embedded.astype(F32) + jnp.dot(own_half, w_mine, preferred_element_type=F32)
    sums, lent_half, encoded, codes = lax.optimization_barrier((sums, lent_half, encoded, codes))
    other_half = swap_with(lent_half, "y")
    encoded = encoded + jnp.dot(other_half, w_theirs, preferred_element_type=F32)
    encoded = encoded.astype(BF16).reshape(1, rows, width)

    slides = lax.axis_size("slide")
    slide_unit_vectors, packed = pl.pallas_call(
        functools.partial(pooled_kernel, length=rows * ranks),
        in_specs=[vmem] * 5,
        out_shape=[
            jax.ShapeDtypeStruct((1, width), F32),
            jax.ShapeDtypeStruct((slides,) + PACK, F32),
        ],
        compiler_params=small,
        name="pooled",
    )(codes, sums, w_out, w_head, report_emb)
    everyone = lax.all_to_all(packed, "slide", 0, 0, tiled=True)
    everyone, encoded = lax.optimization_barrier((everyone, encoded))
    logits, loss = pl.pallas_call(
        contrast_kernel,
        in_specs=[vmem],
        out_shape=[
            jax.ShapeDtypeStruct((slides, slides), F32),
            jax.ShapeDtypeStruct((1, 1), F32),
        ],
        compiler_params=small,
        name="contrast",
    )(everyone)
    return (encoded, slide_unit_vectors, logits, loss.reshape(()))


def solution(mesh):
    split = Mesh(mesh.devices.reshape(4, 2, 4, 8), SEQ_AXES + ("slide",))
    rows = P("slide", SEQ_AXES, None)
    return jax.shard_map(
        on_device,
        mesh=split,
        in_specs=(
            rows,
            P(),
            P(),
            P(),
            P(),
            P(),
            P(),
            P(),
            P(),
            P("slide"),
            P("slide", None),
            P("slide"),
        ),
        out_specs=(rows, P("slide", None), P(), P()),
        check_vma=False,
    )
```

```python
import functools
import math

import jax
import jax.numpy as jnp
from jax import lax
from jax.experimental import pallas as pl
from jax.experimental.pallas import tpu as pltpu
from jax.sharding import Mesh, PartitionSpec as P

RATE = 32
LANES = 128
PACK = (8, 256)
SOFTMAX_TEMPER = 1.0 / 0.07
NORM_EPS = 1e-05
NT = (((1,), (1,)), ((), ()))
NN = (((1,), (0,)), ((), ()))
SMALL_VMEM = 16 << 20
LARGE_VMEM = 58 << 20
EMBED_PIECES = 3
EMBED_VMEM = 59 << 20
SEQ_AXES = ("x", "z_hi", "y")
F32 = jnp.float32
BF16 = jnp.bfloat16


def swap_with(x, axis):
    return lax.ppermute(x, axis, [(i, i ^ 1) for i in range(lax.axis_size(axis))])


def head_window(head, width):
    first = head * width // LANES * LANES
    last = -(-(head * width + width) // LANES) * LANES
    return first, last, head * width - first


def in_head_lanes(head, width):
    first, last, offset = head_window(head, width)
    lane = lax.broadcasted_iota(jnp.int32, (1, last - first), 1)
    return (lane >= offset) & (lane < offset + width)


def attend(queries, keys, values, head_width, mixed_ref, lse_ref, finish=None):
    width = queries.shape[1]
    finished = 0
    for head in range(width // head_width):
        first, last, _ = head_window(head, head_width)
        mine = in_head_lanes(head, head_width)
        masked = jnp.where(mine, queries[:, first:last], jnp.zeros((), queries.dtype))
        scores = lax.dot_general(masked, keys[:, first:last], NT, preferred_element_type=F32)
        peak = jnp.max(scores, axis=1, keepdims=True)
        weights = jnp.exp(scores - peak)
        total = jnp.sum(weights, axis=1, keepdims=True)
        mixed = lax.dot_general(
            weights.astype(BF16), values[:, first:last], NN, preferred_element_type=F32
        )
        mixed = mixed * (1.0 / total)
        lse = jnp.broadcast_to(peak + jnp.log(total), mixed.shape)
        if head > 0:
            mixed = jnp.where(mine, mixed, mixed_ref[:, first:last])
            lse = jnp.where(mine, lse, lse_ref[:, first:last])
        mixed_ref[:, first:last] = mixed
        lse_ref[:, first:last] = lse
        while finish is not None and (finished + 1) * LANES <= (head + 1) * head_width:
            finish(finished, slice(finished * LANES, (finished + 1) * LANES))
            finished += 1


def merge_states(one, one_lse, two, two_lse):
    share = 1.0 / (1.0 + jnp.exp(two_lse - one_lse))
    return two + (one - two) * share


def started(sources, targets, sems, first=0):
    copies = []
    for place, (source, target) in enumerate(zip(sources, targets)):
        copies.append(pltpu.make_async_copy(source, target, sems.at[first + place]))
        copies[-1].start()
    return copies


def embed_kernel(x_hbm, w_hbm, gain_ref, embedded_hbm, normed_ref, sum_ref, x_scr, w_scr,
                 embedded_scr, acc_scr, x_sems, w_sems, out_sems):
    rows = x_scr.shape[0] // x_sems.shape[0]
    spans = [pl.ds(i * rows, rows) for i in range(x_sems.shape[0])]
    pieces = w_sems.shape[0]
    depth = w_scr.shape[0] // pieces
    parts = [pl.ds(i * depth, depth) for i in range(pieces)]
    x_loads = started([x_hbm.at[span] for span in spans], [x_scr.at[span] for span in spans], x_sems)
    started([w_hbm.at[p] for p in parts], [w_scr.at[p] for p in parts], w_sems)
    for load in x_loads:
        load.wait()
    acc_scr[...] = jnp.zeros_like(acc_scr)

    def add_piece(piece, carry):
        span = pl.ds(pl.multiple_of(piece * depth, depth), depth)
        pltpu.make_async_copy(w_hbm.at[span], w_scr.at[span], w_sems.at[piece]).wait()
        acc_scr[...] += jnp.dot(x_scr[:, span], w_scr[span, :], preferred_element_type=F32)
        return carry

    lax.fori_loop(0, pieces, add_piece, 0)
    embedded = acc_scr[...].astype(BF16)
    embedded_scr[...] = embedded
    stores = started([embedded_scr], [embedded_hbm], out_sems)
    floats = embedded.astype(F32)
    centred = floats - jnp.mean(floats, axis=1, keepdims=True)
    spread = jnp.mean(centred * centred, axis=1, keepdims=True)
    normed = centred * lax.rsqrt(spread + NORM_EPS) * gain_ref[...][None, :]
    normed_ref[...] = normed.astype(BF16)
    sum_ref[...] = jnp.sum(floats, axis=0, keepdims=True)
    for store in stores:
        store.wait()


def own_rows_kernel(part_ref, offset_ref, x_ref, wk_ref, wv_ref, far_ref, k_ref, v_ref):
    rows, width = x_ref.shape
    half = width // 2
    heads = offset_ref.shape[0]
    lane = lax.broadcasted_iota(jnp.int32, (1, width), 1)
    lane_offset = jnp.zeros((1, width), jnp.int32)
    for head in range(heads):
        lane_offset = jnp.where(lane >= head * (width // heads), offset_ref[head], lane_offset)
    phase = lax.broadcasted_iota(jnp.int32, (RATE, width), 0)
    chosen = jnp.where(phase == lane_offset, 1.0, 0.0)
    upper = part_ref[0] == 1
    for place, (w_ref, half_ref) in enumerate(((wk_ref, k_ref), (wv_ref, v_ref))):
        full = jnp.dot(x_ref[...], w_ref[...], preferred_element_type=F32)
        half_ref[...] = jnp.where(upper, full[:, half:], full[:, :half]).astype(BF16)
        grouped = full.reshape(rows // RATE, RATE, width) * chosen[None]
        picked = jnp.sum(grouped, axis=1).astype(BF16)
        for part in range(2):
            far_ref[part, :, place * half : (place + 1) * half] = picked[
                :, part * half : (part + 1) * half
            ]


def payload_kernel(own_ref, other_ref, out_ref):
    for place, ref in enumerate((own_ref, other_ref)):
        out_ref[:, :, place, :, :] = jnp.broadcast_to(ref[...][None], out_ref.shape[:2] + ref.shape[1:])


def half_columns(w_hbm, part_ref):
    half = w_hbm.shape[1] // 2
    return w_hbm.at[:, pl.ds(pl.multiple_of(part_ref[0] * half, half), half)]


def own_kernel(part_ref, x_ref, wq_ref, k_ref, v_ref, q_out, mixed_out, lse_out,
               q_scr, mixed_scr, lse_scr, out_sems, *, head_width, score_scale):
    half = wq_ref.shape[1] // 2
    upper = part_ref[0] == 1
    wq = jnp.where(upper, wq_ref[:, half:], wq_ref[:, :half])
    q = jnp.dot(x_ref[...], wq, preferred_element_type=F32) * score_scale
    q_scr[...] = q.astype(BF16)
    stores = started((q_scr,), (q_out,), out_sems)

    def finish(tile, lanes):
        stores.extend(
            started(
                (mixed_scr.at[:, lanes], lse_scr.at[:, lanes]),
                (mixed_out.at[:, lanes], lse_out.at[:, lanes]),
                out_sems,
                1 + 2 * tile,
            )
        )

    attend(q_scr[...], k_ref[...], v_ref[...], head_width, mixed_scr, lse_scr, finish)
    for store in stores:
        store.wait()


def near_kernel(part_ref, other_hbm, k_hbm, v_hbm, q_hbm, own_mixed_hbm, own_lse_hbm,
                wq_hbm, wk_hbm, wv_hbm, q_out, mixed_out, lse_out,
                x_scr, w_scr, k_scr, v_scr, q_scr, own_mixed_scr, own_lse_scr, mixed_scr, lse_scr,
                in_sems, out_sems, *, head_width, score_scale):
    rows = x_scr.shape[0]
    own, other = pl.ds(0, rows), pl.ds(rows, rows)
    loads = started(
        (
            half_columns(wk_hbm, part_ref), other_hbm, half_columns(wv_hbm, part_ref),
            half_columns(wq_hbm, part_ref), k_hbm, v_hbm, q_hbm, own_mixed_hbm, own_lse_hbm,
        ),
        (
            w_scr.at[0], x_scr, w_scr.at[1],
            w_scr.at[2], k_scr.at[own], v_scr.at[own], q_scr.at[own], own_mixed_scr, own_lse_scr,
        ),
        in_sems,
    )
    loads[0].wait()
    loads[1].wait()
    k_scr[rows:, :] = jnp.dot(x_scr[...], w_scr[0], preferred_element_type=F32).astype(BF16)
    loads[2].wait()
    v_scr[rows:, :] = jnp.dot(x_scr[...], w_scr[1], preferred_element_type=F32).astype(BF16)
    loads[3].wait()
    q = jnp.dot(x_scr[...], w_scr[2], preferred_element_type=F32) * score_scale
    q_scr[rows:, :] = q.astype(BF16)
    stores = started((q_scr.at[other],), (q_out.at[other],), out_sems)
    loads[4].wait()
    loads[5].wait()

    def store_block(place, span, first):
        stores.extend(
            started(
                (mixed_scr.at[place], lse_scr.at[place]),
                (mixed_out.at[span], lse_out.at[span]),
                out_sems,
                first,
            )
        )

    attend(q_scr[rows:, :], k_scr[...], v_scr[...], head_width, mixed_scr.at[1], lse_scr.at[1])
    store_block(1, other, 2)
    loads[6].wait()
    stores += started((q_scr.at[own],), (q_out.at[own],), out_sems, 1)
    attend(q_scr[:rows, :], k_scr[rows:, :], v_scr[rows:, :], head_width, mixed_scr.at[0],
           lse_scr.at[0])
    loads[7].wait()
    loads[8].wait()
    own_lse, new_lse = own_lse_scr[...], lse_scr[0]
    mixed_scr[0] = merge_states(own_mixed_scr[...], own_lse, mixed_scr[0], new_lse)
    gap = jnp.exp(-jnp.abs(own_lse - new_lse))
    lse_scr[0] = jnp.maximum(own_lse, new_lse) + jnp.log(1.0 + gap)
    store_block(0, own, 4)
    for store in stores:
        store.wait()


def far_kernel(q_hbm, far_hbm, near_hbm, near_lse_hbm, embedded_sum_ref, own_ref,
               lent_ref, pack_ref, q_scr, far_scr, near_scr, near_lse_scr, mixed_scr, lse_scr, sum_scr,
               in_sems, *, head_width):
    half = q_scr.shape[1]
    rows = mixed_scr.shape[0]
    loads = started(
        (far_hbm, q_hbm, near_hbm, near_lse_hbm), (far_scr, q_scr, near_scr, near_lse_scr), in_sems
    )
    loads[0].wait()
    loads[1].wait()
    sum_scr[...] = jnp.zeros_like(sum_scr)

    def block(place, carry):
        span = pl.ds(pl.multiple_of(place * rows, rows), rows)
        attend(q_scr[span, :], far_scr[:, :half], far_scr[:, half:], head_width, mixed_scr, lse_scr)

        @pl.when(place == 0)
        def _():
            loads[2].wait()
            loads[3].wait()

        attended = merge_states(
            near_scr[span, :], near_lse_scr[span, :], mixed_scr[...], lse_scr[...]
        )
        rounded = attended.astype(BF16)

        @pl.when(place == 0)
        def _():
            own_ref[...] = rounded

        @pl.when(place == 1)
        def _():
            lent_ref[...] = rounded

        sum_scr[...] += jnp.sum(attended, axis=0, keepdims=True)
        return carry

    lax.fori_loop(0, q_scr.shape[0] // rows, block, 0)
    pad = jnp.zeros((1, pack_ref.shape[1] * pack_ref.shape[2] - 3 * half), F32)
    packed = pack_row((embedded_sum_ref[...], sum_scr[...], pad))
    pack_ref[...] = jnp.broadcast_to(packed[None], pack_ref.shape)


def pack_row(pieces):
    flat = jnp.concatenate(pieces, axis=1)
    rows, lanes = PACK
    return jnp.concatenate([flat[:, r * lanes : (r + 1) * lanes] for r in range(rows)], axis=0)


def exact_row_times(row, matrix):
    top = row.astype(BF16).astype(F32)
    middle = (row - top).astype(BF16).astype(F32)
    low = row - top - middle
    parts = jnp.concatenate((top, middle, low, jnp.zeros((13, row.shape[1]), F32)), axis=0)
    product = jnp.dot(parts.astype(BF16), matrix, preferred_element_type=F32)
    return jnp.sum(product, axis=0, keepdims=True)


def unit_row(row):
    return row * lax.rsqrt(jnp.sum(row * row, axis=1, keepdims=True) + 1e-06)


def pooled_kernel(codes_ref, sums_ref, w_out_ref, w_head_ref, report_ref,
                  unit_ref, pack_ref, *, length):
    peers = sums_ref.shape[0]
    width = w_out_ref.shape[0]
    half = width // 2
    even = sums_ref[0]
    odd = sums_ref[1]
    for peer in range(2, peers, 2):
        even = even + sums_ref[peer]
        odd = odd + sums_ref[peer + 1]

    def flat(packed):
        return jnp.concatenate([packed[r : r + 1, :] for r in range(PACK[0])], axis=1)

    even, odd = flat(even), flat(odd)
    embedded_sum = even[:, :width] + odd[:, :width]
    attended_sum = jnp.concatenate(
        (even[:, width : width + half], odd[:, width : width + half]), axis=1
    )
    pooled = (embedded_sum + exact_row_times(attended_sum, w_out_ref[...])) * (1.0 / length)
    unit = unit_row(exact_row_times(pooled, w_head_ref[...]))
    unit_ref[...] = unit
    packed = pack_row((unit, unit_row(report_ref[...].astype(F32)), codes_ref[...][None, :]))
    pack_ref[...] = jnp.broadcast_to(packed[None], pack_ref.shape)


def contrast_kernel(all_ref, logits_ref, loss_ref):
    count = all_ref.shape[0]
    lanes = PACK[1]
    logits = jnp.zeros((count, count), F32)
    parts = 768 // lanes
    for r in range(parts):
        logits += lax.dot_general(
            all_ref[:, r, :], all_ref[:, parts + r, :], NT,
            precision=lax.Precision.HIGHEST, preferred_element_type=F32,
        )
    logits = logits * SOFTMAX_TEMPER
    logits_ref[...] = logits
    codes = all_ref[:, 2 * parts, :]
    down = lax.broadcasted_iota(jnp.int32, (count, count), 0)
    across = lax.broadcasted_iota(jnp.int32, (count, count), 1)
    diagonal = down == across
    slide_codes = codes[:, 0:1]
    report_codes = jnp.sum(jnp.where(diagonal, codes[:, 1:2], 0.0), axis=0, keepdims=True)
    positive = jnp.where((slide_codes == report_codes) | diagonal, 1.0, 0.0)

    def terms(axis):
        peak = jnp.max(logits, axis=axis, keepdims=True)
        lse = peak + jnp.log(jnp.sum(jnp.exp(logits - peak), axis=axis, keepdims=True))
        picked = jnp.sum(positive * (logits - lse), axis=axis, keepdims=True)
        return -picked / jnp.sum(positive, axis=axis, keepdims=True)

    both = jnp.sum(terms(1), axis=0, keepdims=True) + jnp.sum(terms(0), axis=1, keepdims=True)
    loss_ref[...] = both * (0.5 / count)


def on_device(
    tiles,
    w_embed,
    attn_gain,
    w_query,
    w_key,
    w_value,
    w_out,
    w_head,
    head_offset,
    slide_code,
    report_emb,
    report_code,
):
    _, rows, in_width = tiles.shape
    width = w_embed.shape[1]
    half = width // 2
    heads_count = head_offset.shape[0]
    head_width = width // heads_count
    ranks = lax.axis_size(SEQ_AXES)
    plane = lax.axis_size(("x", "y"))
    score_scale = 1.0 / math.sqrt(head_width)
    part = lax.axis_index("y") % 2
    parts = part.reshape(1)
    params = pltpu.CompilerParams(vmem_limit_bytes=LARGE_VMEM)
    small = pltpu.CompilerParams(vmem_limit_bytes=SMALL_VMEM)
    smem = pl.BlockSpec(memory_space=pltpu.SMEM)
    vmem = pl.BlockSpec(memory_space=pltpu.VMEM)
    anywhere = pl.BlockSpec(memory_space=pl.ANY)

    embedded, normed, embedded_sum = pl.pallas_call(
        embed_kernel,
        in_specs=[anywhere, anywhere, vmem],
        out_specs=[anywhere, vmem, vmem],
        out_shape=[
            jax.ShapeDtypeStruct((rows, width), BF16),
            pltpu.VMEM((rows, width), BF16),
            jax.ShapeDtypeStruct((1, width), F32),
        ],
        scratch_shapes=[
            pltpu.VMEM((rows, in_width), BF16),
            pltpu.VMEM((in_width, width), BF16),
            pltpu.VMEM((rows, width), BF16),
            pltpu.VMEM((rows, width), F32),
            pltpu.SemaphoreType.DMA((2,)),
            pltpu.SemaphoreType.DMA((EMBED_PIECES,)),
            pltpu.SemaphoreType.DMA((1,)),
        ],
        compiler_params=pltpu.CompilerParams(vmem_limit_bytes=EMBED_VMEM),
        name="embed",
    )(tiles.reshape(rows, in_width), w_embed, attn_gain)
    other_normed = swap_with(normed, "y")

    far_rows = rows // RATE
    far_own, keys_own, values_own = pl.pallas_call(
        own_rows_kernel,
        in_specs=[smem, smem, vmem, vmem, vmem],
        out_specs=[vmem, vmem, vmem],
        out_shape=[
            jax.ShapeDtypeStruct((2, far_rows, width), BF16),
            jax.ShapeDtypeStruct((rows, half), BF16),
            jax.ShapeDtypeStruct((rows, half), BF16),
        ],
        compiler_params=small,
        name="own_rows",
    )(parts, head_offset, normed, w_key, w_value)
    far_other = swap_with(far_own, "z_hi")
    payload = pl.pallas_call(
        payload_kernel,
        in_specs=[vmem, vmem],
        out_shape=jax.ShapeDtypeStruct((plane // 2, 2, 2, far_rows, width), BF16),
        compiler_params=small,
        name="payload",
    )(far_own, far_other).reshape(plane, 2 * far_rows, width)
    far = lax.all_to_all(payload, ("x", "y"), 0, 0, tiled=True).reshape(ranks * far_rows, width)

    lane_tiles = half // LANES
    half_rows = jax.ShapeDtypeStruct((rows, half), BF16)
    queries_own, own_mixed, own_lse = pl.pallas_call(
        functools.partial(own_kernel, head_width=head_width, score_scale=score_scale),
        in_specs=[smem] + [vmem] * 4,
        out_specs=[anywhere] * 3,
        out_shape=[
            pltpu.HBM((rows, half), BF16),
            pltpu.HBM((rows, half), F32),
            pltpu.HBM((rows, half), F32),
        ],
        scratch_shapes=[
            pltpu.VMEM((rows, half), BF16),
            pltpu.VMEM((rows, half), F32),
            pltpu.VMEM((rows, half), F32),
            pltpu.SemaphoreType.DMA((1 + 2 * lane_tiles,)),
        ],
        compiler_params=pltpu.CompilerParams(vmem_limit_bytes=32 << 20),
        cost_estimate=pl.CostEstimate(
            flops=3_000_000_000, bytes_accessed=4_000_000, transcendentals=2_000_000
        ),
        name="own_attention",
    )(parts, normed, w_query, keys_own, values_own)

    both_rows = jax.ShapeDtypeStruct((2 * rows, half), BF16)
    both_state = jax.ShapeDtypeStruct((2 * rows, half), F32)
    queries, near_mixed, near_lse = pl.pallas_call(
        functools.partial(near_kernel, head_width=head_width, score_scale=score_scale),
        in_specs=[smem] + [anywhere] * 9,
        out_specs=[anywhere] * 3,
        out_shape=[both_rows, both_state, both_state],
        scratch_shapes=[
            pltpu.VMEM((rows, width), BF16),
            pltpu.VMEM((3, width, half), BF16),
            pltpu.VMEM((2 * rows, half), BF16),
            pltpu.VMEM((2 * rows, half), BF16),
            pltpu.VMEM((2 * rows, half), BF16),
            pltpu.VMEM((rows, half), F32),
            pltpu.VMEM((rows, half), F32),
            pltpu.VMEM((2, rows, half), F32),
            pltpu.VMEM((2, rows, half), F32),
            pltpu.SemaphoreType.DMA((9,)),
            pltpu.SemaphoreType.DMA((6,)),
        ],
        compiler_params=params,
        cost_estimate=pl.CostEstimate(
            flops=9_000_000_000, bytes_accessed=8_000_000, transcendentals=6_000_000
        ),
        name="near_attention",
    )(parts, other_normed, keys_own, values_own, queries_own, own_mixed, own_lse,
      w_query, w_key, w_value)

    own_half, lent_half, sums = pl.pallas_call(
        functools.partial(far_kernel, head_width=head_width),
        in_specs=[anywhere] * 4 + [vmem],
        out_specs=[vmem, vmem, vmem],
        out_shape=[half_rows, half_rows, jax.ShapeDtypeStruct((ranks,) + PACK, F32)],
        scratch_shapes=[
            pltpu.VMEM((2 * rows, half), BF16),
            pltpu.VMEM((ranks * far_rows, width), BF16),
            pltpu.VMEM((2 * rows, half), F32),
            pltpu.VMEM((2 * rows, half), F32),
            pltpu.VMEM((rows, half), F32),
            pltpu.VMEM((rows, half), F32),
            pltpu.VMEM((1, half), F32),
            pltpu.SemaphoreType.DMA((4,)),
        ],
        compiler_params=params,
        cost_estimate=pl.CostEstimate(
            flops=6_000_000_000, bytes_accessed=6_000_000, transcendentals=4_000_000
        ),
        name="far_attention",
    )(queries, far, near_mixed, near_lse, embedded_sum)

    sums = lax.all_to_all(sums, SEQ_AXES, 0, 0, tiled=True)
    lane = jnp.arange(2 * PACK[1], dtype=jnp.int32)
    codes = jnp.where(lane == 0, slide_code, jnp.where(lane == 1, report_code, 0)).astype(F32)
    w_mine = lax.dynamic_slice_in_dim(w_out, part * half, half, axis=0)
    w_theirs = lax.dynamic_slice_in_dim(w_out, (1 - part) * half, half, axis=0)
    encoded = embedded.astype(F32) + jnp.dot(own_half, w_mine, preferred_element_type=F32)
    sums, lent_half, encoded, codes = lax.optimization_barrier((sums, lent_half, encoded, codes))
    other_half = swap_with(lent_half, "y")
    encoded = encoded + jnp.dot(other_half, w_theirs, preferred_element_type=F32)
    encoded = encoded.astype(BF16).reshape(1, rows, width)

    slides = lax.axis_size("slide")
    slide_unit_vectors, packed = pl.pallas_call(
        functools.partial(pooled_kernel, length=rows * ranks),
        in_specs=[vmem] * 5,
        out_shape=[
            jax.ShapeDtypeStruct((1, width), F32),
            jax.ShapeDtypeStruct((slides,) + PACK, F32),
        ],
        compiler_params=small,
        name="pooled",
    )(codes, sums, w_out, w_head, report_emb)
    everyone = lax.all_to_all(packed, "slide", 0, 0, tiled=True)
    everyone, encoded = lax.optimization_barrier((everyone, encoded))
    logits, loss = pl.pallas_call(
        contrast_kernel,
        in_specs=[vmem],
        out_shape=[
            jax.ShapeDtypeStruct((slides, slides), F32),
            jax.ShapeDtypeStruct((1, 1), F32),
        ],
        compiler_params=small,
        name="contrast",
    )(everyone)
    return (encoded, slide_unit_vectors, logits, loss.reshape(()))


def solution(mesh):
    split = Mesh(mesh.devices.reshape(4, 2, 4, 8), SEQ_AXES + ("slide",))
    rows = P("slide", SEQ_AXES, None)
    return jax.shard_map(
        on_device,
        mesh=split,
        in_specs=(
            rows,
            P(),
            P(),
            P(),
            P(),
            P(),
            P(),
            P(),
            P(),
            P("slide"),
            P("slide", None),
            P("slide"),
        ),
        out_specs=(rows, P("slide", None), P(), P()),
        check_vma=False,
    )
```

```python
import functools
import math

import jax
import jax.numpy as jnp
from jax import lax
from jax.experimental import pallas as pl
from jax.experimental.pallas import tpu as pltpu
from jax.sharding import Mesh, PartitionSpec as P

RATE = 32
LANES = 128
PACK = (8, 256)
SOFTMAX_TEMPER = 1.0 / 0.07
NORM_EPS = 1e-05
NT = (((1,), (1,)), ((), ()))
NN = (((1,), (0,)), ((), ()))
SMALL_VMEM = 16 << 20
LARGE_VMEM = 58 << 20
EMBED_PIECES = 3
EMBED_VMEM = 59 << 20
SEQ_AXES = ("x", "z_hi", "y")
F32 = jnp.float32
BF16 = jnp.bfloat16


def swap_with(x, axis):
    return lax.ppermute(x, axis, [(i, i ^ 1) for i in range(lax.axis_size(axis))])


def head_window(head, width):
    first = head * width // LANES * LANES
    last = -(-(head * width + width) // LANES) * LANES
    return first, last, head * width - first


def in_head_lanes(head, width):
    first, last, offset = head_window(head, width)
    lane = lax.broadcasted_iota(jnp.int32, (1, last - first), 1)
    return (lane >= offset) & (lane < offset + width)


def attend(queries, keys, values, head_width, mixed_ref, lse_ref, finish=None):
    width = queries.shape[1]
    finished = 0
    for head in range(width // head_width):
        first, last, _ = head_window(head, head_width)
        mine = in_head_lanes(head, head_width)
        masked = jnp.where(mine, queries[:, first:last], jnp.zeros((), queries.dtype))
        scores = lax.dot_general(masked, keys[:, first:last], NT, preferred_element_type=F32)
        peak = jnp.max(scores, axis=1, keepdims=True)
        weights = jnp.exp(scores - peak)
        total = jnp.sum(weights, axis=1, keepdims=True)
        mixed = lax.dot_general(
            weights.astype(BF16), values[:, first:last], NN, preferred_element_type=F32
        )
        mixed = mixed * (1.0 / total)
        lse = jnp.broadcast_to(peak + jnp.log(total), mixed.shape)
        if head > 0:
            mixed = jnp.where(mine, mixed, mixed_ref[:, first:last])
            lse = jnp.where(mine, lse, lse_ref[:, first:last])
        mixed_ref[:, first:last] = mixed
        lse_ref[:, first:last] = lse
        while finish is not None and (finished + 1) * LANES <= (head + 1) * head_width:
            finish(finished, slice(finished * LANES, (finished + 1) * LANES))
            finished += 1


def merge_states(one, one_lse, two, two_lse):
    share = 1.0 / (1.0 + jnp.exp(two_lse - one_lse))
    return two + (one - two) * share


def started(sources, targets, sems, first=0):
    copies = []
    for place, (source, target) in enumerate(zip(sources, targets)):
        copies.append(pltpu.make_async_copy(source, target, sems.at[first + place]))
        copies[-1].start()
    return copies


def embed_kernel(x_hbm, w_hbm, gain_ref, embedded_hbm, normed_ref, sum_ref, x_scr, w_scr,
                 embedded_scr, x_sems, w_sems, out_sems):
    rows = x_scr.shape[0] // x_sems.shape[0]
    spans = [pl.ds(i * rows, rows) for i in range(x_sems.shape[0])]
    pieces = w_sems.shape[0]
    depth = w_scr.shape[0] // pieces
    parts = [pl.ds(i * depth, depth) for i in range(pieces)]
    x_loads = started([x_hbm.at[span] for span in spans], [x_scr.at[span] for span in spans], x_sems)
    w_loads = started([w_hbm.at[p] for p in parts], [w_scr.at[p] for p in parts], w_sems)
    for load in x_loads:
        load.wait()
    total = None
    for piece, load in enumerate(w_loads):
        load.wait()
        columns = slice(piece * depth, (piece + 1) * depth)
        product = jnp.dot(x_scr[:, columns], w_scr[columns, :], preferred_element_type=F32)
        total = product if total is None else total + product
    embedded = total.astype(BF16)
    embedded_scr[...] = embedded
    stores = started([embedded_scr], [embedded_hbm], out_sems)
    floats = embedded.astype(F32)
    centred = floats - jnp.mean(floats, axis=1, keepdims=True)
    spread = jnp.mean(centred * centred, axis=1, keepdims=True)
    normed = centred * lax.rsqrt(spread + NORM_EPS) * gain_ref[...][None, :]
    normed_ref[...] = normed.astype(BF16)
    sum_ref[...] = jnp.sum(floats, axis=0, keepdims=True)
    for store in stores:
        store.wait()


def own_rows_kernel(part_ref, offset_ref, x_ref, wk_ref, wv_ref, far_ref, k_ref, v_ref):
    rows, width = x_ref.shape
    half = width // 2
    heads = offset_ref.shape[0]
    lane = lax.broadcasted_iota(jnp.int32, (1, width), 1)
    lane_offset = jnp.zeros((1, width), jnp.int32)
    for head in range(heads):
        lane_offset = jnp.where(lane >= head * (width // heads), offset_ref[head], lane_offset)
    phase = lax.broadcasted_iota(jnp.int32, (RATE, width), 0)
    chosen = jnp.where(phase == lane_offset, 1.0, 0.0)
    upper = part_ref[0] == 1
    for place, (w_ref, half_ref) in enumerate(((wk_ref, k_ref), (wv_ref, v_ref))):
        full = jnp.dot(x_ref[...], w_ref[...], preferred_element_type=F32)
        half_ref[...] = jnp.where(upper, full[:, half:], full[:, :half]).astype(BF16)
        grouped = full.reshape(rows // RATE, RATE, width) * chosen[None]
        picked = jnp.sum(grouped, axis=1).astype(BF16)
        for part in range(2):
            far_ref[part, :, place * half : (place + 1) * half] = picked[
                :, part * half : (part + 1) * half
            ]


def payload_kernel(own_ref, other_ref, out_ref):
    for place, ref in enumerate((own_ref, other_ref)):
        out_ref[:, :, place, :, :] = jnp.broadcast_to(ref[...][None], out_ref.shape[:2] + ref.shape[1:])


def half_columns(w_hbm, part_ref):
    half = w_hbm.shape[1] // 2
    return w_hbm.at[:, pl.ds(pl.multiple_of(part_ref[0] * half, half), half)]


def own_kernel(part_ref, x_ref, wq_ref, k_ref, v_ref, q_out, mixed_out, lse_out,
               q_scr, mixed_scr, lse_scr, rounded_scr, out_sems, *, head_width, score_scale):
    half = wq_ref.shape[1] // 2
    upper = part_ref[0] == 1
    wq = jnp.where(upper, wq_ref[:, half:], wq_ref[:, :half])
    q = jnp.dot(x_ref[...], wq, preferred_element_type=F32) * score_scale
    q_scr[...] = q.astype(BF16)
    stores = started((q_scr,), (q_out,), out_sems)

    def finish(tile, lanes):
        rounded_scr[:, lanes] = mixed_scr[:, lanes].astype(BF16)
        stores.extend(
            started(
                (rounded_scr.at[:, lanes], lse_scr.at[:, lanes]),
                (mixed_out.at[:, lanes], lse_out.at[:, lanes]),
                out_sems,
                1 + 2 * tile,
            )
        )

    attend(q_scr[...], k_ref[...], v_ref[...], head_width, mixed_scr, lse_scr, finish)
    for store in stores:
        store.wait()


def near_kernel(part_ref, other_hbm, k_hbm, v_hbm, q_hbm, own_mixed_hbm, own_lse_hbm,
                wq_hbm, wk_hbm, wv_hbm, q_out, mixed_out, lse_out,
                x_scr, w_scr, k_scr, v_scr, q_scr, own_mixed_scr, own_lse_scr, mixed_scr, lse_scr,
                rounded_scr, in_sems, out_sems, *, head_width, score_scale):
    rows = x_scr.shape[0]
    own, other = pl.ds(0, rows), pl.ds(rows, rows)
    loads = started(
        (
            half_columns(wk_hbm, part_ref), other_hbm, half_columns(wv_hbm, part_ref),
            half_columns(wq_hbm, part_ref), k_hbm, v_hbm, q_hbm, own_mixed_hbm, own_lse_hbm,
        ),
        (
            w_scr.at[0], x_scr, w_scr.at[1],
            w_scr.at[2], k_scr.at[own], v_scr.at[own], q_scr.at[own], own_mixed_scr, own_lse_scr,
        ),
        in_sems,
    )
    loads[0].wait()
    loads[1].wait()
    k_scr[rows:, :] = jnp.dot(x_scr[...], w_scr[0], preferred_element_type=F32).astype(BF16)
    loads[2].wait()
    v_scr[rows:, :] = jnp.dot(x_scr[...], w_scr[1], preferred_element_type=F32).astype(BF16)
    loads[3].wait()
    q = jnp.dot(x_scr[...], w_scr[2], preferred_element_type=F32) * score_scale
    q_scr[rows:, :] = q.astype(BF16)
    stores = started((q_scr.at[other],), (q_out.at[other],), out_sems)
    loads[4].wait()
    loads[5].wait()

    def store_block(place, span, first):
        rounded_scr[place] = mixed_scr[place].astype(BF16)
        stores.extend(
            started(
                (rounded_scr.at[place], lse_scr.at[place]),
                (mixed_out.at[span], lse_out.at[span]),
                out_sems,
                first,
            )
        )

    attend(q_scr[rows:, :], k_scr[...], v_scr[...], head_width, mixed_scr.at[1], lse_scr.at[1])
    store_block(1, other, 2)
    loads[6].wait()
    stores += started((q_scr.at[own],), (q_out.at[own],), out_sems, 1)
    attend(q_scr[:rows, :], k_scr[rows:, :], v_scr[rows:, :], head_width, mixed_scr.at[0],
           lse_scr.at[0])
    loads[7].wait()
    loads[8].wait()
    own_lse, new_lse = own_lse_scr[...], lse_scr[0]
    mixed_scr[0] = merge_states(own_mixed_scr[...].astype(F32), own_lse, mixed_scr[0], new_lse)
    gap = jnp.exp(-jnp.abs(own_lse - new_lse))
    lse_scr[0] = jnp.maximum(own_lse, new_lse) + jnp.log(1.0 + gap)
    store_block(0, own, 4)
    for store in stores:
        store.wait()


def far_kernel(q_hbm, far_hbm, near_hbm, near_lse_hbm, embedded_sum_ref, own_ref,
               lent_ref, pack_ref, q_scr, far_scr, near_scr, near_lse_scr, mixed_scr, lse_scr, sum_scr,
               in_sems, *, head_width):
    half = q_scr.shape[1]
    rows = mixed_scr.shape[0]
    loads = started(
        (far_hbm, q_hbm, near_hbm, near_lse_hbm), (far_scr, q_scr, near_scr, near_lse_scr), in_sems
    )
    loads[0].wait()
    loads[1].wait()
    sum_scr[...] = jnp.zeros_like(sum_scr)

    def block(place, carry):
        span = pl.ds(pl.multiple_of(place * rows, rows), rows)
        attend(q_scr[span, :], far_scr[:, :half], far_scr[:, half:], head_width, mixed_scr, lse_scr)

        @pl.when(place == 0)
        def _():
            loads[2].wait()
            loads[3].wait()

        attended = merge_states(
            near_scr[span, :].astype(F32), near_lse_scr[span, :], mixed_scr[...], lse_scr[...]
        )
        rounded = attended.astype(BF16)

        @pl.when(place == 0)
        def _():
            own_ref[...] = rounded

        @pl.when(place == 1)
        def _():
            lent_ref[...] = rounded

        sum_scr[...] += jnp.sum(attended, axis=0, keepdims=True)
        return carry

    lax.fori_loop(0, q_scr.shape[0] // rows, block, 0)
    pad = jnp.zeros((1, pack_ref.shape[1] * pack_ref.shape[2] - 3 * half), F32)
    packed = pack_row((embedded_sum_ref[...], sum_scr[...], pad))
    pack_ref[...] = jnp.broadcast_to(packed[None], pack_ref.shape)


def pack_row(pieces):
    flat = jnp.concatenate(pieces, axis=1)
    rows, lanes = PACK
    return jnp.concatenate([flat[:, r * lanes : (r + 1) * lanes] for r in range(rows)], axis=0)


def exact_row_times(row, matrix):
    top = row.astype(BF16).astype(F32)
    middle = (row - top).astype(BF16).astype(F32)
    low = row - top - middle
    parts = jnp.concatenate((top, middle, low, jnp.zeros((13, row.shape[1]), F32)), axis=0)
    product = jnp.dot(parts.astype(BF16), matrix, preferred_element_type=F32)
    return jnp.sum(product, axis=0, keepdims=True)


def unit_row(row):
    return row * lax.rsqrt(jnp.sum(row * row, axis=1, keepdims=True) + 1e-06)


def pooled_kernel(codes_ref, sums_ref, w_out_ref, w_head_ref, report_ref,
                  unit_ref, pack_ref, *, length):
    peers = sums_ref.shape[0]
    width = w_out_ref.shape[0]
    half = width // 2
    even = sums_ref[0]
    odd = sums_ref[1]
    for peer in range(2, peers, 2):
        even = even + sums_ref[peer]
        odd = odd + sums_ref[peer + 1]

    def flat(packed):
        return jnp.concatenate([packed[r : r + 1, :] for r in range(PACK[0])], axis=1)

    even, odd = flat(even), flat(odd)
    embedded_sum = even[:, :width] + odd[:, :width]
    attended_sum = jnp.concatenate(
        (even[:, width : width + half], odd[:, width : width + half]), axis=1
    )
    pooled = (embedded_sum + exact_row_times(attended_sum, w_out_ref[...])) * (1.0 / length)
    unit = unit_row(exact_row_times(pooled, w_head_ref[...]))
    unit_ref[...] = unit
    packed = pack_row((unit, unit_row(report_ref[...].astype(F32)), codes_ref[...][None, :]))
    pack_ref[...] = jnp.broadcast_to(packed[None], pack_ref.shape)


def contrast_kernel(all_ref, logits_ref, loss_ref):
    count = all_ref.shape[0]
    lanes = PACK[1]
    logits = jnp.zeros((count, count), F32)
    parts = 768 // lanes
    for r in range(parts):
        logits += lax.dot_general(
            all_ref[:, r, :], all_ref[:, parts + r, :], NT,
            precision=lax.Precision.HIGHEST, preferred_element_type=F32,
        )
    logits = logits * SOFTMAX_TEMPER
    logits_ref[...] = logits
    codes = all_ref[:, 2 * parts, :]
    down = lax.broadcasted_iota(jnp.int32, (count, count), 0)
    across = lax.broadcasted_iota(jnp.int32, (count, count), 1)
    diagonal = down == across
    slide_codes = codes[:, 0:1]
    report_codes = jnp.sum(jnp.where(diagonal, codes[:, 1:2], 0.0), axis=0, keepdims=True)
    positive = jnp.where((slide_codes == report_codes) | diagonal, 1.0, 0.0)

    def terms(axis):
        peak = jnp.max(logits, axis=axis, keepdims=True)
        lse = peak + jnp.log(jnp.sum(jnp.exp(logits - peak), axis=axis, keepdims=True))
        picked = jnp.sum(positive * (logits - lse), axis=axis, keepdims=True)
        return -picked / jnp.sum(positive, axis=axis, keepdims=True)

    both = jnp.sum(terms(1), axis=0, keepdims=True) + jnp.sum(terms(0), axis=1, keepdims=True)
    loss_ref[...] = both * (0.5 / count)


def on_device(
    tiles,
    w_embed,
    attn_gain,
    w_query,
    w_key,
    w_value,
    w_out,
    w_head,
    head_offset,
    slide_code,
    report_emb,
    report_code,
):
    _, rows, in_width = tiles.shape
    width = w_embed.shape[1]
    half = width // 2
    heads_count = head_offset.shape[0]
    head_width = width // heads_count
    ranks = lax.axis_size(SEQ_AXES)
    plane = lax.axis_size(("x", "y"))
    score_scale = 1.0 / math.sqrt(head_width)
    part = lax.axis_index("y") % 2
    parts = part.reshape(1)
    params = pltpu.CompilerParams(vmem_limit_bytes=LARGE_VMEM)
    small = pltpu.CompilerParams(vmem_limit_bytes=SMALL_VMEM)
    smem = pl.BlockSpec(memory_space=pltpu.SMEM)
    vmem = pl.BlockSpec(memory_space=pltpu.VMEM)
    anywhere = pl.BlockSpec(memory_space=pl.ANY)

    embedded, normed, embedded_sum = pl.pallas_call(
        embed_kernel,
        in_specs=[anywhere, anywhere, vmem],
        out_specs=[anywhere, vmem, vmem],
        out_shape=[
            jax.ShapeDtypeStruct((rows, width), BF16),
            pltpu.VMEM((rows, width), BF16),
            jax.ShapeDtypeStruct((1, width), F32),
        ],
        scratch_shapes=[
            pltpu.VMEM((rows, in_width), BF16),
            pltpu.VMEM((in_width, width), BF16),
            pltpu.VMEM((rows, width), BF16),
            pltpu.SemaphoreType.DMA((2,)),
            pltpu.SemaphoreType.DMA((EMBED_PIECES,)),
            pltpu.SemaphoreType.DMA((1,)),
        ],
        compiler_params=pltpu.CompilerParams(vmem_limit_bytes=EMBED_VMEM),
        name="embed",
    )(tiles.reshape(rows, in_width), w_embed, attn_gain)
    other_normed = swap_with(normed, "y")

    far_rows = rows // RATE
    far_own, keys_own, values_own = pl.pallas_call(
        own_rows_kernel,
        in_specs=[smem, smem, vmem, vmem, vmem],
        out_specs=[vmem, vmem, vmem],
        out_shape=[
            jax.ShapeDtypeStruct((2, far_rows, width), BF16),
            jax.ShapeDtypeStruct((rows, half), BF16),
            jax.ShapeDtypeStruct((rows, half), BF16),
        ],
        compiler_params=small,
        name="own_rows",
    )(parts, head_offset, normed, w_key, w_value)
    far_other = swap_with(far_own, "z_hi")
    payload = pl.pallas_call(
        payload_kernel,
        in_specs=[vmem, vmem],
        out_shape=jax.ShapeDtypeStruct((plane // 2, 2, 2, far_rows, width), BF16),
        compiler_params=small,
        name="payload",
    )(far_own, far_other).reshape(plane, 2 * far_rows, width)
    far = lax.all_to_all(payload, ("x", "y"), 0, 0, tiled=True).reshape(ranks * far_rows, width)

    lane_tiles = half // LANES
    half_rows = jax.ShapeDtypeStruct((rows, half), BF16)
    queries_own, own_mixed, own_lse = pl.pallas_call(
        functools.partial(own_kernel, head_width=head_width, score_scale=score_scale),
        in_specs=[smem] + [vmem] * 4,
        out_specs=[anywhere] * 3,
        out_shape=[
            pltpu.HBM((rows, half), BF16),
            pltpu.HBM((rows, half), BF16),
            pltpu.HBM((rows, half), F32),
        ],
        scratch_shapes=[
            pltpu.VMEM((rows, half), BF16),
            pltpu.VMEM((rows, half), F32),
            pltpu.VMEM((rows, half), F32),
            pltpu.VMEM((rows, half), BF16),
            pltpu.SemaphoreType.DMA((1 + 2 * lane_tiles,)),
        ],
        compiler_params=pltpu.CompilerParams(vmem_limit_bytes=32 << 20),
        cost_estimate=pl.CostEstimate(
            flops=3_000_000_000, bytes_accessed=4_000_000, transcendentals=2_000_000
        ),
        name="own_attention",
    )(parts, normed, w_query, keys_own, values_own)

    both_rows = jax.ShapeDtypeStruct((2 * rows, half), BF16)
    both_state = jax.ShapeDtypeStruct((2 * rows, half), F32)
    queries, near_mixed, near_lse = pl.pallas_call(
        functools.partial(near_kernel, head_width=head_width, score_scale=score_scale),
        in_specs=[smem] + [anywhere] * 9,
        out_specs=[anywhere] * 3,
        out_shape=[both_rows, both_rows, both_state],
        scratch_shapes=[
            pltpu.VMEM((rows, width), BF16),
            pltpu.VMEM((3, width, half), BF16),
            pltpu.VMEM((2 * rows, half), BF16),
            pltpu.VMEM((2 * rows, half), BF16),
            pltpu.VMEM((2 * rows, half), BF16),
            pltpu.VMEM((rows, half), BF16),
            pltpu.VMEM((rows, half), F32),
            pltpu.VMEM((2, rows, half), F32),
            pltpu.VMEM((2, rows, half), F32),
            pltpu.VMEM((2, rows, half), BF16),
            pltpu.SemaphoreType.DMA((9,)),
            pltpu.SemaphoreType.DMA((6,)),
        ],
        compiler_params=params,
        cost_estimate=pl.CostEstimate(
            flops=9_000_000_000, bytes_accessed=8_000_000, transcendentals=6_000_000
        ),
        name="near_attention",
    )(parts, other_normed, keys_own, values_own, queries_own, own_mixed, own_lse,
      w_query, w_key, w_value)

    own_half, lent_half, sums = pl.pallas_call(
        functools.partial(far_kernel, head_width=head_width),
        in_specs=[anywhere] * 4 + [vmem],
        out_specs=[vmem, vmem, vmem],
        out_shape=[half_rows, half_rows, jax.ShapeDtypeStruct((ranks,) + PACK, F32)],
        scratch_shapes=[
            pltpu.VMEM((2 * rows, half), BF16),
            pltpu.VMEM((ranks * far_rows, width), BF16),
            pltpu.VMEM((2 * rows, half), BF16),
            pltpu.VMEM((2 * rows, half), F32),
            pltpu.VMEM((rows, half), F32),
            pltpu.VMEM((rows, half), F32),
            pltpu.VMEM((1, half), F32),
            pltpu.SemaphoreType.DMA((4,)),
        ],
        compiler_params=params,
        cost_estimate=pl.CostEstimate(
            flops=6_000_000_000, bytes_accessed=6_000_000, transcendentals=4_000_000
        ),
        name="far_attention",
    )(queries, far, near_mixed, near_lse, embedded_sum)

    sums = lax.all_to_all(sums, SEQ_AXES, 0, 0, tiled=True)
    lane = jnp.arange(2 * PACK[1], dtype=jnp.int32)
    codes = jnp.where(lane == 0, slide_code, jnp.where(lane == 1, report_code, 0)).astype(F32)
    w_mine = lax.dynamic_slice_in_dim(w_out, part * half, half, axis=0)
    w_theirs = lax.dynamic_slice_in_dim(w_out, (1 - part) * half, half, axis=0)
    encoded = embedded.astype(F32) + jnp.dot(own_half, w_mine, preferred_element_type=F32)
    sums, lent_half, encoded, codes = lax.optimization_barrier((sums, lent_half, encoded, codes))
    other_half = swap_with(lent_half, "y")
    encoded = encoded + jnp.dot(other_half, w_theirs, preferred_element_type=F32)
    encoded = encoded.astype(BF16).reshape(1, rows, width)

    slides = lax.axis_size("slide")
    slide_unit_vectors, packed = pl.pallas_call(
        functools.partial(pooled_kernel, length=rows * ranks),
        in_specs=[vmem] * 5,
        out_shape=[
            jax.ShapeDtypeStruct((1, width), F32),
            jax.ShapeDtypeStruct((slides,) + PACK, F32),
        ],
        compiler_params=small,
        name="pooled",
    )(codes, sums, w_out, w_head, report_emb)
    everyone = lax.all_to_all(packed, "slide", 0, 0, tiled=True)
    everyone, encoded = lax.optimization_barrier((everyone, encoded))
    logits, loss = pl.pallas_call(
        contrast_kernel,
        in_specs=[vmem],
        out_shape=[
            jax.ShapeDtypeStruct((slides, slides), F32),
            jax.ShapeDtypeStruct((1, 1), F32),
        ],
        compiler_params=small,
        name="contrast",
    )(everyone)
    return (encoded, slide_unit_vectors, logits, loss.reshape(()))


def solution(mesh):
    split = Mesh(mesh.devices.reshape(4, 2, 4, 8), SEQ_AXES + ("slide",))
    rows = P("slide", SEQ_AXES, None)
    return jax.shard_map(
        on_device,
        mesh=split,
        in_specs=(
            rows,
            P(),
            P(),
            P(),
            P(),
            P(),
            P(),
            P(),
            P(),
            P("slide"),
            P("slide", None),
            P("slide"),
        ),
        out_specs=(rows, P("slide", None), P(), P()),
        check_vma=False,
    )
```

```python
import functools
import math

import jax
import jax.numpy as jnp
from jax import lax
from jax.experimental import pallas as pl
from jax.experimental.pallas import tpu as pltpu
from jax.sharding import Mesh, PartitionSpec as P

RATE = 32
LANES = 128
PACK = (8, 256)
SOFTMAX_TEMPER = 1.0 / 0.07
NORM_EPS = 1e-05
NT = (((1,), (1,)), ((), ()))
NN = (((1,), (0,)), ((), ()))
SMALL_VMEM = 16 << 20
LARGE_VMEM = 58 << 20
EMBED_PIECES = 3
EMBED_VMEM = 59 << 20
SEQ_AXES = ("x", "z_hi", "y")
F32 = jnp.float32
BF16 = jnp.bfloat16


def swap_with(x, axis):
    return lax.ppermute(x, axis, [(i, i ^ 1) for i in range(lax.axis_size(axis))])


def head_window(head, width):
    first = head * width // LANES * LANES
    last = -(-(head * width + width) // LANES) * LANES
    return first, last, head * width - first


def in_head_lanes(head, width):
    first, last, offset = head_window(head, width)
    lane = lax.broadcasted_iota(jnp.int32, (1, last - first), 1)
    return (lane >= offset) & (lane < offset + width)


def attend(queries, keys, values, head_width, mixed_ref, lse_ref, finish=None):
    width = queries.shape[1]
    finished = 0
    for head in range(width // head_width):
        first, last, _ = head_window(head, head_width)
        mine = in_head_lanes(head, head_width)
        masked = jnp.where(mine, queries[:, first:last], jnp.zeros((), queries.dtype))
        scores = lax.dot_general(masked, keys[:, first:last], NT, preferred_element_type=F32)
        peak = jnp.max(scores, axis=1, keepdims=True)
        weights = jnp.exp(scores - peak)
        total = jnp.sum(weights, axis=1, keepdims=True)
        mixed = lax.dot_general(
            weights.astype(BF16), values[:, first:last], NN, preferred_element_type=F32
        )
        mixed = mixed * (1.0 / total)
        lse = jnp.broadcast_to(peak + jnp.log(total), mixed.shape)
        if head > 0:
            mixed = jnp.where(mine, mixed, mixed_ref[:, first:last])
            lse = jnp.where(mine, lse, lse_ref[:, first:last])
        mixed_ref[:, first:last] = mixed
        lse_ref[:, first:last] = lse
        while finish is not None and (finished + 1) * LANES <= (head + 1) * head_width:
            finish(finished, slice(finished * LANES, (finished + 1) * LANES))
            finished += 1


def merge_states(one, one_lse, two, two_lse):
    share = 1.0 / (1.0 + jnp.exp(two_lse - one_lse))
    return two + (one - two) * share


def started(sources, targets, sems, first=0):
    copies = []
    for place, (source, target) in enumerate(zip(sources, targets)):
        copies.append(pltpu.make_async_copy(source, target, sems.at[first + place]))
        copies[-1].start()
    return copies


def embed_kernel(x_hbm, w_hbm, gain_ref, embedded_hbm, normed_ref, sum_ref, x_scr, w_scr,
                 embedded_scr, x_sems, w_sems, out_sems):
    rows = x_scr.shape[0] // x_sems.shape[0]
    spans = [pl.ds(i * rows, rows) for i in range(x_sems.shape[0])]
    pieces = w_sems.shape[0]
    depth = w_scr.shape[0] // pieces
    parts = [pl.ds(i * depth, depth) for i in range(pieces)]
    x_loads = started([x_hbm.at[span] for span in spans], [x_scr.at[span] for span in spans], x_sems)
    w_loads = started([w_hbm.at[p] for p in parts], [w_scr.at[p] for p in parts], w_sems)
    for load in x_loads:
        load.wait()
    total = None
    for piece, load in enumerate(w_loads):
        load.wait()
        columns = slice(piece * depth, (piece + 1) * depth)
        product = jnp.dot(x_scr[:, columns], w_scr[columns, :], preferred_element_type=F32)
        total = product if total is None else total + product
    embedded = total.astype(BF16)
    embedded_scr[...] = embedded
    stores = started([embedded_scr], [embedded_hbm], out_sems)
    floats = embedded.astype(F32)
    centred = floats - jnp.mean(floats, axis=1, keepdims=True)
    spread = jnp.mean(centred * centred, axis=1, keepdims=True)
    normed = centred * lax.rsqrt(spread + NORM_EPS) * gain_ref[...][None, :]
    normed_ref[...] = normed.astype(BF16)
    sum_ref[...] = jnp.sum(floats, axis=0, keepdims=True)
    for store in stores:
        store.wait()


def own_rows_kernel(part_ref, offset_ref, x_ref, wk_ref, wv_ref, far_ref, k_ref, v_ref):
    rows, width = x_ref.shape
    half = width // 2
    heads = offset_ref.shape[0]
    lane = lax.broadcasted_iota(jnp.int32, (1, width), 1)
    lane_offset = jnp.zeros((1, width), jnp.int32)
    for head in range(heads):
        lane_offset = jnp.where(lane >= head * (width // heads), offset_ref[head], lane_offset)
    phase = lax.broadcasted_iota(jnp.int32, (RATE, width), 0)
    chosen = jnp.where(phase == lane_offset, 1.0, 0.0)
    upper = part_ref[0] == 1
    for place, (w_ref, half_ref) in enumerate(((wk_ref, k_ref), (wv_ref, v_ref))):
        full = jnp.dot(x_ref[...], w_ref[...], preferred_element_type=F32)
        half_ref[...] = jnp.where(upper, full[:, half:], full[:, :half]).astype(BF16)
        grouped = full.reshape(rows // RATE, RATE, width) * chosen[None]
        picked = jnp.sum(grouped, axis=1).astype(BF16)
        for part in range(2):
            far_ref[part, :, place * half : (place + 1) * half] = picked[
                :, part * half : (part + 1) * half
            ]


def payload_kernel(own_ref, other_ref, out_ref):
    for place, ref in enumerate((own_ref, other_ref)):
        out_ref[:, :, place, :, :] = jnp.broadcast_to(ref[...][None], out_ref.shape[:2] + ref.shape[1:])


def half_columns(w_hbm, part_ref):
    half = w_hbm.shape[1] // 2
    return w_hbm.at[:, pl.ds(pl.multiple_of(part_ref[0] * half, half), half)]


def own_kernel(part_ref, x_ref, wq_ref, k_ref, v_ref, q_out, mixed_out, lse_out,
               q_scr, mixed_scr, lse_scr, out_sems, *, head_width, score_scale):
    half = wq_ref.shape[1] // 2
    upper = part_ref[0] == 1
    wq = jnp.where(upper, wq_ref[:, half:], wq_ref[:, :half])
    q = jnp.dot(x_ref[...], wq, preferred_element_type=F32) * score_scale
    q_scr[...] = q.astype(BF16)
    stores = started((q_scr,), (q_out,), out_sems)

    def finish(tile, lanes):
        stores.extend(
            started(
                (mixed_scr.at[:, lanes], lse_scr.at[:, lanes]),
                (mixed_out.at[:, lanes], lse_out.at[:, lanes]),
                out_sems,
                1 + 2 * tile,
            )
        )

    attend(q_scr[...], k_ref[...], v_ref[...], head_width, mixed_scr, lse_scr, finish)
    for store in stores:
        store.wait()


def near_kernel(part_ref, other_hbm, k_hbm, v_hbm, q_hbm, own_mixed_hbm, own_lse_hbm,
                wq_hbm, wk_hbm, wv_hbm, q_out, mixed_out, lse_out,
                x_scr, w_scr, k_scr, v_scr, q_scr, own_mixed_scr, own_lse_scr, mixed_scr, lse_scr,
                in_sems, out_sems, *, head_width, score_scale):
    rows = x_scr.shape[0]
    own, other = pl.ds(0, rows), pl.ds(rows, rows)
    loads = started(
        (
            half_columns(wk_hbm, part_ref), other_hbm, half_columns(wv_hbm, part_ref),
            half_columns(wq_hbm, part_ref), k_hbm, v_hbm, q_hbm, own_mixed_hbm, own_lse_hbm,
        ),
        (
            w_scr.at[0], x_scr, w_scr.at[1],
            w_scr.at[2], k_scr.at[own], v_scr.at[own], q_scr.at[own], own_mixed_scr, own_lse_scr,
        ),
        in_sems,
    )
    loads[0].wait()
    loads[1].wait()
    k_scr[rows:, :] = jnp.dot(x_scr[...], w_scr[0], preferred_element_type=F32).astype(BF16)
    loads[2].wait()
    v_scr[rows:, :] = jnp.dot(x_scr[...], w_scr[1], preferred_element_type=F32).astype(BF16)
    loads[3].wait()
    q = jnp.dot(x_scr[...], w_scr[2], preferred_element_type=F32) * score_scale
    q_scr[rows:, :] = q.astype(BF16)
    stores = started((q_scr.at[other],), (q_out.at[other],), out_sems)
    loads[4].wait()
    loads[5].wait()

    def store_block(place, span, first):
        stores.extend(
            started(
                (mixed_scr.at[place], lse_scr.at[place]),
                (mixed_out.at[span], lse_out.at[span]),
                out_sems,
                first,
            )
        )

    attend(q_scr[rows:, :], k_scr[...], v_scr[...], head_width, mixed_scr.at[1], lse_scr.at[1])
    store_block(1, other, 2)
    loads[6].wait()
    stores += started((q_scr.at[own],), (q_out.at[own],), out_sems, 1)
    attend(q_scr[:rows, :], k_scr[rows:, :], v_scr[rows:, :], head_width, mixed_scr.at[0],
           lse_scr.at[0])
    loads[7].wait()
    loads[8].wait()
    own_lse, new_lse = own_lse_scr[...], lse_scr[0]
    mixed_scr[0] = merge_states(own_mixed_scr[...], own_lse, mixed_scr[0], new_lse)
    gap = jnp.exp(-jnp.abs(own_lse - new_lse))
    lse_scr[0] = jnp.maximum(own_lse, new_lse) + jnp.log(1.0 + gap)
    store_block(0, own, 4)
    for store in stores:
        store.wait()


def far_kernel(q_hbm, far_hbm, near_hbm, near_lse_hbm, embedded_sum_ref, own_ref, lent_ref,
               pack_ref, q_scr, far_scr, near_scr, near_lse_scr, mixed_scr, lse_scr, sems,
               *, head_width):
    half = q_scr.shape[1]
    rows = own_ref.shape[0]
    loads = started(
        (far_hbm, q_hbm, near_hbm, near_lse_hbm), (far_scr, q_scr, near_scr, near_lse_scr), sems
    )
    loads[0].wait()
    loads[1].wait()
    total = jnp.zeros((1, half), F32)
    for place, out_ref in enumerate((own_ref, lent_ref)):
        span = slice(place * rows, (place + 1) * rows)
        attend(q_scr[span, :], far_scr[:, :half], far_scr[:, half:], head_width,
               mixed_scr.at[place], lse_scr.at[place])
        if place == 0:
            loads[2].wait()
            loads[3].wait()
        attended = merge_states(
            near_scr[span, :], near_lse_scr[span, :], mixed_scr[place], lse_scr[place]
        )
        out_ref[...] = attended.astype(BF16)
        total += jnp.sum(attended, axis=0, keepdims=True)
    pad = jnp.zeros((1, pack_ref.shape[1] * pack_ref.shape[2] - 3 * half), F32)
    packed = pack_row((embedded_sum_ref[...], total, pad))
    pack_ref[...] = jnp.broadcast_to(packed[None], pack_ref.shape)


def pack_row(pieces):
    flat = jnp.concatenate(pieces, axis=1)
    rows, lanes = PACK
    return jnp.concatenate([flat[:, r * lanes : (r + 1) * lanes] for r in range(rows)], axis=0)


def exact_row_times(row, matrix):
    top = row.astype(BF16).astype(F32)
    middle = (row - top).astype(BF16).astype(F32)
    low = row - top - middle
    parts = jnp.concatenate((top, middle, low, jnp.zeros((13, row.shape[1]), F32)), axis=0)
    product = jnp.dot(parts.astype(BF16), matrix, preferred_element_type=F32)
    return jnp.sum(product, axis=0, keepdims=True)


def unit_row(row):
    return row * lax.rsqrt(jnp.sum(row * row, axis=1, keepdims=True) + 1e-06)


def pooled_kernel(codes_ref, sums_ref, w_out_ref, w_head_ref, report_ref,
                  unit_ref, pack_ref, *, length):
    peers = sums_ref.shape[0]
    width = w_out_ref.shape[0]
    half = width // 2
    even = sums_ref[0]
    odd = sums_ref[1]
    for peer in range(2, peers, 2):
        even = even + sums_ref[peer]
        odd = odd + sums_ref[peer + 1]

    def flat(packed):
        return jnp.concatenate([packed[r : r + 1, :] for r in range(PACK[0])], axis=1)

    even, odd = flat(even), flat(odd)
    embedded_sum = even[:, :width] + odd[:, :width]
    attended_sum = jnp.concatenate(
        (even[:, width : width + half], odd[:, width : width + half]), axis=1
    )
    pooled = (embedded_sum + exact_row_times(attended_sum, w_out_ref[...])) * (1.0 / length)
    unit = unit_row(exact_row_times(pooled, w_head_ref[...]))
    unit_ref[...] = unit
    packed = pack_row((unit, unit_row(report_ref[...].astype(F32)), codes_ref[...][None, :]))
    pack_ref[...] = jnp.broadcast_to(packed[None], pack_ref.shape)


def contrast_kernel(all_ref, logits_ref, loss_ref):
    count = all_ref.shape[0]
    lanes = PACK[1]
    logits = jnp.zeros((count, count), F32)
    parts = 768 // lanes
    for r in range(parts):
        logits += lax.dot_general(
            all_ref[:, r, :], all_ref[:, parts + r, :], NT,
            precision=lax.Precision.HIGHEST, preferred_element_type=F32,
        )
    logits = logits * SOFTMAX_TEMPER
    logits_ref[...] = logits
    codes = all_ref[:, 2 * parts, :]
    down = lax.broadcasted_iota(jnp.int32, (count, count), 0)
    across = lax.broadcasted_iota(jnp.int32, (count, count), 1)
    diagonal = down == across
    slide_codes = codes[:, 0:1]
    report_codes = jnp.sum(jnp.where(diagonal, codes[:, 1:2], 0.0), axis=0, keepdims=True)
    positive = jnp.where((slide_codes == report_codes) | diagonal, 1.0, 0.0)

    def terms(axis):
        peak = jnp.max(logits, axis=axis, keepdims=True)
        lse = peak + jnp.log(jnp.sum(jnp.exp(logits - peak), axis=axis, keepdims=True))
        picked = jnp.sum(positive * (logits - lse), axis=axis, keepdims=True)
        return -picked / jnp.sum(positive, axis=axis, keepdims=True)

    both = jnp.sum(terms(1), axis=0, keepdims=True) + jnp.sum(terms(0), axis=1, keepdims=True)
    loss_ref[...] = both * (0.5 / count)


def on_device(
    tiles,
    w_embed,
    attn_gain,
    w_query,
    w_key,
    w_value,
    w_out,
    w_head,
    head_offset,
    slide_code,
    report_emb,
    report_code,
):
    _, rows, in_width = tiles.shape
    width = w_embed.shape[1]
    half = width // 2
    heads_count = head_offset.shape[0]
    head_width = width // heads_count
    ranks = lax.axis_size(SEQ_AXES)
    plane = lax.axis_size(("x", "y"))
    score_scale = 1.0 / math.sqrt(head_width)
    part = lax.axis_index("y") % 2
    parts = part.reshape(1)
    params = pltpu.CompilerParams(vmem_limit_bytes=LARGE_VMEM)
    small = pltpu.CompilerParams(vmem_limit_bytes=SMALL_VMEM)
    smem = pl.BlockSpec(memory_space=pltpu.SMEM)
    vmem = pl.BlockSpec(memory_space=pltpu.VMEM)
    anywhere = pl.BlockSpec(memory_space=pl.ANY)

    embedded, normed, embedded_sum = pl.pallas_call(
        embed_kernel,
        in_specs=[anywhere, anywhere, vmem],
        out_specs=[anywhere, vmem, vmem],
        out_shape=[
            jax.ShapeDtypeStruct((rows, width), BF16),
            pltpu.VMEM((rows, width), BF16),
            jax.ShapeDtypeStruct((1, width), F32),
        ],
        scratch_shapes=[
            pltpu.VMEM((rows, in_width), BF16),
            pltpu.VMEM((in_width, width), BF16),
            pltpu.VMEM((rows, width), BF16),
            pltpu.SemaphoreType.DMA((2,)),
            pltpu.SemaphoreType.DMA((EMBED_PIECES,)),
            pltpu.SemaphoreType.DMA((1,)),
        ],
        compiler_params=pltpu.CompilerParams(vmem_limit_bytes=EMBED_VMEM),
        name="embed",
    )(tiles.reshape(rows, in_width), w_embed, attn_gain)
    other_normed = swap_with(normed, "y")

    far_rows = rows // RATE
    far_own, keys_own, values_own = pl.pallas_call(
        own_rows_kernel,
        in_specs=[smem, smem, vmem, vmem, vmem],
        out_specs=[vmem, vmem, vmem],
        out_shape=[
            jax.ShapeDtypeStruct((2, far_rows, width), BF16),
            jax.ShapeDtypeStruct((rows, half), BF16),
            jax.ShapeDtypeStruct((rows, half), BF16),
        ],
        compiler_params=small,
        name="own_rows",
    )(parts, head_offset, normed, w_key, w_value)
    far_other = swap_with(far_own, "z_hi")
    payload = pl.pallas_call(
        payload_kernel,
        in_specs=[vmem, vmem],
        out_shape=jax.ShapeDtypeStruct((plane // 2, 2, 2, far_rows, width), BF16),
        compiler_params=small,
        name="payload",
    )(far_own, far_other).reshape(plane, 2 * far_rows, width)
    far = lax.all_to_all(payload, ("x", "y"), 0, 0, tiled=True).reshape(ranks * far_rows, width)

    lane_tiles = half // LANES
    half_rows = jax.ShapeDtypeStruct((rows, half), BF16)
    queries_own, own_mixed, own_lse = pl.pallas_call(
        functools.partial(own_kernel, head_width=head_width, score_scale=score_scale),
        in_specs=[smem] + [vmem] * 4,
        out_specs=[anywhere] * 3,
        out_shape=[
            pltpu.HBM((rows, half), BF16),
            pltpu.HBM((rows, half), F32),
            pltpu.HBM((rows, half), F32),
        ],
        scratch_shapes=[
            pltpu.VMEM((rows, half), BF16),
            pltpu.VMEM((rows, half), F32),
            pltpu.VMEM((rows, half), F32),
            pltpu.SemaphoreType.DMA((1 + 2 * lane_tiles,)),
        ],
        compiler_params=pltpu.CompilerParams(vmem_limit_bytes=32 << 20),
        cost_estimate=pl.CostEstimate(
            flops=3_000_000_000, bytes_accessed=4_000_000, transcendentals=2_000_000
        ),
        name="own_attention",
    )(parts, normed, w_query, keys_own, values_own)

    both_rows = jax.ShapeDtypeStruct((2 * rows, half), BF16)
    both_state = jax.ShapeDtypeStruct((2 * rows, half), F32)
    queries, near_mixed, near_lse = pl.pallas_call(
        functools.partial(near_kernel, head_width=head_width, score_scale=score_scale),
        in_specs=[smem] + [anywhere] * 9,
        out_specs=[anywhere] * 3,
        out_shape=[both_rows, both_state, both_state],
        scratch_shapes=[
            pltpu.VMEM((rows, width), BF16),
            pltpu.VMEM((3, width, half), BF16),
            pltpu.VMEM((2 * rows, half), BF16),
            pltpu.VMEM((2 * rows, half), BF16),
            pltpu.VMEM((2 * rows, half), BF16),
            pltpu.VMEM((rows, half), F32),
            pltpu.VMEM((rows, half), F32),
            pltpu.VMEM((2, rows, half), F32),
            pltpu.VMEM((2, rows, half), F32),
            pltpu.SemaphoreType.DMA((9,)),
            pltpu.SemaphoreType.DMA((6,)),
        ],
        compiler_params=params,
        cost_estimate=pl.CostEstimate(
            flops=9_000_000_000, bytes_accessed=8_000_000, transcendentals=6_000_000
        ),
        name="near_attention",
    )(parts, other_normed, keys_own, values_own, queries_own, own_mixed, own_lse,
      w_query, w_key, w_value)

    own_half, lent_half, sums = pl.pallas_call(
        functools.partial(far_kernel, head_width=head_width),
        in_specs=[anywhere] * 4 + [vmem],
        out_specs=[vmem] * 3,
        out_shape=[half_rows, half_rows, jax.ShapeDtypeStruct((ranks,) + PACK, F32)],
        scratch_shapes=[
            pltpu.VMEM((2 * rows, half), BF16),
            pltpu.VMEM((ranks * far_rows, width), BF16),
            pltpu.VMEM((2 * rows, half), F32),
            pltpu.VMEM((2 * rows, half), F32),
            pltpu.VMEM((2, rows, half), F32),
            pltpu.VMEM((2, rows, half), F32),
            pltpu.SemaphoreType.DMA((4,)),
        ],
        compiler_params=params,
        cost_estimate=pl.CostEstimate(
            flops=6_000_000_000, bytes_accessed=6_000_000, transcendentals=4_000_000
        ),
        name="far_attention",
    )(queries, far, near_mixed, near_lse, embedded_sum)

    sums = lax.all_to_all(sums, SEQ_AXES, 0, 0, tiled=True)
    lane = jnp.arange(2 * PACK[1], dtype=jnp.int32)
    codes = jnp.where(lane == 0, slide_code, jnp.where(lane == 1, report_code, 0)).astype(F32)
    w_mine = lax.dynamic_slice_in_dim(w_out, part * half, half, axis=0)
    w_theirs = lax.dynamic_slice_in_dim(w_out, (1 - part) * half, half, axis=0)
    encoded = embedded.astype(F32) + jnp.dot(own_half, w_mine, preferred_element_type=F32)
    sums, lent_half, encoded, codes = lax.optimization_barrier((sums, lent_half, encoded, codes))
    other_half = swap_with(lent_half, "y")
    encoded = encoded + jnp.dot(other_half, w_theirs, preferred_element_type=F32)
    encoded = encoded.astype(BF16).reshape(1, rows, width)

    slides = lax.axis_size("slide")
    slide_unit_vectors, packed = pl.pallas_call(
        functools.partial(pooled_kernel, length=rows * ranks),
        in_specs=[vmem] * 5,
        out_shape=[
            jax.ShapeDtypeStruct((1, width), F32),
            jax.ShapeDtypeStruct((slides,) + PACK, F32),
        ],
        compiler_params=small,
        name="pooled",
    )(codes, sums, w_out, w_head, report_emb)
    everyone = lax.all_to_all(packed, "slide", 0, 0, tiled=True)
    everyone, encoded = lax.optimization_barrier((everyone, encoded))
    logits, loss = pl.pallas_call(
        contrast_kernel,
        in_specs=[vmem],
        out_shape=[
            jax.ShapeDtypeStruct((slides, slides), F32),
            jax.ShapeDtypeStruct((1, 1), F32),
        ],
        compiler_params=small,
        name="contrast",
    )(everyone)
    return (encoded, slide_unit_vectors, logits, loss.reshape(()))


def solution(mesh):
    split = Mesh(mesh.devices.reshape(4, 2, 4, 8), SEQ_AXES + ("slide",))
    rows = P("slide", SEQ_AXES, None)
    return jax.shard_map(
        on_device,
        mesh=split,
        in_specs=(
            rows,
            P(),
            P(),
            P(),
            P(),
            P(),
            P(),
            P(),
            P(),
            P("slide"),
            P("slide", None),
            P("slide"),
        ),
        out_specs=(rows, P("slide", None), P(), P()),
        check_vma=False,
    )
```
